128 devices in a mesh: ctx: 32 (over y, z_lo, x), tp: 4 (over z_hi, core).
Axes of the slice: x: 4, y: 4, z: 4 (z_hi: 2, z_lo: 2; z = z_hi * 2 + z_lo), core: 2. Of those that a mesh axis runs over, the one named last changes fastest.
Arguments:
- balance_list: int32 [8192], replicated, may hold values from 0 to 8191, as said below
- doc_ids: int32 [8192], replicated, may hold values from 0 to 15, never falling along the last dimension, each value on 1 to 2048 neighbouring positions
- raw_queries: bfloat16 [8192, 4096], P('ctx', 'tp'), may hold values from -120 to 120
- raw_keys: bfloat16 [8192, 512], P('ctx', 'tp'), may hold values from -6 to 6
- values: bfloat16 [8192, 512], P('ctx', 'tp'), may hold values from -6 to 6
- out_weight: bfloat16 [4096, 8192], P(None, 'tp'), may hold values from -0.375 to 0.375
Outputs:
- layer_out: bfloat16 [8192, 8192], P('ctx', 'tp')
The draws below stay inside these ranges and needn't reach their ends.
Inputs may be any that keep to these rules, and one draw needn't show every extreme that they name: `balance_list`: A permutation of the 8192 positions. Entries j * 256 to (j + 1) * 256 - 1 list the tokens that device j of ctx holds after rebalancing. Token t first lies on device t // 256. The tokens one device gives to one owner come in whole groups of 4; at most 4 such groups (16 tokens) go to one owner, and in every draw each device gives exactly 4 groups to some owner. `doc_ids`: document numbers never fall along the sequence.
All inputs are finite; a program needn't handle non-finite values.
Results may differ from the reference program's by a relative error of at most 0.012.
Values may be sent and summed in bfloat16 or wider, within the bound.
A program may use at most 64 MiB of HBM per device.

```python
import math
import jax
import jax.numpy as jnp
import numpy as np
from jax import lax

D = 8192
HD = 128
HQ = 32
HK = 4
DOCS = 16
TOK_DEV = 256
SEQ = 8192
PIECE = 4
N_CTX = 32


def shared_keys(key):
    return jnp.clip(jax.random.normal(key, (SEQ, HK * HD), jnp.float32), -4.0, 4.0)


def shuffle_rows(subkey):
    return jax.random.permutation(subkey, TOK_DEV)


def draw_balance_list(key, part):
    key = jax.random.fold_in(key, 11)
    key_perm, key_spread, key_rows, key_inner = jax.random.split(key, 4)
    groups = 2 * N_CTX
    device_perm = jax.random.permutation(key_perm, N_CTX)
    spread = jax.random.randint(key_spread, ((N_CTX - 2) // 2,), -1, 2)
    others = jnp.stack([2 + spread, 2 - spread], axis=1).reshape(-1)
    multiple = jnp.concatenate([jnp.array([4, 0], jnp.int32), others.astype(jnp.int32)])
    bounds = jnp.cumsum(multiple)
    group_ids = jnp.arange(groups, dtype=jnp.int32)
    group_rank = jnp.sum((group_ids[:, None] >= bounds[None, :]).astype(jnp.int32), axis=1)
    shifts = device_perm[group_rank]
    row_perm = jax.vmap(shuffle_rows)(jax.random.split(key_rows, N_CTX)).reshape(N_CTX, groups, PIECE)
    owners = jnp.arange(N_CTX, dtype=jnp.int32)[:, None]
    sources = (owners - shifts[None, :]) % N_CTX
    picked = sources[:, :, None] * TOK_DEV + row_perm[sources, group_ids[None, :], :]
    picked = picked.reshape(N_CTX, TOK_DEV)
    inner = jax.vmap(shuffle_rows)(jax.random.split(key_inner, N_CTX))
    picked = jnp.take_along_axis(picked, inner, axis=1)
    return picked.reshape(-1).astype(jnp.int32)


def draw_raw_keys(key, part):
    base = shared_keys(key)
    return base.astype(jnp.bfloat16)


def draw_raw_queries(key, part):
    key = jax.random.fold_in(key, 7)
    fresh = jnp.clip(jax.random.normal(key, (SEQ, HQ * HD), jnp.float32), -4.0, 4.0)
    return fresh.astype(jnp.bfloat16)


def shard_levels(key, extent, shards, least, high):
    def one(axis_at, parts):
        draws = jax.random.uniform(jax.random.fold_in(jax.random.fold_in(key, 6), axis_at), (parts,), jnp.float32, least / len(shards), high / len(shards))
        return jnp.repeat(jnp.exp(draws), extent[axis_at] // parts).reshape((-1,) + (1,) * (len(extent) - axis_at - 1))

    loudness = one(*shards[0])
    for cut in shards[1:]:
        loudness = loudness * one(*cut)
    return loudness


def profile(number_of, total, bound, lean):
    weights = [(1 << 20) // math.isqrt(standing ** lean) + 1 for standing in range(2, number_of + 1)]
    rest, counts = total - bound - (number_of - 1), [1] * (number_of - 1)
    while rest > 0:
        movable = [i for i in range(number_of - 1) if counts[i] < bound]
        whole, budget = sum([weights[i] for i in movable]), rest
        for i in movable:
            extra = min(bound - counts[i], max(1, budget * weights[i] // whole), rest)
            counts[i] = counts[i] + extra
            rest = rest - extra
    return np.array([bound] + counts)


def uneven(key, number_of, total, limit, skew):
    if number_of == 2:
        one = jax.random.randint(key, (), max(1, total - limit), min(limit, total - 1) + 1)
        return jnp.stack([one, total - one])
    sizes = jnp.asarray(profile(number_of, total, limit, skew), jnp.int32)
    twos = (number_of - 1) // 2
    giver, receiver = sizes[1:1 + 2 * twos:2], sizes[2:2 + 2 * twos:2]
    room = jnp.minimum(giver - 1, limit - receiver)
    moved = jax.random.randint(jax.random.fold_in(key, 1), (twos,), 0, 1 << 20) % (room + 1)
    sizes = sizes.at[1:1 + 2 * twos:2].set(giver - moved).at[2:2 + 2 * twos:2].set(receiver + moved)
    return sizes[jax.random.permutation(jax.random.fold_in(key, 2), number_of)]


def noise(stream_key, shape, scale, bound, shards=(), kind=jnp.bfloat16):
    result = scale * jax.random.normal(stream_key, shape, jnp.float32)
    if shards:
        result = result * shard_levels(stream_key, shape, shards, -0.22, 0.18)
    return jnp.clip(result, -bound, bound).astype(kind)


def setup_inputs(seed: int = 0) -> dict:
    key_list = jax.random.split(jax.random.key(seed), 7)
    balance_list = draw_balance_list(jax.random.fold_in(key_list[6], 71), 0)
    doc_ids = jnp.searchsorted(jnp.cumsum(uneven(key_list[1], DOCS, SEQ, SEQ // 4, 1)), jnp.arange(SEQ), side="right").astype(jnp.int32)
    raw_queries = draw_raw_queries(jax.random.fold_in(key_list[6], 71), 0)
    raw_keys = draw_raw_keys(jax.random.fold_in(key_list[6], 71), 0)
    values = noise(key_list[4], (SEQ, HK * HD), 1.0, 6.0, ((0, 32), (1, 4)))
    out_weight = noise(key_list[5], (HQ * HD, D), (HQ * HD // 16) ** -0.5, 0.375, ((1, 4),))
    return {"balance_list": balance_list, "doc_ids": doc_ids, "raw_queries": raw_queries, "raw_keys": raw_keys, "values": values, "out_weight": out_weight}


ROPE_BASE = 500000.0

def rotate(matrix, positions):
    row_count = matrix.shape[0]
    col_count = matrix.shape[1]
    head_count = col_count // HD
    half_dim = HD // 2
    vectors = matrix.astype(jnp.float32).reshape(row_count, head_count, HD)
    frequency = ROPE_BASE ** (-(jnp.arange(half_dim, dtype=jnp.float32) * 2.0 / HD))
    angles = positions.astype(jnp.float32)[:, None] * frequency[None, :]
    cosine = jnp.cos(angles)[:, None, :]
    sine = jnp.sin(angles)[:, None, :]
    first_half = vectors[..., :half_dim]
    second_half = vectors[..., half_dim:]
    rotated = jnp.concatenate([first_half * cosine - second_half * sine, second_half * cosine + first_half * sine], axis=-1)
    return rotated.reshape(row_count, col_count).astype(jnp.bfloat16)

def reference(balance_list, doc_ids, raw_queries, raw_keys, values, out_weight):
    positions = jnp.arange(SEQ, dtype=jnp.int32)
    q_rot = rotate(raw_queries, positions)
    k_rot = rotate(raw_keys, positions)
    q_heads = q_rot.reshape(SEQ, HQ, HD).transpose(1, 0, 2)
    k_heads = k_rot.reshape(SEQ, HK, HD).transpose(1, 0, 2)
    v_heads = values.reshape(SEQ, HK, HD).transpose(1, 0, 2)
    block_rows = math.gcd(SEQ, 1024)
    block_count = SEQ // block_rows
    scale = 1.0 / math.sqrt(HD)

    def head_block(head_index):
        group = head_index // (HQ // HK)
        query_head = q_heads[head_index]
        key_head = k_heads[group]
        value_head = v_heads[group]

        def query_block(block_index):
            start = (block_index * block_rows).astype(jnp.int32)
            rows_here = lax.dynamic_slice_in_dim(query_head, start, block_rows)
            query_pos = start + jnp.arange(block_rows, dtype=jnp.int32)
            query_doc = lax.dynamic_slice_in_dim(doc_ids, start, block_rows)
            allowed = (doc_ids[None, :] == query_doc[:, None]) & (positions[None, :] <= query_pos[:, None])
            scores = jnp.dot(rows_here, key_head.T, preferred_element_type=jnp.float32) * scale
            scores = jnp.where(allowed, scores, -1e+30)
            largest = lax.optimization_barrier(jnp.max(scores, axis=-1, keepdims=True))
            weights = jnp.where(allowed, jnp.exp(scores - largest), 0.0)
            denom = lax.optimization_barrier(jnp.sum(weights, axis=-1, keepdims=True))
            mixed = jnp.dot(weights.astype(jnp.bfloat16), value_head, preferred_element_type=jnp.float32)
            return mixed / denom
        return lax.map(query_block, jnp.arange(block_count, dtype=jnp.int32)).reshape(SEQ, HD)
    attention = lax.map(head_block, jnp.arange(HQ, dtype=jnp.int32))
    attention = attention.transpose(1, 0, 2).reshape(SEQ, HQ * HD).astype(jnp.bfloat16)
    projected = jnp.dot(attention, out_weight, preferred_element_type=jnp.float32).astype(jnp.bfloat16)
    return projected[balance_list]
```

```python
import functools
import math

import jax
import jax.numpy as jnp
import numpy as np
from jax import lax
from jax.experimental import pallas as pl
from jax.experimental.pallas import tpu as pltpu
from jax.sharding import PartitionSpec as P

MESH = pl.DeviceIdType.MESH
HD = 128
NCTX = 32
ROWS = 256
HEADS = 8
BACK = 8
SLOTS = 16
CHUNKS = 4
PER_CHUNK = HEADS // CHUNKS
WIDTH = HEADS * HD // CHUNKS
OUT = 2048
FAR = 1048576.0
ROPE_BASE = 500000.0
F32 = jnp.float32
BF16 = jnp.bfloat16


def rope_tables():
    freq = ROPE_BASE ** (-(np.arange(HD // 2, dtype=np.float64) * 2.0 / HD))
    freq = np.concatenate([freq, freq])[None, :]
    inner = np.arange(ROWS, dtype=np.float64)[:, None] * freq
    outer = (np.arange(NCTX, dtype=np.float64) * ROWS)[:, None] * freq
    inner = np.stack([np.cos(inner), np.sin(inner)]).astype(np.float32)
    outer = np.stack([np.cos(outer), np.sin(outer)]).astype(np.float32)
    return inner, outer


def iota(shape, dim):
    return lax.broadcasted_iota(jnp.int32, shape, dim)


def kernel(
    bl, docs, q_in, k_in, v_in, inner, outer, w_hbm, out,
    qx, kv, feat, scores, tops, code, local, pack_m, unpack_m, packed, landed, merged, gath, w, acc,
    kv_send, kv_recv, a_send, a_recv, n_send, n_recv, z_send, z_recv, c_send, c_recv, f_send, f_recv, w_sem,
):
    me = lax.axis_index("ctx")
    tp = lax.axis_index("tp")
    hi, core = tp // 2, tp % 2
    mate = hi * 2 + 1 - core
    across = (1 - hi) * 2 + core
    across_mate = (1 - hi) * 2 + 1 - core
    twin = me + 4 - 8 * ((me // 4) % 2)

    w_copy = pltpu.make_async_copy(w_hbm, w, w_sem)
    w_copy.start()

    barrier = pltpu.get_barrier_semaphore()

    def greet(d, carry):
        pl.semaphore_signal(barrier, inc=1, device_id=((me + d) % NCTX, tp), device_id_type=MESH)
        return carry

    lax.fori_loop(1, NCTX, greet, 0)
    pl.semaphore_signal(barrier, inc=1, device_id=(me, mate), device_id_type=MESH)
    pl.semaphore_signal(barrier, inc=1, device_id=(twin, across), device_id_type=MESH)

    cos_o = outer[0, pl.ds(me, 1), :]
    sin_o = outer[1, pl.ds(me, 1), :]
    cos = cos_o * inner[0] - sin_o * inner[1]
    sin = sin_o * inner[0] + cos_o * inner[1]
    lane = iota((ROWS, HD), 1)
    sin = jnp.where(lane < HD // 2, -sin, sin)

    def rotate(x):
        x = x.astype(F32)
        return (x * cos + pltpu.roll(x, HD // 2, 1) * sin).astype(BF16)

    kv[0, 0:HD, :] = jnp.transpose(rotate(k_in[...]).astype(F32)).astype(BF16)
    kv[0, HD : 2 * HD, 0:HD] = v_in[0:HD, :]
    kv[0, HD : 2 * HD, HD : 2 * HD] = v_in[HD : 2 * HD, :]

    pl.semaphore_wait(barrier, NCTX + 1)

    def key_copy(source, d, to):
        return pltpu.make_async_remote_copy(
            src_ref=kv.at[source],
            dst_ref=kv.at[d],
            send_sem=kv_send.at[d - 1],
            recv_sem=kv_recv.at[d - 1],
            device_id=((me + to + NCTX) % NCTX, tp),
            device_id_type=MESH,
        )

    for d in (1, 7, 3, 5, 4, 8):
        key_copy(0, d, d).start()

    def doc_row(block):
        row = jnp.concatenate([docs[pl.ds(2 * block, 1), :], docs[pl.ds(2 * block + 1, 1), :]], axis=1)
        return jnp.broadcast_to(row, (HD, ROWS))

    far = jnp.where(jnp.transpose(doc_row(me).astype(F32)) == lane.astype(F32), 0.0, -FAR).astype(BF16)
    for h in range(HEADS):
        c, at = h // PER_CHUNK, h % PER_CHUNK * ROWS
        qx[c, at : at + ROWS, 0:HD] = rotate(q_in[:, h * HD : (h + 1) * HD])
        qx[c, at : at + ROWS, HD : 2 * HD] = far

    doc_iota = iota((HD, ROWS), 0)

    def features(d, carry):
        feat[d] = jnp.where(doc_row((me - d + NCTX) % NCTX) == doc_iota, 1.0, 0.0).astype(BF16)
        return carry

    lax.fori_loop(0, BACK + 1, features, 0)

    square_r, square_c = iota((ROWS, ROWS), 0), iota((ROWS, ROWS), 1)
    lists = jnp.concatenate(
        [bl[pl.ds(0, NCTX, stride=2), :], bl[pl.ds(1, NCTX, stride=2), :]], axis=1
    )
    mine = (lists >> 8) == me
    before = jnp.where(square_r < square_c, 1.0, 0.0).astype(BF16)
    rank = jnp.dot(jnp.where(mine, 1.0, 0.0).astype(BF16), before, preferred_element_type=F32)
    code[...] = jnp.where(mine, rank, -1.0)
    local[...] = ((lists & 255) + 1).astype(F32)
    slot_iota = iota((SLOTS, ROWS), 0).astype(F32)
    lane_next = (iota((SLOTS, ROWS), 1) + 1).astype(F32)

    def pack_rows(o, carry):
        hit = code[pl.ds(o, 1), :] == slot_iota
        token = jnp.sum(jnp.where(hit, local[pl.ds(o, 1), :], 0.0), axis=1, keepdims=True)
        at = pl.multiple_of(o * SLOTS, SLOTS)
        pack_m[pl.ds(at, SLOTS), :] = jnp.where(token == lane_next, 1.0, 0.0).astype(BF16)
        return carry

    lax.fori_loop(0, NCTX, pack_rows, 0)

    own = jnp.concatenate([bl[pl.ds(2 * twin, 1), :], bl[pl.ds(2 * twin + 1, 1), :]], axis=1)
    source_row = (own >> 8).astype(F32)
    source_col = jnp.sum(jnp.where(square_r == square_c, source_row, 0.0), axis=1, keepdims=True)
    earlier = (source_row == source_col) & (square_c < square_r)
    slot_col = jnp.sum(jnp.where(earlier, 1.0, 0.0), axis=1, keepdims=True)
    place = source_col * SLOTS + slot_col
    wide = iota((ROWS, NCTX * SLOTS), 1).astype(F32)
    unpack_m[...] = jnp.where(wide == place, 1.0, 0.0).astype(BF16)

    factor = math.log2(math.e) / math.sqrt(HD)
    chunk_rows = PER_CHUNK * ROWS

    def score(d):
        def one(c, carry):
            keys = jnp.concatenate([kv[d, 0:HD, :], feat[d]], axis=0)
            part = jnp.dot(qx[c], keys, preferred_element_type=F32) * factor
            if d == 0:
                part = jnp.where(
                    iota((chunk_rows, ROWS), 1) <= (iota((chunk_rows, ROWS), 0) & (ROWS - 1)), part, -2.0 * FAR
                )
            scores[c, d] = part
            top = jnp.maximum(part[:, 0:HD], part[:, HD:])
            tops[c] = top if d == 0 else jnp.maximum(tops[c], top)
            return carry

        lax.fori_loop(0, CHUNKS, one, 0)

    score(0)
    key_copy(0, 1, 1).wait_recv()
    key_copy(1, 2, 1).start()
    key_copy(0, 7, 7).wait_recv()
    key_copy(7, 6, -1).start()
    score(1)
    score(7)
    for d in (3, 5, 4, 8, 2, 6):
        key_copy(0, d, d).wait_recv()
        score(d)

    def attend(c, carry):
        ones = jnp.ones((ROWS, HD), BF16)
        vals = []
        for d in range(BACK + 1):
            block = jnp.concatenate([kv[d, HD : 2 * HD, 0:HD], kv[d, HD : 2 * HD, HD : 2 * HD]], axis=0)
            vals.append(jnp.concatenate([block, ones], axis=1))
        vals = jnp.concatenate(vals, axis=0)
        part = []
        for h in range(PER_CHUNK):
            rows = slice(h * ROWS, (h + 1) * ROWS)
            top = jnp.max(tops[c, rows, :], axis=1, keepdims=True)
            weights = [jnp.exp2(scores[c, d, rows, :] - top).astype(BF16) for d in range(BACK + 1)]
            mixed = jnp.dot(jnp.concatenate(weights, axis=1), vals, preferred_element_type=F32)
            part.append((mixed[:, 0:HD] / mixed[:, HD : 2 * HD]).astype(BF16))
        part = jnp.concatenate(part, axis=1)
        rows = jnp.dot(pack_m[...], part, preferred_element_type=F32).astype(BF16)
        packed[c] = rows.reshape(NCTX, SLOTS, WIDTH)
        landed[c, me] = packed[c, twin]

        def send(d, inner_carry):
            to = (me + d) % NCTX
            pltpu.make_async_remote_copy(
                src_ref=packed.at[c, to + 4 - 8 * ((to // 4) % 2)],
                dst_ref=landed.at[c, me],
                send_sem=a_send.at[c],
                recv_sem=a_recv.at[c],
                device_id=(to, tp),
                device_id_type=MESH,
            ).start()
            return inner_carry

        return lax.fori_loop(1, NCTX, send, carry)

    lax.fori_loop(0, CHUNKS, attend, 0)

    def hand(c, to, sems):
        return pltpu.make_async_remote_copy(
            src_ref=merged.at[c],
            dst_ref=gath.at[c, tp],
            send_sem=sems[0].at[c],
            recv_sem=sems[1].at[c],
            device_id=(twin, to),
            device_id_type=MESH,
        )

    near, far_off, mate_near, mate_far = (n_send, n_recv), (z_send, z_recv), (c_send, c_recv), (f_send, f_recv)

    def share(c, slot, sems):
        return pltpu.make_async_remote_copy(
            src_ref=gath.at[c, slot],
            dst_ref=gath.at[c, slot],
            send_sem=sems[0].at[c],
            recv_sem=sems[1].at[c],
            device_id=(me, mate),
            device_id_type=MESH,
        )

    def unpack(c):
        rest = packed.at[c, pl.ds(0, NCTX - 1)]
        pltpu.make_async_copy(rest, rest, a_recv.at[c]).wait()
        rows = jnp.dot(unpack_m[...], landed[c].reshape(NCTX * SLOTS, WIDTH), preferred_element_type=F32)
        merged[c] = rows.astype(BF16)
        hand(c, tp, near).start()
        hand(c, across, far_off).start()

    def forward(c):
        hand(c, tp, near).wait_recv()
        share(c, tp, mate_near).start()
        hand(c, across, far_off).wait_recv()
        share(c, across, mate_far).start()

    def project(c):
        share(c, mate, mate_near).wait_recv()
        share(c, across_mate, mate_far).wait_recv()

        def columns(n, carry):
            cols = pl.ds(pl.multiple_of(n * 512, 512), 512)
            total = jnp.zeros((ROWS, 512), F32)
            for t in range(4):
                first = t * HEADS * HD + c * WIDTH
                total += jnp.dot(gath[c, t], w[first : first + WIDTH, cols], preferred_element_type=F32)
            if c > 0:
                total += acc[:, cols]
            if c < CHUNKS - 1:
                acc[:, cols] = total
            else:
                out[:, cols] = total.astype(BF16)
            return carry

        lax.fori_loop(0, OUT // 512, columns, 0)

    unpack(0)
    unpack(1)
    forward(0)
    unpack(2)
    forward(1)
    w_copy.wait()
    project(0)
    unpack(3)
    forward(2)
    project(1)
    forward(3)
    project(2)
    project(3)

    for d in range(1, BACK + 1):
        key_copy(0, d, d).wait_send()
    for c in range(CHUNKS):
        rest = packed.at[c, pl.ds(0, NCTX - 1)]
        pltpu.make_async_copy(rest, rest, a_send.at[c]).wait()
        hand(c, tp, near).wait_send()
        hand(c, across, far_off).wait_send()
        share(c, tp, mate_near).wait_send()
        share(c, across, mate_far).wait_send()


def on_device(balance_list, doc_ids, raw_queries, raw_keys, values, out_weight):
    inner, outer = rope_tables()
    vmem = pl.BlockSpec(memory_space=pltpu.VMEM)
    dma = pltpu.SemaphoreType.DMA
    return pl.pallas_call(
        kernel,
        out_shape=jax.ShapeDtypeStruct((ROWS, OUT), BF16),
        in_specs=[vmem] * 7 + [pl.BlockSpec(memory_space=pl.ANY)],
        out_specs=vmem,
        scratch_shapes=[
            pltpu.VMEM((CHUNKS, PER_CHUNK * ROWS, 2 * HD), BF16),
            pltpu.VMEM((BACK + 1, ROWS, 2 * HD), BF16),
            pltpu.VMEM((BACK + 1, HD, ROWS), BF16),
            pltpu.VMEM((CHUNKS, BACK + 1, PER_CHUNK * ROWS, ROWS), F32),
            pltpu.VMEM((CHUNKS, PER_CHUNK * ROWS, HD), F32),
            pltpu.VMEM((NCTX, ROWS), F32),
            pltpu.VMEM((NCTX, ROWS), F32),
            pltpu.VMEM((NCTX * SLOTS, ROWS), BF16),
            pltpu.VMEM((ROWS, NCTX * SLOTS), BF16),
            pltpu.VMEM((CHUNKS, NCTX, SLOTS, WIDTH), BF16),
            pltpu.VMEM((CHUNKS, NCTX, SLOTS, WIDTH), BF16),
            pltpu.VMEM((CHUNKS, ROWS, WIDTH), BF16),
            pltpu.VMEM((CHUNKS, 4, ROWS, WIDTH), BF16),
            pltpu.VMEM((4096, OUT), BF16),
            pltpu.VMEM((ROWS, OUT), F32),
            dma((BACK,)), dma((BACK,)),
            dma((CHUNKS,)), dma((CHUNKS,)),
            dma((CHUNKS,)), dma((CHUNKS,)),
            dma((CHUNKS,)), dma((CHUNKS,)),
            dma((CHUNKS,)), dma((CHUNKS,)),
            dma((CHUNKS,)), dma((CHUNKS,)),
            dma,
        ],
        compiler_params=pltpu.CompilerParams(
            collective_id=0, has_side_effects=True, vmem_limit_bytes=56 * 1024 * 1024
        ),
        cost_estimate=pl.CostEstimate(
            flops=7_000_000_000, bytes_accessed=19_000_000, transcendentals=4_700_000
        ),
    )(
        balance_list.reshape(64, 128), doc_ids.reshape(64, 128), raw_queries, raw_keys, values,
        jnp.asarray(inner), jnp.asarray(outer), out_weight,
    )


def solution(mesh):
    in_specs = (P(), P(), P("ctx", "tp"), P("ctx", "tp"), P("ctx", "tp"), P(None, "tp"))
    out_specs = P("ctx", "tp")
    return jax.shard_map(
        on_device, mesh=mesh, in_specs=in_specs, out_specs=out_specs, check_vma=False
    )
```

```python
import functools
import math

import jax
import jax.numpy as jnp
import numpy as np
from jax import lax
from jax.experimental import pallas as pl
from jax.experimental.pallas import tpu as pltpu
from jax.sharding import PartitionSpec as P

MESH = pl.DeviceIdType.MESH
HD = 128
NCTX = 32
ROWS = 256
HEADS = 8
BACK = 8
SLOTS = 16
CHUNKS = 4
LAG = 3
PER_CHUNK = HEADS // CHUNKS
WIDTH = HEADS * HD // CHUNKS
OUT = 2048
FAR = 1048576.0
ROPE_BASE = 500000.0
F32 = jnp.float32
BF16 = jnp.bfloat16


def rope_tables():
    freq = ROPE_BASE ** (-(np.arange(HD // 2, dtype=np.float64) * 2.0 / HD))
    freq = np.concatenate([freq, freq])[None, :]
    inner = np.arange(ROWS, dtype=np.float64)[:, None] * freq
    outer = (np.arange(NCTX, dtype=np.float64) * ROWS)[:, None] * freq
    inner = np.stack([np.cos(inner), np.sin(inner)]).astype(np.float32)
    outer = np.stack([np.cos(outer), np.sin(outer)]).astype(np.float32)
    return inner, outer


def iota(shape, dim):
    return lax.broadcasted_iota(jnp.int32, shape, dim)


def kernel(
    bl_h, docs_h, q_h, k_h, v_h, inner_h, outer_h, w_hbm, out,
    bl, docs, q_in, k_in, v_in, inner, outer,
    qx, kv, feat, scores, tops, code, local, pack_m, unpack_m, packed, landed, merged, gath, w, acc,
    kv_send, kv_recv, a_send, a_recv, n_send, n_recv, z_send, z_recv, c_send, c_recv, f_send, f_recv, w_sem, in_sem,
):
    me = lax.axis_index("ctx")
    tp = lax.axis_index("tp")
    hi, core = tp // 2, tp % 2
    mate = hi * 2 + 1 - core
    across = (1 - hi) * 2 + core
    across_mate = (1 - hi) * 2 + 1 - core
    twin = me + 4 - 8 * ((me // 4) % 2)

    w_copy = pltpu.make_async_copy(w_hbm, w, w_sem)
    pairs = (
        (k_h, k_in), (inner_h, inner), (outer_h, outer), (v_h, v_in), (q_h, q_in), (docs_h, docs), (bl_h, bl)
    )
    loads = [pltpu.make_async_copy(a, b, in_sem.at[n]) for n, (a, b) in enumerate(pairs)]
    for load in loads:
        load.start()

    barrier = pltpu.get_barrier_semaphore()

    def others(body):
        lax.fori_loop(me + 1, NCTX, body, 0)
        lax.fori_loop(0, me, body, 0)

    def greet(to, carry):
        pl.semaphore_signal(barrier, inc=1, device_id=(to, tp), device_id_type=MESH)
        return carry

    others(greet)
    pl.semaphore_signal(barrier, inc=1, device_id=(me, mate), device_id_type=MESH)
    pl.semaphore_signal(barrier, inc=1, device_id=(twin, across), device_id_type=MESH)

    for load in loads[:4]:
        load.wait()
    cos_o = outer[0, pl.ds(me, 1), :]
    sin_o = outer[1, pl.ds(me, 1), :]
    cos = cos_o * inner[0] - sin_o * inner[1]
    sin = sin_o * inner[0] + cos_o * inner[1]
    lane = iota((ROWS, HD), 1)
    sin = jnp.where(lane < HD // 2, -sin, sin)

    def rotate(x):
        x = x.astype(F32)
        return (x * cos + pltpu.roll(x, HD // 2, 1) * sin).astype(BF16)

    kv[0, 0:HD, :] = jnp.transpose(rotate(k_in[...]).astype(F32)).astype(BF16)
    kv[0, HD : 2 * HD, 0:HD] = v_in[0:HD, :]
    kv[0, HD : 2 * HD, HD : 2 * HD] = v_in[HD : 2 * HD, :]

    pl.semaphore_wait(barrier, NCTX + 1)

    def key_copy(source, d, to):
        return pltpu.make_async_remote_copy(
            src_ref=kv.at[source],
            dst_ref=kv.at[d],
            send_sem=kv_send.at[d - 1],
            recv_sem=kv_recv.at[d - 1],
            device_id=(to, tp),
            device_id_type=MESH,
        )

    slab, place_in = me // BACK * BACK, me % BACK
    key_copy(0, BACK, (me + BACK) % NCTX).start()

    def send_own(d, carry):
        @pl.when(place_in + d < BACK)
        def _():
            key_copy(0, d, me + d).start()

        return carry

    def send_previous(d, carry):
        @pl.when(place_in + d >= BACK)
        def _():
            key_copy(BACK, d, slab + (place_in + d) % BACK).start()

        return carry

    lax.fori_loop(1, BACK, send_own, 0)
    w_copy.start()
    for load in loads[4:]:
        load.wait()

    def doc_row(block):
        row = jnp.concatenate([docs[pl.ds(2 * block, 1), :], docs[pl.ds(2 * block + 1, 1), :]], axis=1)
        return jnp.broadcast_to(row, (HD, ROWS))

    far = jnp.where(jnp.transpose(doc_row(me).astype(F32)) == lane.astype(F32), 0.0, -FAR).astype(BF16)

    def queries(h, carry):
        rows = pl.ds(pl.multiple_of(h * ROWS, ROWS), ROWS)
        qx[rows, 0:HD] = rotate(q_in[:, pl.ds(pl.multiple_of(h * HD, HD), HD)])
        qx[rows, HD : 2 * HD] = far
        return carry

    lax.fori_loop(0, HEADS, queries, 0)
    key_copy(0, BACK, me).wait_recv()
    lax.fori_loop(1, BACK, send_previous, 0)

    doc_iota = iota((HD, ROWS), 0)

    def features(d, carry):
        feat[d] = jnp.where(doc_row((me - d + NCTX) % NCTX) == doc_iota, 1.0, 0.0).astype(BF16)
        return carry

    lax.fori_loop(0, BACK + 1, features, 0)

    square_r, square_c = iota((ROWS, ROWS), 0), iota((ROWS, ROWS), 1)
    lists = jnp.concatenate(
        [bl[pl.ds(0, NCTX, stride=2), :], bl[pl.ds(1, NCTX, stride=2), :]], axis=1
    )
    mine = (lists >> 8) == me
    before = jnp.where(square_r < square_c, 1.0, 0.0).astype(BF16)
    rank = jnp.dot(jnp.where(mine, 1.0, 0.0).astype(BF16), before, preferred_element_type=F32)
    code[...] = jnp.where(mine, rank, -1.0)
    local[...] = ((lists & 255) + 1).astype(F32)
    slot_iota = iota((SLOTS, ROWS), 0).astype(F32)
    lane_next = (iota((SLOTS, ROWS), 1) + 1).astype(F32)

    def pack_rows(o, carry):
        hit = code[pl.ds(o, 1), :] == slot_iota
        token = jnp.sum(jnp.where(hit, local[pl.ds(o, 1), :], 0.0), axis=1, keepdims=True)
        at = pl.multiple_of((o + 4 - 8 * ((o // 4) % 2)) * SLOTS, SLOTS)
        pack_m[pl.ds(at, SLOTS), :] = jnp.where(token == lane_next, 1.0, 0.0).astype(BF16)
        return carry

    lax.fori_loop(0, NCTX, pack_rows, 0, unroll=8)

    own = jnp.concatenate([bl[pl.ds(2 * twin, 1), :], bl[pl.ds(2 * twin + 1, 1), :]], axis=1)
    source_row = (own >> 8).astype(F32)
    source_col = jnp.sum(jnp.where(square_r == square_c, source_row, 0.0), axis=1, keepdims=True)
    earlier = (source_row == source_col) & (square_c < square_r)
    slot_col = jnp.sum(jnp.where(earlier, 1.0, 0.0), axis=1, keepdims=True)
    place = source_col * SLOTS + slot_col
    wide = iota((ROWS, NCTX * SLOTS), 1).astype(F32)
    unpack_m[...] = jnp.where(wide == place, 1.0, 0.0).astype(BF16)

    factor = math.log2(math.e) / math.sqrt(HD)
    chunk_rows = PER_CHUNK * ROWS

    def score_own(c, carry):
        keys = jnp.concatenate([kv[0, 0:HD, :], feat[0]], axis=0)
        rows = pl.ds(pl.multiple_of(c * chunk_rows, chunk_rows), chunk_rows)
        part = jnp.dot(qx[rows, :], keys, preferred_element_type=F32) * factor
        allowed = iota((chunk_rows, ROWS), 1) <= (iota((chunk_rows, ROWS), 0) & (ROWS - 1))
        part = jnp.where(allowed, part, -2.0 * FAR)
        scores[c, 0] = part
        tops[c] = jnp.maximum(part[:, 0:HD], part[:, HD:])
        return carry

    lax.fori_loop(0, CHUNKS, score_own, 0)

    def score(i, carry):
        d = (i + BACK - 1) % BACK + 1

        @pl.when(i > 0)
        def _():
            key_copy(0, d, me).wait_recv()

        keys = jnp.concatenate([kv[d, 0:HD, :], feat[d]], axis=0)
        for c in range(CHUNKS):
            rows = slice(c * chunk_rows, (c + 1) * chunk_rows)
            part = jnp.dot(qx[rows, :], keys, preferred_element_type=F32) * factor
            scores[c, d] = part
            tops[c] = jnp.maximum(tops[c], jnp.maximum(part[:, 0:HD], part[:, HD:]))
        return carry

    lax.fori_loop(0, BACK, score, 0)

    def attend(c):
        ones = jnp.ones((ROWS, HD), BF16)
        vals = []
        for d in range(BACK + 1):
            block = jnp.concatenate([kv[d, HD : 2 * HD, 0:HD], kv[d, HD : 2 * HD, HD : 2 * HD]], axis=0)
            vals.append(jnp.concatenate([block, ones], axis=1))
        vals = jnp.concatenate(vals, axis=0)
        part = []
        for h in range(PER_CHUNK):
            rows = slice(h * ROWS, (h + 1) * ROWS)
            top = jnp.max(tops[c, rows, :], axis=1, keepdims=True)
            weights = [jnp.exp2(scores[c, d, rows, :] - top).astype(BF16) for d in range(BACK + 1)]
            mixed = jnp.dot(jnp.concatenate(weights, axis=1), vals, preferred_element_type=F32)
            part.append((mixed[:, 0:HD] / mixed[:, HD : 2 * HD]).astype(BF16))
        part = jnp.concatenate(part, axis=1)
        rows = jnp.dot(pack_m[...], part, preferred_element_type=F32).astype(BF16)
        packed[c] = rows.reshape(NCTX, SLOTS, WIDTH)
        landed[c, me] = packed[c, me]

        def send(to, inner_carry):
            pltpu.make_async_remote_copy(
                src_ref=packed.at[c, to],
                dst_ref=landed.at[c, me],
                send_sem=a_send.at[c],
                recv_sem=a_recv.at[c],
                device_id=(to, tp),
                device_id_type=MESH,
            ).start()
            return inner_carry

        others(send)

    def hand(c, to, sems):
        return pltpu.make_async_remote_copy(
            src_ref=merged.at[c],
            dst_ref=gath.at[c, tp],
            send_sem=sems[0].at[c],
            recv_sem=sems[1].at[c],
            device_id=(twin, to),
            device_id_type=MESH,
        )

    near, far_off, mate_near, mate_far = (n_send, n_recv), (z_send, z_recv), (c_send, c_recv), (f_send, f_recv)

    def share(c, slot, sems):
        return pltpu.make_async_remote_copy(
            src_ref=gath.at[c, slot],
            dst_ref=gath.at[c, slot],
            send_sem=sems[0].at[c],
            recv_sem=sems[1].at[c],
            device_id=(me, mate),
            device_id_type=MESH,
        )

    def unpack(c):
        rest = packed.at[c, pl.ds(0, NCTX - 1)]
        pltpu.make_async_copy(rest, rest, a_recv.at[c]).wait()
        rows = jnp.dot(unpack_m[...], landed[c].reshape(NCTX * SLOTS, WIDTH), preferred_element_type=F32)
        merged[c] = rows.astype(BF16)
        hand(c, tp, near).start()
        hand(c, across, far_off).start()

    def forward(c):
        hand(c, tp, near).wait_recv()
        share(c, tp, mate_near).start()
        hand(c, across, far_off).wait_recv()
        share(c, across, mate_far).start()

    def project(c, final):
        share(c, mate, mate_near).wait_recv()
        share(c, across_mate, mate_far).wait_recv()
        rows = jnp.concatenate([gath[c, t] for t in range(4)], axis=1)

        def columns(n, carry):
            cols = pl.ds(pl.multiple_of(n * 512, 512), 512)
            part = [
                w[pl.ds(pl.multiple_of(t * HEADS * HD + c * WIDTH, WIDTH), WIDTH), cols] for t in range(4)
            ]
            total = jnp.dot(rows, jnp.concatenate(part, axis=0), preferred_element_type=F32) + acc[:, cols]
            if final:
                out[:, cols] = total.astype(BF16)
            else:
                acc[:, cols] = total
            return carry

        lax.fori_loop(0, OUT // 512, columns, 0)

    def step(s, carry):
        @pl.when((s >= LAG) & (s < CHUNKS + LAG))
        def _():
            unpack(s - LAG)

        @pl.when(s < CHUNKS)
        def _():
            attend(s)

        @pl.when((s >= LAG + 1) & (s < CHUNKS + LAG + 1))
        def _():
            forward(s - LAG - 1)

        @pl.when(s == LAG + 1)
        def _():
            w_copy.wait()

        @pl.when(s >= LAG + 2)
        def _():
            project(s - LAG - 2, False)

        return carry

    acc[...] = jnp.zeros((ROWS, OUT), F32)
    lax.fori_loop(0, CHUNKS + LAG + 1, step, 0)
    project(CHUNKS - 1, True)

    for d in range(1, BACK + 1):
        key_copy(0, d, me).wait_send()
    for c in range(CHUNKS):
        rest = packed.at[c, pl.ds(0, NCTX - 1)]
        pltpu.make_async_copy(rest, rest, a_send.at[c]).wait()
        hand(c, tp, near).wait_send()
        hand(c, across, far_off).wait_send()
        share(c, tp, mate_near).wait_send()
        share(c, across, mate_far).wait_send()


def on_device(balance_list, doc_ids, raw_queries, raw_keys, values, out_weight):
    inner, outer = rope_tables()
    vmem = pl.BlockSpec(memory_space=pltpu.VMEM)
    dma = pltpu.SemaphoreType.DMA
    return pl.pallas_call(
        kernel,
        out_shape=jax.ShapeDtypeStruct((ROWS, OUT), BF16),
        in_specs=[pl.BlockSpec(memory_space=pl.ANY)] * 8,
        out_specs=vmem,
        scratch_shapes=[
            pltpu.VMEM((64, 128), jnp.int32),
            pltpu.VMEM((64, 128), jnp.int32),
            pltpu.VMEM((ROWS, HEADS * HD), BF16),
            pltpu.VMEM((ROWS, HD), BF16),
            pltpu.VMEM((ROWS, HD), BF16),
            pltpu.VMEM((2, ROWS, HD), F32),
            pltpu.VMEM((2, NCTX, HD), F32),
            pltpu.VMEM((HEADS * ROWS, 2 * HD), BF16),
            pltpu.VMEM((BACK + 1, ROWS, 2 * HD), BF16),
            pltpu.VMEM((BACK + 1, HD, ROWS), BF16),
            pltpu.VMEM((CHUNKS, BACK + 1, PER_CHUNK * ROWS, ROWS), F32),
            pltpu.VMEM((CHUNKS, PER_CHUNK * ROWS, HD), F32),
            pltpu.VMEM((NCTX, ROWS), F32),
            pltpu.VMEM((NCTX, ROWS), F32),
            pltpu.VMEM((NCTX * SLOTS, ROWS), BF16),
            pltpu.VMEM((ROWS, NCTX * SLOTS), BF16),
            pltpu.VMEM((CHUNKS, NCTX, SLOTS, WIDTH), BF16),
            pltpu.VMEM((CHUNKS, NCTX, SLOTS, WIDTH), BF16),
            pltpu.VMEM((CHUNKS, ROWS, WIDTH), BF16),
            pltpu.VMEM((CHUNKS, 4, ROWS, WIDTH), BF16),
            pltpu.VMEM((4096, OUT), BF16),
            pltpu.VMEM((ROWS, OUT), F32),
            dma((BACK,)), dma((BACK,)),
            dma((CHUNKS,)), dma((CHUNKS,)),
            dma((CHUNKS,)), dma((CHUNKS,)),
            dma((CHUNKS,)), dma((CHUNKS,)),
            dma((CHUNKS,)), dma((CHUNKS,)),
            dma((CHUNKS,)), dma((CHUNKS,)),
            dma,
            dma((7,)),
        ],
        compiler_params=pltpu.CompilerParams(
            collective_id=0, has_side_effects=True, vmem_limit_bytes=60 * 1024 * 1024
        ),
        cost_estimate=pl.CostEstimate(
            flops=7_000_000_000, bytes_accessed=19_000_000, transcendentals=4_700_000
        ),
    )(
        balance_list.reshape(64, 128), doc_ids.reshape(64, 128), raw_queries, raw_keys, values,
        jnp.asarray(inner), jnp.asarray(outer), out_weight,
    )


def solution(mesh):
    in_specs = (P(), P(), P("ctx", "tp"), P("ctx", "tp"), P("ctx", "tp"), P(None, "tp"))
    out_specs = P("ctx", "tp")
    return jax.shard_map(
        on_device, mesh=mesh, in_specs=in_specs, out_specs=out_specs, check_vma=False
    )
```

```python
import functools
import math

import jax
import jax.numpy as jnp
import numpy as np
from jax import lax
from jax.experimental import pallas as pl
from jax.experimental.pallas import tpu as pltpu
from jax.sharding import PartitionSpec as P

MESH = pl.DeviceIdType.MESH
HD = 128
NCTX = 32
PLANE = 16
ROWS = 256
HEADS = 8
BACK = 8
SLOTS = 16
CHUNKS = 4
LAG = 3
PER_CHUNK = HEADS // CHUNKS
WIDTH = HEADS * HD // CHUNKS
OUT = 2048
FAR = 1048576.0
ROPE_BASE = 500000.0
F32 = jnp.float32
BF16 = jnp.bfloat16


def rope_tables():
    freq = ROPE_BASE ** (-(np.arange(HD // 2, dtype=np.float64) * 2.0 / HD))
    freq = np.concatenate([freq, freq])[None, :]
    inner = np.arange(ROWS, dtype=np.float64)[:, None] * freq
    outer = (np.arange(NCTX, dtype=np.float64) * ROWS)[:, None] * freq
    inner = np.stack([np.cos(inner), np.sin(inner)]).astype(np.float32)
    outer = np.stack([np.cos(outer), np.sin(outer)]).astype(np.float32)
    return inner, outer


def iota(shape, dim):
    return lax.broadcasted_iota(jnp.int32, shape, dim)


def kernel(
    bl_h, docs_h, q_h, k_h, v_h, inner_h, outer_h, w_hbm, out,
    bl, docs, q_in, k_in, v_in, inner, outer,
    qx, kv, feat, scores, tops, code, local, pack_m, unpack_m, pair, packed, landed, merged, gath, w, acc,
    kv_send, kv_recv, p_send, p_recv, a_send, a_recv, h_send, h_recv, c_send, c_recv, w_sem, in_sem,
):
    me = lax.axis_index("ctx")
    tp = lax.axis_index("tp")
    hi, core = tp // 2, tp % 2
    mate = hi * 2 + 1 - core
    across = (1 - hi) * 2 + core
    across_mate = (1 - hi) * 2 + 1 - core
    lo = (me // 4) % 2
    twin = me + 4 - 8 * lo
    mine_xy = me // 8 * 4 + me % 4

    def in_plane(xy):
        return xy // 4 * 8 + lo * 4 + xy % 4

    def others(body):
        lax.fori_loop(mine_xy + 1, PLANE, body, 0)
        lax.fori_loop(0, mine_xy, body, 0)


    w_copy = pltpu.make_async_copy(w_hbm, w, w_sem)
    pairs = (
        (k_h, k_in), (inner_h, inner), (outer_h, outer), (v_h, v_in), (q_h, q_in), (docs_h, docs), (bl_h, bl)
    )
    loads = [pltpu.make_async_copy(a, b, in_sem.at[n]) for n, (a, b) in enumerate(pairs)]
    for load in loads:
        load.start()

    barrier = pltpu.get_barrier_semaphore()

    def greet(xy, carry):
        pl.semaphore_signal(barrier, inc=1, device_id=(in_plane(xy), tp), device_id_type=MESH)
        return carry

    def greet_other_plane(x, carry):
        to = me // 8 * 8 + (1 - lo) * 4 + x
        pl.semaphore_signal(barrier, inc=1, device_id=(to, tp), device_id_type=MESH)
        return carry

    lax.fori_loop(0, 4, greet_other_plane, 0)
    others(greet)
    for who in ((me, mate), (me, across), (twin, across)):
        pl.semaphore_signal(barrier, inc=1, device_id=who, device_id_type=MESH)

    for load in loads[:4]:
        load.wait()
    cos_o = outer[0, pl.ds(me, 1), :]
    sin_o = outer[1, pl.ds(me, 1), :]
    cos = cos_o * inner[0] - sin_o * inner[1]
    sin = sin_o * inner[0] + cos_o * inner[1]
    lane = iota((ROWS, HD), 1)
    sin = jnp.where(lane < HD // 2, -sin, sin)

    def rotate(x):
        x = x.astype(F32)
        return (x * cos + pltpu.roll(x, HD // 2, 1) * sin).astype(BF16)

    kv[0, 0:HD, :] = jnp.transpose(rotate(k_in[...]).astype(F32)).astype(BF16)
    kv[0, HD : 2 * HD, 0:HD] = v_in[0:HD, :]
    kv[0, HD : 2 * HD, HD : 2 * HD] = v_in[HD : 2 * HD, :]

    pl.semaphore_wait(barrier, PLANE - 1 + 4 + 3)

    def key_copy(source, d, to):
        return pltpu.make_async_remote_copy(
            src_ref=kv.at[source],
            dst_ref=kv.at[d],
            send_sem=kv_send.at[d - 1],
            recv_sem=kv_recv.at[d - 1],
            device_id=(to, tp),
            device_id_type=MESH,
        )

    slab, place_in = me // BACK * BACK, me % BACK
    key_copy(0, BACK, (me + BACK) % NCTX).start()

    def send_own(d, carry):
        @pl.when(place_in + d < BACK)
        def _():
            key_copy(0, d, me + d).start()

        return carry

    def send_previous(d, carry):
        @pl.when(place_in + d >= BACK)
        def _():
            key_copy(BACK, d, slab + (place_in + d) % BACK).start()

        return carry

    lax.fori_loop(1, BACK, send_own, 0)
    w_copy.start()
    for load in loads[4:]:
        load.wait()

    def doc_row(block):
        row = jnp.concatenate([docs[pl.ds(2 * block, 1), :], docs[pl.ds(2 * block + 1, 1), :]], axis=1)
        return jnp.broadcast_to(row, (HD, ROWS))

    far = jnp.where(jnp.transpose(doc_row(me).astype(F32)) == lane.astype(F32), 0.0, -FAR).astype(BF16)

    def queries(h, carry):
        rows = pl.ds(pl.multiple_of(h * ROWS, ROWS), ROWS)
        qx[rows, 0:HD] = rotate(q_in[:, pl.ds(pl.multiple_of(h * HD, HD), HD)])
        qx[rows, HD : 2 * HD] = far
        return carry

    lax.fori_loop(0, HEADS, queries, 0)
    key_copy(0, BACK, me).wait_recv()
    lax.fori_loop(1, BACK, send_previous, 0)

    doc_iota = iota((HD, ROWS), 0)

    def features(d, carry):
        feat[d] = jnp.where(doc_row((me - d + NCTX) % NCTX) == doc_iota, 1.0, 0.0).astype(BF16)
        return carry

    lax.fori_loop(0, BACK + 1, features, 0)

    square_r, square_c = iota((ROWS, ROWS), 0), iota((ROWS, ROWS), 1)
    lists = jnp.concatenate(
        [bl[pl.ds(0, NCTX, stride=2), :], bl[pl.ds(1, NCTX, stride=2), :]], axis=1
    )
    before = jnp.where(square_r < square_c, 1.0, 0.0).astype(BF16)
    local[...] = ((lists & 255) + 1).astype(F32)
    slot_iota = iota((SLOTS, ROWS), 0).astype(F32)
    lane_next = (iota((SLOTS, ROWS), 1) + 1).astype(F32)
    for n, source in enumerate((me, twin)):
        held = (lists >> 8) == source
        rank = jnp.dot(jnp.where(held, 1.0, 0.0).astype(BF16), before, preferred_element_type=F32)
        code[n] = jnp.where(held, rank, -1.0)

    def pack_rows(o, carry):
        at = pl.multiple_of(((o // 8 * 4 + o % 4) * 2 + (o // 4) % 2) * SLOTS, SLOTS)
        for n in range(2):
            hit = code[n, pl.ds(o, 1), :] == slot_iota
            token = jnp.sum(jnp.where(hit, local[pl.ds(o, 1), :], 0.0), axis=1, keepdims=True)
            pack_m[n, pl.ds(at, SLOTS), :] = jnp.where(token == lane_next, 1.0, 0.0).astype(BF16)
        return carry

    lax.fori_loop(0, NCTX, pack_rows, 0, unroll=4)

    wide = iota((ROWS, NCTX * SLOTS), 1).astype(F32)

    def unpack_rows(l, carry):
        owner = me // 8 * 8 + l * 4 + me % 4
        own = jnp.concatenate([bl[pl.ds(2 * owner, 1), :], bl[pl.ds(2 * owner + 1, 1), :]], axis=1) >> 8
        source_row = own.astype(F32)
        source_col = jnp.sum(jnp.where(square_r == square_c, source_row, 0.0), axis=1, keepdims=True)
        earlier = (source_row == source_col) & (square_c < square_r)
        slot_col = jnp.sum(jnp.where(earlier, 1.0, 0.0), axis=1, keepdims=True)
        spot = ((((own >> 3) * 4 + (own & 3)) * 2 + ((own >> 2) & 1)) * SLOTS).astype(F32)
        spot_col = jnp.sum(jnp.where(square_r == square_c, spot, 0.0), axis=1, keepdims=True)
        place = spot_col + slot_col
        unpack_m[l] = jnp.where(wide == place, 1.0, 0.0).astype(BF16)
        return carry

    lax.fori_loop(0, 2, unpack_rows, 0)

    factor = math.log2(math.e) / math.sqrt(HD)
    chunk_rows = PER_CHUNK * ROWS

    def score_own(c, carry):
        keys = jnp.concatenate([kv[0, 0:HD, :], feat[0]], axis=0)
        rows = pl.ds(pl.multiple_of(c * chunk_rows, chunk_rows), chunk_rows)
        part = jnp.dot(qx[rows, :], keys, preferred_element_type=F32) * factor
        allowed = iota((chunk_rows, ROWS), 1) <= (iota((chunk_rows, ROWS), 0) & (ROWS - 1))
        part = jnp.where(allowed, part, -2.0 * FAR)
        scores[c, 0] = part
        tops[c] = jnp.maximum(part[:, 0:HD], part[:, HD:])
        return carry

    lax.fori_loop(0, CHUNKS, score_own, 0)

    def score(i, carry):
        d = (i + BACK - 1) % BACK + 1

        @pl.when(i > 0)
        def _():
            key_copy(0, d, me).wait_recv()

        keys = jnp.concatenate([kv[d, 0:HD, :], feat[d]], axis=0)
        for c in range(CHUNKS):
            rows = slice(c * chunk_rows, (c + 1) * chunk_rows)
            part = jnp.dot(qx[rows, :], keys, preferred_element_type=F32) * factor
            scores[c, d] = part
            tops[c] = jnp.maximum(tops[c], jnp.maximum(part[:, 0:HD], part[:, HD:]))
        return carry

    lax.fori_loop(0, BACK, score, 0)

    def attend(c):
        ones = jnp.ones((ROWS, HD), BF16)
        vals = []
        for d in range(BACK + 1):
            block = jnp.concatenate([kv[d, HD : 2 * HD, 0:HD], kv[d, HD : 2 * HD, HD : 2 * HD]], axis=0)
            vals.append(jnp.concatenate([block, ones], axis=1))
        vals = jnp.concatenate(vals, axis=0)
        part = []
        for h in range(PER_CHUNK):
            rows = slice(h * ROWS, (h + 1) * ROWS)
            top = jnp.max(tops[c, rows, :], axis=1, keepdims=True)
            weights = [jnp.exp2(scores[c, d, rows, :] - top).astype(BF16) for d in range(BACK + 1)]
            mixed = jnp.dot(jnp.concatenate(weights, axis=1), vals, preferred_element_type=F32)
            part.append((mixed[:, 0:HD] / mixed[:, HD : 2 * HD]).astype(BF16))
        part = jnp.concatenate(part, axis=1)
        pair[c, lo] = part
        swap(c).start()
        spread(c, 0)

    def swap(c):
        return pltpu.make_async_remote_copy(
            src_ref=pair.at[c, lo],
            dst_ref=pair.at[c, lo],
            send_sem=p_send.at[c],
            recv_sem=p_recv.at[c],
            device_id=(twin, tp),
            device_id_type=MESH,
        )

    def spread(c, n):
        source_lo = lo if n == 0 else 1 - lo
        rows = jnp.dot(pack_m[n], pair[c, source_lo], preferred_element_type=F32).astype(BF16)
        packed[c, n] = rows.reshape(PLANE, 2, SLOTS, WIDTH)
        landed[c, :, mine_xy, source_lo] = packed[c, n, mine_xy]

        def send(xy, inner_carry):
            pltpu.make_async_remote_copy(
                src_ref=packed.at[c, n, xy],
                dst_ref=landed.at[c, :, mine_xy, source_lo],
                send_sem=a_send.at[c],
                recv_sem=a_recv.at[c],
                device_id=(in_plane(xy), tp),
                device_id_type=MESH,
            ).start()
            return inner_carry

        others(send)

    def spread_twin(c):
        swap(c).wait_recv()
        spread(c, 1)

    def hand(c):
        return pltpu.make_async_remote_copy(
            src_ref=merged.at[c],
            dst_ref=gath.at[c, tp],
            send_sem=h_send.at[c],
            recv_sem=h_recv.at[c],
            device_id=(twin, across),
            device_id_type=MESH,
        )

    def share(c, slot, n):
        return pltpu.make_async_remote_copy(
            src_ref=gath.at[c, slot],
            dst_ref=gath.at[c, slot],
            send_sem=c_send.at[c, n],
            recv_sem=c_recv.at[c, n],
            device_id=(me, mate),
            device_id_type=MESH,
        )

    def whole(c):
        return packed.at[c, :, pl.ds(0, PLANE - 1)]

    def unpack(c):
        pltpu.make_async_copy(whole(c), whole(c), a_recv.at[c]).wait()

        def merge(l):
            rows = landed[c, l].reshape(NCTX * SLOTS, WIDTH)
            return jnp.dot(unpack_m[l], rows, preferred_element_type=F32).astype(BF16)

        merged[c] = merge(1 - lo)
        hand(c).start()
        gath[c, tp] = merge(lo)
        share(c, tp, 0).start()

    def forward(c):
        hand(c).wait_recv()
        share(c, across, 1).start()

    def project(c, final):
        share(c, mate, 0).wait_recv()
        share(c, across_mate, 1).wait_recv()
        rows = jnp.concatenate([gath[c, t] for t in range(4)], axis=1)

        def columns(n, carry):
            cols = pl.ds(pl.multiple_of(n * 512, 512), 512)
            part = [
                w[pl.ds(pl.multiple_of(t * HEADS * HD + c * WIDTH, WIDTH), WIDTH), cols] for t in range(4)
            ]
            total = jnp.dot(rows, jnp.concatenate(part, axis=0), preferred_element_type=F32) + acc[:, cols]
            if final:
                out[:, cols] = total.astype(BF16)
            else:
                acc[:, cols] = total
            return carry

        lax.fori_loop(0, OUT // 512, columns, 0)

    def step(s, carry):
        @pl.when((s >= LAG) & (s < CHUNKS + LAG))
        def _():
            unpack(s - LAG)

        @pl.when(s < CHUNKS)
        def _():
            attend(s)

        @pl.when((s >= 1) & (s < CHUNKS + 1))
        def _():
            spread_twin(s - 1)

        @pl.when((s >= LAG + 1) & (s < CHUNKS + LAG + 1))
        def _():
            forward(s - LAG - 1)

        @pl.when(s == LAG + 1)
        def _():
            w_copy.wait()

        @pl.when(s >= LAG + 2)
        def _():
            project(s - LAG - 2, False)

        return carry

    acc[...] = jnp.zeros((ROWS, OUT), F32)
    lax.fori_loop(0, CHUNKS + LAG + 1, step, 0)
    project(CHUNKS - 1, True)

    for d in range(1, BACK + 1):
        key_copy(0, d, me).wait_send()
    for c in range(CHUNKS):
        swap(c).wait_send()
        pltpu.make_async_copy(whole(c), whole(c), a_send.at[c]).wait()
        hand(c).wait_send()
        share(c, tp, 0).wait_send()
        share(c, across, 1).wait_send()


def on_device(balance_list, doc_ids, raw_queries, raw_keys, values, out_weight):
    inner, outer = rope_tables()
    vmem = pl.BlockSpec(memory_space=pltpu.VMEM)
    dma = pltpu.SemaphoreType.DMA
    return pl.pallas_call(
        kernel,
        out_shape=jax.ShapeDtypeStruct((ROWS, OUT), BF16),
        in_specs=[pl.BlockSpec(memory_space=pl.ANY)] * 8,
        out_specs=vmem,
        scratch_shapes=[
            pltpu.VMEM((64, 128), jnp.int32),
            pltpu.VMEM((64, 128), jnp.int32),
            pltpu.VMEM((ROWS, HEADS * HD), BF16),
            pltpu.VMEM((ROWS, HD), BF16),
            pltpu.VMEM((ROWS, HD), BF16),
            pltpu.VMEM((2, ROWS, HD), F32),
            pltpu.VMEM((2, NCTX, HD), F32),
            pltpu.VMEM((HEADS * ROWS, 2 * HD), BF16),
            pltpu.VMEM((BACK + 1, ROWS, 2 * HD), BF16),
            pltpu.VMEM((BACK + 1, HD, ROWS), BF16),
            pltpu.VMEM((CHUNKS, BACK + 1, PER_CHUNK * ROWS, ROWS), F32),
            pltpu.VMEM((CHUNKS, PER_CHUNK * ROWS, HD), F32),
            pltpu.VMEM((2, NCTX, ROWS), F32),
            pltpu.VMEM((NCTX, ROWS), F32),
            pltpu.VMEM((2, NCTX * SLOTS, ROWS), BF16),
            pltpu.VMEM((2, ROWS, NCTX * SLOTS), BF16),
            pltpu.VMEM((CHUNKS, 2, ROWS, WIDTH), BF16),
            pltpu.VMEM((CHUNKS, 2, PLANE, 2, SLOTS, WIDTH), BF16),
            pltpu.VMEM((CHUNKS, 2, PLANE, 2, SLOTS, WIDTH), BF16),
            pltpu.VMEM((CHUNKS, ROWS, WIDTH), BF16),
            pltpu.VMEM((CHUNKS, 4, ROWS, WIDTH), BF16),
            pltpu.VMEM((4096, OUT), BF16),
            pltpu.VMEM((ROWS, OUT), F32),
            dma((BACK,)), dma((BACK,)),
            dma((CHUNKS,)), dma((CHUNKS,)),
            dma((CHUNKS,)), dma((CHUNKS,)),
            dma((CHUNKS,)), dma((CHUNKS,)),
            dma((CHUNKS, 2)), dma((CHUNKS, 2)),
            dma,
            dma((7,)),
        ],
        compiler_params=pltpu.CompilerParams(
            collective_id=0, has_side_effects=True, vmem_limit_bytes=60 * 1024 * 1024
        ),
        cost_estimate=pl.CostEstimate(
            flops=7_000_000_000, bytes_accessed=19_000_000, transcendentals=4_700_000
        ),
    )(
        balance_list.reshape(64, 128), doc_ids.reshape(64, 128), raw_queries, raw_keys, values,
        jnp.asarray(inner), jnp.asarray(outer), out_weight,
    )


def solution(mesh):
    in_specs = (P(), P(), P("ctx", "tp"), P("ctx", "tp"), P("ctx", "tp"), P(None, "tp"))
    out_specs = P("ctx", "tp")
    return jax.shard_map(
        on_device, mesh=mesh, in_specs=in_specs, out_specs=out_specs, check_vma=False
    )
```

```python
import functools
import math

import jax
import jax.numpy as jnp
import numpy as np
from jax import lax
from jax.experimental import pallas as pl
from jax.experimental.pallas import tpu as pltpu
from jax.sharding import PartitionSpec as P

MESH = pl.DeviceIdType.MESH
HD = 128
NCTX = 32
ROWS = 256
HEADS = 8
BACK = 8
SLOTS = 16
CHUNKS = 4
LAG = 3
PER_CHUNK = HEADS // CHUNKS
WIDTH = HEADS * HD // CHUNKS
OUT = 2048
FAR = 1048576.0
ROPE_BASE = 500000.0
F32 = jnp.float32
BF16 = jnp.bfloat16


def rope_tables():
    freq = ROPE_BASE ** (-(np.arange(HD // 2, dtype=np.float64) * 2.0 / HD))
    freq = np.concatenate([freq, freq])[None, :]
    inner = np.arange(ROWS, dtype=np.float64)[:, None] * freq
    outer = (np.arange(NCTX, dtype=np.float64) * ROWS)[:, None] * freq
    inner = np.stack([np.cos(inner), np.sin(inner)]).astype(np.float32)
    outer = np.stack([np.cos(outer), np.sin(outer)]).astype(np.float32)
    return inner, outer


def iota(shape, dim):
    return lax.broadcasted_iota(jnp.int32, shape, dim)


def kernel(
    bl_h, docs_h, q_h, k_h, v_h, inner_h, outer_h, w_hbm, out,
    bl, docs, q_in, k_in, v_in, inner, outer,
    qx, kv, feat, scores, tops, code, local, pack_m, unpack_m, packed, landed, merged, gath, w, acc,
    kv_send, kv_recv, a_send, a_recv, n_send, n_recv, z_send, z_recv, c_send, c_recv, f_send, f_recv, w_sem, in_sem,
):
    me = lax.axis_index("ctx")
    tp = lax.axis_index("tp")
    hi, core = tp // 2, tp % 2
    mate = hi * 2 + 1 - core
    across = (1 - hi) * 2 + core
    across_mate = (1 - hi) * 2 + 1 - core
    twin = me + 4 - 8 * ((me // 4) % 2)

    w_copy = pltpu.make_async_copy(w_hbm, w, w_sem)
    pairs = (
        (k_h, k_in), (inner_h, inner), (outer_h, outer), (v_h, v_in), (q_h, q_in), (docs_h, docs), (bl_h, bl)
    )
    loads = [pltpu.make_async_copy(a, b, in_sem.at[n]) for n, (a, b) in enumerate(pairs)]
    for load in loads:
        load.start()

    barrier = pltpu.get_barrier_semaphore()

    def others(body):
        lax.fori_loop(1, NCTX, lambda d, carry: body(lax.rem(me + d, NCTX), carry), 0, unroll=NCTX - 1)

    def greet(to, carry):
        pl.semaphore_signal(barrier, inc=1, device_id=(to, tp), device_id_type=MESH)
        return carry

    others(greet)
    pl.semaphore_signal(barrier, inc=1, device_id=(me, mate), device_id_type=MESH)
    pl.semaphore_signal(barrier, inc=1, device_id=(twin, across), device_id_type=MESH)

    for load in loads[:4]:
        load.wait()
    cos_o = outer[0, pl.ds(me, 1), :]
    sin_o = outer[1, pl.ds(me, 1), :]
    cos = cos_o * inner[0] - sin_o * inner[1]
    sin = sin_o * inner[0] + cos_o * inner[1]
    lane = iota((ROWS, HD), 1)
    sin = jnp.where(lane < HD // 2, -sin, sin)

    def rotate(x):
        x = x.astype(F32)
        return (x * cos + pltpu.roll(x, HD // 2, 1) * sin).astype(BF16)

    kv[0, 0:HD, :] = jnp.transpose(rotate(k_in[...]).astype(F32)).astype(BF16)
    kv[0, HD : 2 * HD, 0:HD] = v_in[0:HD, :]
    kv[0, HD : 2 * HD, HD : 2 * HD] = v_in[HD : 2 * HD, :]

    pl.semaphore_wait(barrier, NCTX + 1)

    def key_copy(source, d, to, sem=None):
        return pltpu.make_async_remote_copy(
            src_ref=kv.at[source],
            dst_ref=kv.at[d],
            send_sem=kv_send.at[d - 1 if sem is None else sem],
            recv_sem=kv_recv.at[d - 1],
            device_id=(to, tp),
            device_id_type=MESH,
        )

    slab, place_in = me // BACK * BACK, me % BACK

    def direct(d):
        skip_two = (d == 2) & (place_in != 6)
        skip_six = (d == 6) & (place_in != 1)
        return jnp.logical_not(skip_two | skip_six)

    key_copy(0, BACK, (me + BACK) % NCTX).start()

    def send_own(d, carry):
        @pl.when((place_in + d < BACK) & direct(d))
        def _():
            key_copy(0, d, me + d).start()

        return carry

    def send_previous(n, carry):
        d = BACK - n

        @pl.when((place_in + d >= BACK) & direct(d))
        def _():
            key_copy(BACK, d, slab + (place_in + d) % BACK).start()

        return carry

    relay_two = key_copy(1, 2, slab + (place_in + 1) % BACK, BACK)
    relay_six = key_copy(7, 6, slab + (place_in + 7) % BACK, BACK + 1)

    lax.fori_loop(1, BACK, send_own, 0)
    w_copy.start()
    for load in loads[4:]:
        load.wait()

    def doc_row(block):
        row = jnp.concatenate([docs[pl.ds(2 * block, 1), :], docs[pl.ds(2 * block + 1, 1), :]], axis=1)
        return jnp.broadcast_to(row, (HD, ROWS))

    far = jnp.where(jnp.transpose(doc_row(me).astype(F32)) == lane.astype(F32), 0.0, -FAR).astype(BF16)

    def queries(h, carry):
        rows = pl.ds(pl.multiple_of(h * ROWS, ROWS), ROWS)
        qx[rows, 0:HD] = rotate(q_in[:, pl.ds(pl.multiple_of(h * HD, HD), HD)])
        qx[rows, HD : 2 * HD] = far
        return carry

    lax.fori_loop(0, HEADS, queries, 0)
    key_copy(0, BACK, me).wait_recv()
    lax.fori_loop(1, BACK, send_previous, 0)

    doc_iota = iota((HD, ROWS), 0)

    def features(d, carry):
        feat[d] = jnp.where(doc_row((me - d + NCTX) % NCTX) == doc_iota, 1.0, 0.0).astype(BF16)
        return carry

    lax.fori_loop(0, BACK + 1, features, 0)

    square_r, square_c = iota((ROWS, ROWS), 0), iota((ROWS, ROWS), 1)
    lists = jnp.concatenate(
        [bl[pl.ds(0, NCTX, stride=2), :], bl[pl.ds(1, NCTX, stride=2), :]], axis=1
    )
    mine = (lists >> 8) == me
    before = jnp.where(square_r < square_c, 1.0, 0.0).astype(BF16)
    rank = jnp.dot(jnp.where(mine, 1.0, 0.0).astype(BF16), before, preferred_element_type=F32)
    code[...] = jnp.where(mine, rank, -1.0)
    local[...] = ((lists & 255) + 1).astype(F32)
    slot_iota = iota((SLOTS, ROWS), 0).astype(F32)
    lane_next = (iota((SLOTS, ROWS), 1) + 1).astype(F32)

    def pack_rows(o, carry):
        hit = code[pl.ds(o, 1), :] == slot_iota
        token = jnp.sum(jnp.where(hit, local[pl.ds(o, 1), :], 0.0), axis=1, keepdims=True)
        at = pl.multiple_of((o + 4 - 8 * ((o // 4) % 2)) * SLOTS, SLOTS)
        pack_m[pl.ds(at, SLOTS), :] = jnp.where(token == lane_next, 1.0, 0.0).astype(BF16)
        return carry

    lax.fori_loop(0, NCTX, pack_rows, 0, unroll=8)

    own = jnp.concatenate([bl[pl.ds(2 * twin, 1), :], bl[pl.ds(2 * twin + 1, 1), :]], axis=1)
    source_row = (own >> 8).astype(F32)
    source_col = jnp.sum(jnp.where(square_r == square_c, source_row, 0.0), axis=1, keepdims=True)
    earlier = (source_row == source_col) & (square_c < square_r)
    slot_col = jnp.sum(jnp.where(earlier, 1.0, 0.0), axis=1, keepdims=True)
    place = source_col * SLOTS + slot_col
    wide = iota((ROWS, NCTX * SLOTS), 1).astype(F32)
    unpack_m[...] = jnp.where(wide == place, 1.0, 0.0).astype(BF16)

    factor = math.log2(math.e) / math.sqrt(HD)
    chunk_rows = PER_CHUNK * ROWS

    def score_own(c, carry):
        keys = jnp.concatenate([kv[0, 0:HD, :], feat[0]], axis=0)
        rows = pl.ds(pl.multiple_of(c * chunk_rows, chunk_rows), chunk_rows)
        part = jnp.dot(qx[rows, :], keys, preferred_element_type=F32) * factor
        allowed = iota((chunk_rows, ROWS), 1) <= (iota((chunk_rows, ROWS), 0) & (ROWS - 1))
        part = jnp.where(allowed, part, -2.0 * FAR)
        scores[c, 0] = part
        tops[c] = jnp.maximum(part[:, 0:HD], part[:, HD:])
        return carry

    lax.fori_loop(0, CHUNKS, score_own, 0)

    def score(i, carry):
        third, seventh, last = (i + 6) // 8 - (i + 5) // 8, (i + 2) // 8, (i + 1) // 8
        d = (i + BACK - 1) % BACK + 1 + 5 * third - 4 * seventh + 3 * last

        @pl.when(i > 0)
        def _():
            key_copy(0, d, me).wait_recv()

        @pl.when((d == 1) & (place_in != 7))
        def _():
            relay_two.start()

        @pl.when((d == 7) & (place_in != 0))
        def _():
            relay_six.start()

        keys = jnp.concatenate([kv[d, 0:HD, :], feat[d]], axis=0)
        for c in range(CHUNKS):
            rows = slice(c * chunk_rows, (c + 1) * chunk_rows)
            part = jnp.dot(qx[rows, :], keys, preferred_element_type=F32) * factor
            scores[c, d] = part
            tops[c] = jnp.maximum(tops[c], jnp.maximum(part[:, 0:HD], part[:, HD:]))
        return carry

    lax.fori_loop(0, BACK, score, 0)

    def attend(c):
        ones = jnp.ones((ROWS, HD), BF16)
        vals = []
        for d in range(BACK + 1):
            block = jnp.concatenate([kv[d, HD : 2 * HD, 0:HD], kv[d, HD : 2 * HD, HD : 2 * HD]], axis=0)
            vals.append(jnp.concatenate([block, ones], axis=1))
        vals = jnp.concatenate(vals, axis=0)
        part = []
        for h in range(PER_CHUNK):
            rows = slice(h * ROWS, (h + 1) * ROWS)
            top = jnp.max(tops[c, rows, :], axis=1, keepdims=True)
            weights = [jnp.exp2(scores[c, d, rows, :] - top).astype(BF16) for d in range(BACK + 1)]
            mixed = jnp.dot(jnp.concatenate(weights, axis=1), vals, preferred_element_type=F32)
            part.append((mixed[:, 0:HD] / mixed[:, HD : 2 * HD]).astype(BF16))
        part = jnp.concatenate(part, axis=1)
        rows = jnp.dot(pack_m[...], part, preferred_element_type=F32).astype(BF16)
        packed[c] = rows.reshape(NCTX, SLOTS, WIDTH)
        landed[c, me] = packed[c, me]

        def send(to, inner_carry):
            pltpu.make_async_remote_copy(
                src_ref=packed.at[c, to],
                dst_ref=landed.at[c, me],
                send_sem=a_send.at[c],
                recv_sem=a_recv.at[c],
                device_id=(to, tp),
                device_id_type=MESH,
            ).start()
            return inner_carry

        others(send)

    def hand(c, to, sems):
        return pltpu.make_async_remote_copy(
            src_ref=merged.at[c],
            dst_ref=gath.at[c, tp],
            send_sem=sems[0].at[c],
            recv_sem=sems[1].at[c],
            device_id=(twin, to),
            device_id_type=MESH,
        )

    near, far_off, mate_near, mate_far = (n_send, n_recv), (z_send, z_recv), (c_send, c_recv), (f_send, f_recv)

    def share(c, slot, sems):
        return pltpu.make_async_remote_copy(
            src_ref=gath.at[c, slot],
            dst_ref=gath.at[c, slot],
            send_sem=sems[0].at[c],
            recv_sem=sems[1].at[c],
            device_id=(me, mate),
            device_id_type=MESH,
        )

    def unpack(c):
        rest = packed.at[c, pl.ds(0, NCTX - 1)]
        pltpu.make_async_copy(rest, rest, a_recv.at[c]).wait()
        rows = jnp.dot(unpack_m[...], landed[c].reshape(NCTX * SLOTS, WIDTH), preferred_element_type=F32)
        merged[c] = rows.astype(BF16)
        hand(c, tp, near).start()
        hand(c, across, far_off).start()

    def forward(c):
        hand(c, tp, near).wait_recv()
        share(c, tp, mate_near).start()
        hand(c, across, far_off).wait_recv()
        share(c, across, mate_far).start()

    def project(c, final):
        share(c, mate, mate_near).wait_recv()
        share(c, across_mate, mate_far).wait_recv()
        rows = jnp.concatenate([gath[c, t] for t in range(4)], axis=1)

        def columns(n, carry):
            cols = pl.ds(pl.multiple_of(n * 512, 512), 512)
            part = [
                w[pl.ds(pl.multiple_of(t * HEADS * HD + c * WIDTH, WIDTH), WIDTH), cols] for t in range(4)
            ]
            total = jnp.dot(rows, jnp.concatenate(part, axis=0), preferred_element_type=F32) + acc[:, cols]
            if final:
                out[:, cols] = total.astype(BF16)
            else:
                acc[:, cols] = total
            return carry

        lax.fori_loop(0, OUT // 512, columns, 0)

    def step(s, carry):
        @pl.when((s >= LAG) & (s < CHUNKS + LAG))
        def _():
            unpack(s - LAG)

        @pl.when(s < CHUNKS)
        def _():
            attend(s)

        @pl.when((s >= LAG + 1) & (s < CHUNKS + LAG + 1))
        def _():
            forward(s - LAG - 1)

        @pl.when(s == LAG + 1)
        def _():
            w_copy.wait()

        @pl.when(s >= LAG + 2)
        def _():
            project(s - LAG - 2, False)

        return carry

    acc[...] = jnp.zeros((ROWS, OUT), F32)
    lax.fori_loop(0, CHUNKS + LAG + 1, step, 0)
    project(CHUNKS - 1, True)

    def sent(d, carry):
        @pl.when(direct(d))
        def _():
            key_copy(0, d, me).wait_send()

        return carry

    lax.fori_loop(1, BACK + 1, sent, 0)
    pl.when(place_in != 7)(relay_two.wait_send)
    pl.when(place_in != 0)(relay_six.wait_send)
    for c in range(CHUNKS):
        rest = packed.at[c, pl.ds(0, NCTX - 1)]
        pltpu.make_async_copy(rest, rest, a_send.at[c]).wait()
        hand(c, tp, near).wait_send()
        hand(c, across, far_off).wait_send()
        share(c, tp, mate_near).wait_send()
        share(c, across, mate_far).wait_send()


def on_device(balance_list, doc_ids, raw_queries, raw_keys, values, out_weight):
    inner, outer = rope_tables()
    vmem = pl.BlockSpec(memory_space=pltpu.VMEM)
    dma = pltpu.SemaphoreType.DMA
    return pl.pallas_call(
        kernel,
        out_shape=jax.ShapeDtypeStruct((ROWS, OUT), BF16),
        in_specs=[pl.BlockSpec(memory_space=pl.ANY)] * 8,
        out_specs=vmem,
        scratch_shapes=[
            pltpu.VMEM((64, 128), jnp.int32),
            pltpu.VMEM((64, 128), jnp.int32),
            pltpu.VMEM((ROWS, HEADS * HD), BF16),
            pltpu.VMEM((ROWS, HD), BF16),
            pltpu.VMEM((ROWS, HD), BF16),
            pltpu.VMEM((2, ROWS, HD), F32),
            pltpu.VMEM((2, NCTX, HD), F32),
            pltpu.VMEM((HEADS * ROWS, 2 * HD), BF16),
            pltpu.VMEM((BACK + 1, ROWS, 2 * HD), BF16),
            pltpu.VMEM((BACK + 1, HD, ROWS), BF16),
            pltpu.VMEM((CHUNKS, BACK + 1, PER_CHUNK * ROWS, ROWS), F32),
            pltpu.VMEM((CHUNKS, PER_CHUNK * ROWS, HD), F32),
            pltpu.VMEM((NCTX, ROWS), F32),
            pltpu.VMEM((NCTX, ROWS), F32),
            pltpu.VMEM((NCTX * SLOTS, ROWS), BF16),
            pltpu.VMEM((ROWS, NCTX * SLOTS), BF16),
            pltpu.VMEM((CHUNKS, NCTX, SLOTS, WIDTH), BF16),
            pltpu.VMEM((CHUNKS, NCTX, SLOTS, WIDTH), BF16),
            pltpu.VMEM((CHUNKS, ROWS, WIDTH), BF16),
            pltpu.VMEM((CHUNKS, 4, ROWS, WIDTH), BF16),
            pltpu.VMEM((4096, OUT), BF16),
            pltpu.VMEM((ROWS, OUT), F32),
            dma((BACK + 2,)), dma((BACK,)),
            dma((CHUNKS,)), dma((CHUNKS,)),
            dma((CHUNKS,)), dma((CHUNKS,)),
            dma((CHUNKS,)), dma((CHUNKS,)),
            dma((CHUNKS,)), dma((CHUNKS,)),
            dma((CHUNKS,)), dma((CHUNKS,)),
            dma,
            dma((7,)),
        ],
        compiler_params=pltpu.CompilerParams(
            collective_id=0, has_side_effects=True, vmem_limit_bytes=60 * 1024 * 1024
        ),
        cost_estimate=pl.CostEstimate(
            flops=7_000_000_000, bytes_accessed=19_000_000, transcendentals=4_700_000
        ),
    )(
        balance_list.reshape(64, 128), doc_ids.reshape(64, 128), raw_queries, raw_keys, values,
        jnp.asarray(inner), jnp.asarray(outer), out_weight,
    )


def solution(mesh):
    in_specs = (P(), P(), P("ctx", "tp"), P("ctx", "tp"), P("ctx", "tp"), P(None, "tp"))
    out_specs = P("ctx", "tp")
    return jax.shard_map(
        on_device, mesh=mesh, in_specs=in_specs, out_specs=out_specs, check_vma=False
    )
```

```python
import functools
import math

import jax
import jax.numpy as jnp
import numpy as np
from jax import lax
from jax.experimental import pallas as pl
from jax.experimental.pallas import tpu as pltpu
from jax.sharding import PartitionSpec as P

MESH = pl.DeviceIdType.MESH
HD = 128
NCTX = 32
ROWS = 256
HEADS = 8
BACK = 8
SLOTS = 16
CHUNKS = 4
LAG = 3
PER_CHUNK = HEADS // CHUNKS
WIDTH = HEADS * HD // CHUNKS
OUT = 2048
FAR = 1048576.0
ROPE_BASE = 500000.0
F32 = jnp.float32
BF16 = jnp.bfloat16


def hops(d):
    return min(d % 4, 4 - d % 4) + min(d // 8, 4 - d // 8) + d // 4 % 2


FAR_FIRST = sorted(range(1, NCTX), key=hops, reverse=True)


def rope_tables():
    freq = ROPE_BASE ** (-(np.arange(HD // 2, dtype=np.float64) * 2.0 / HD))
    freq = np.concatenate([freq, freq])[None, :]
    inner = np.arange(ROWS, dtype=np.float64)[:, None] * freq
    outer = (np.arange(NCTX, dtype=np.float64) * ROWS)[:, None] * freq
    inner = np.stack([np.cos(inner), np.sin(inner)]).astype(np.float32)
    outer = np.stack([np.cos(outer), np.sin(outer)]).astype(np.float32)
    return inner, outer


def iota(shape, dim):
    return lax.broadcasted_iota(jnp.int32, shape, dim)


def kernel(
    bl_h, docs_h, q_h, k_h, v_h, inner_h, outer_h, w_hbm, out,
    bl, docs, q_in, k_in, v_in, inner, outer,
    qx, kv, feat, scores, tops, code, local, pack_m, unpack_m, packed, landed, merged, gath, w, acc,
    kv_send, kv_recv, a_send, a_recv, n_send, n_recv, z_send, z_recv, c_send, c_recv, f_send, f_recv, w_sem, in_sem,
):
    me = lax.axis_index("ctx")
    tp = lax.axis_index("tp")
    hi, core = tp // 2, tp % 2
    mate = hi * 2 + 1 - core
    across = (1 - hi) * 2 + core
    across_mate = (1 - hi) * 2 + 1 - core
    twin = me + 4 - 8 * ((me // 4) % 2)

    w_copy = pltpu.make_async_copy(w_hbm, w, w_sem)
    pairs = (
        (k_h, k_in), (inner_h, inner), (outer_h, outer), (v_h, v_in), (q_h, q_in), (docs_h, docs), (bl_h, bl)
    )
    loads = [pltpu.make_async_copy(a, b, in_sem.at[n]) for n, (a, b) in enumerate(pairs)]
    for load in loads:
        load.start()

    barrier = pltpu.get_barrier_semaphore()

    def others(body):
        for d in FAR_FIRST:
            body(lax.rem(me + d, NCTX), 0)

    def greet(to, carry):
        pl.semaphore_signal(barrier, inc=1, device_id=(to, tp), device_id_type=MESH)
        return carry

    others(greet)
    pl.semaphore_signal(barrier, inc=1, device_id=(me, mate), device_id_type=MESH)
    pl.semaphore_signal(barrier, inc=1, device_id=(twin, across), device_id_type=MESH)

    for load in loads[:4]:
        load.wait()
    cos_o = outer[0, pl.ds(me, 1), :]
    sin_o = outer[1, pl.ds(me, 1), :]
    cos = cos_o * inner[0] - sin_o * inner[1]
    sin = sin_o * inner[0] + cos_o * inner[1]
    lane = iota((ROWS, HD), 1)
    sin = jnp.where(lane < HD // 2, -sin, sin)

    def rotate(x):
        x = x.astype(F32)
        return (x * cos + pltpu.roll(x, HD // 2, 1) * sin).astype(BF16)

    kv[0, 0:HD, :] = jnp.transpose(rotate(k_in[...]).astype(F32)).astype(BF16)
    kv[0, HD : 2 * HD, 0:HD] = v_in[0:HD, :]
    kv[0, HD : 2 * HD, HD : 2 * HD] = v_in[HD : 2 * HD, :]

    pl.semaphore_wait(barrier, NCTX + 1)

    def key_copy(source, d, to, sem=None):
        return pltpu.make_async_remote_copy(
            src_ref=kv.at[source],
            dst_ref=kv.at[d],
            send_sem=kv_send.at[d - 1 if sem is None else sem],
            recv_sem=kv_recv.at[d - 1],
            device_id=(to, tp),
            device_id_type=MESH,
        )

    slab, place_in = me // BACK * BACK, me % BACK

    def direct(d):
        skip_two = (d == 2) & (place_in != 6)
        skip_six = (d == 6) & (place_in != 1)
        return jnp.logical_not(skip_two | skip_six)

    key_copy(0, BACK, (me + BACK) % NCTX).start()

    def send_own(d, carry):
        @pl.when((place_in + d < BACK) & direct(d))
        def _():
            key_copy(0, d, me + d).start()

        return carry

    def send_previous(n, carry):
        d = BACK - n

        @pl.when((place_in + d >= BACK) & direct(d))
        def _():
            key_copy(BACK, d, slab + (place_in + d) % BACK).start()

        return carry

    relay_two = key_copy(1, 2, slab + (place_in + 1) % BACK, BACK)
    relay_six = key_copy(7, 6, slab + (place_in + 7) % BACK, BACK + 1)

    lax.fori_loop(1, BACK, send_own, 0)
    w_copy.start()
    for load in loads[4:]:
        load.wait()

    def doc_row(block):
        row = jnp.concatenate([docs[pl.ds(2 * block, 1), :], docs[pl.ds(2 * block + 1, 1), :]], axis=1)
        return jnp.broadcast_to(row, (HD, ROWS))

    far = jnp.where(jnp.transpose(doc_row(me).astype(F32)) == lane.astype(F32), 0.0, -FAR).astype(BF16)

    def queries(h, carry):
        rows = pl.ds(pl.multiple_of(h * ROWS, ROWS), ROWS)
        qx[rows, 0:HD] = rotate(q_in[:, pl.ds(pl.multiple_of(h * HD, HD), HD)])
        qx[rows, HD : 2 * HD] = far
        return carry

    lax.fori_loop(0, HEADS, queries, 0)
    key_copy(0, BACK, me).wait_recv()
    lax.fori_loop(1, BACK, send_previous, 0)

    doc_iota = iota((HD, ROWS), 0)

    def features(d, carry):
        feat[d] = jnp.where(doc_row((me - d + NCTX) % NCTX) == doc_iota, 1.0, 0.0).astype(BF16)
        return carry

    lax.fori_loop(0, BACK + 1, features, 0)

    square_r, square_c = iota((ROWS, ROWS), 0), iota((ROWS, ROWS), 1)
    lists = jnp.concatenate(
        [bl[pl.ds(0, NCTX, stride=2), :], bl[pl.ds(1, NCTX, stride=2), :]], axis=1
    )
    mine = (lists >> 8) == me
    before = jnp.where(square_r < square_c, 1.0, 0.0).astype(BF16)
    rank = jnp.dot(jnp.where(mine, 1.0, 0.0).astype(BF16), before, preferred_element_type=F32)
    code[...] = jnp.where(mine, rank, -1.0)
    local[...] = ((lists & 255) + 1).astype(F32)
    slot_iota = iota((SLOTS, ROWS), 0).astype(F32)
    lane_next = (iota((SLOTS, ROWS), 1) + 1).astype(F32)

    def pack_rows(o, carry):
        hit = code[pl.ds(o, 1), :] == slot_iota
        token = jnp.sum(jnp.where(hit, local[pl.ds(o, 1), :], 0.0), axis=1, keepdims=True)
        at = pl.multiple_of((o + 4 - 8 * ((o // 4) % 2)) * SLOTS, SLOTS)
        pack_m[pl.ds(at, SLOTS), :] = jnp.where(token == lane_next, 1.0, 0.0).astype(BF16)
        return carry

    lax.fori_loop(0, NCTX, pack_rows, 0, unroll=8)

    own = jnp.concatenate([bl[pl.ds(2 * twin, 1), :], bl[pl.ds(2 * twin + 1, 1), :]], axis=1)
    source_row = (own >> 8).astype(F32)
    source_col = jnp.sum(jnp.where(square_r == square_c, source_row, 0.0), axis=1, keepdims=True)
    earlier = (source_row == source_col) & (square_c < square_r)
    slot_col = jnp.sum(jnp.where(earlier, 1.0, 0.0), axis=1, keepdims=True)
    place = source_col * SLOTS + slot_col
    wide = iota((ROWS, NCTX * SLOTS), 1).astype(F32)
    unpack_m[...] = jnp.where(wide == place, 1.0, 0.0).astype(BF16)

    factor = math.log2(math.e) / math.sqrt(HD)
    chunk_rows = PER_CHUNK * ROWS

    def score_own(c, carry):
        keys = jnp.concatenate([kv[0, 0:HD, :], feat[0]], axis=0)
        rows = pl.ds(pl.multiple_of(c * chunk_rows, chunk_rows), chunk_rows)
        part = jnp.dot(qx[rows, :], keys, preferred_element_type=F32) * factor
        allowed = iota((chunk_rows, ROWS), 1) <= (iota((chunk_rows, ROWS), 0) & (ROWS - 1))
        part = jnp.where(allowed, part, -2.0 * FAR)
        scores[c, 0] = part
        tops[c] = jnp.maximum(part[:, 0:HD], part[:, HD:])
        return carry

    lax.fori_loop(0, CHUNKS, score_own, 0)

    def score(i, carry):
        third, seventh, last = (i + 6) // 8 - (i + 5) // 8, (i + 2) // 8, (i + 1) // 8
        d = (i + BACK - 1) % BACK + 1 + 5 * third - 4 * seventh + 3 * last

        @pl.when(i > 0)
        def _():
            key_copy(0, d, me).wait_recv()

        @pl.when((d == 1) & (place_in != 7))
        def _():
            relay_two.start()

        @pl.when((d == 7) & (place_in != 0))
        def _():
            relay_six.start()

        keys = jnp.concatenate([kv[d, 0:HD, :], feat[d]], axis=0)
        for c in range(CHUNKS):
            rows = slice(c * chunk_rows, (c + 1) * chunk_rows)
            part = jnp.dot(qx[rows, :], keys, preferred_element_type=F32) * factor
            scores[c, d] = part
            tops[c] = jnp.maximum(tops[c], jnp.maximum(part[:, 0:HD], part[:, HD:]))
        return carry

    lax.fori_loop(0, BACK, score, 0)

    def attend(c):
        ones = jnp.ones((ROWS, HD), BF16)
        vals = []
        for d in range(BACK + 1):
            block = jnp.concatenate([kv[d, HD : 2 * HD, 0:HD], kv[d, HD : 2 * HD, HD : 2 * HD]], axis=0)
            vals.append(jnp.concatenate([block, ones], axis=1))
        vals = jnp.concatenate(vals, axis=0)
        part = []
        for h in range(PER_CHUNK):
            rows = slice(h * ROWS, (h + 1) * ROWS)
            top = jnp.max(tops[c, rows, :], axis=1, keepdims=True)
            weights = [jnp.exp2(scores[c, d, rows, :] - top).astype(BF16) for d in range(BACK + 1)]
            mixed = jnp.dot(jnp.concatenate(weights, axis=1), vals, preferred_element_type=F32)
            part.append((mixed[:, 0:HD] / mixed[:, HD : 2 * HD]).astype(BF16))
        part = jnp.concatenate(part, axis=1)
        rows = jnp.dot(pack_m[...], part, preferred_element_type=F32).astype(BF16)
        packed[c] = rows.reshape(NCTX, SLOTS, WIDTH)
        landed[c, me] = packed[c, me]

        def send(to, inner_carry):
            pltpu.make_async_remote_copy(
                src_ref=packed.at[c, to],
                dst_ref=landed.at[c, me],
                send_sem=a_send.at[c],
                recv_sem=a_recv.at[c],
                device_id=(to, tp),
                device_id_type=MESH,
            ).start()
            return inner_carry

        others(send)

    def hand(c, to, sems):
        return pltpu.make_async_remote_copy(
            src_ref=merged.at[c],
            dst_ref=gath.at[c, tp],
            send_sem=sems[0].at[c],
            recv_sem=sems[1].at[c],
            device_id=(twin, to),
            device_id_type=MESH,
        )

    near, far_off, mate_near, mate_far = (n_send, n_recv), (z_send, z_recv), (c_send, c_recv), (f_send, f_recv)

    def share(c, slot, sems):
        return pltpu.make_async_remote_copy(
            src_ref=gath.at[c, slot],
            dst_ref=gath.at[c, slot],
            send_sem=sems[0].at[c],
            recv_sem=sems[1].at[c],
            device_id=(me, mate),
            device_id_type=MESH,
        )

    def unpack(c):
        rest = packed.at[c, pl.ds(0, NCTX - 1)]
        pltpu.make_async_copy(rest, rest, a_recv.at[c]).wait()
        rows = jnp.dot(unpack_m[...], landed[c].reshape(NCTX * SLOTS, WIDTH), preferred_element_type=F32)
        merged[c] = rows.astype(BF16)
        hand(c, tp, near).start()
        hand(c, across, far_off).start()

    def forward(c):
        hand(c, tp, near).wait_recv()
        share(c, tp, mate_near).start()
        hand(c, across, far_off).wait_recv()
        share(c, across, mate_far).start()

    def add_columns(c, slots, target):
        rows = jnp.concatenate([gath[c, t] for t in slots], axis=1)

        def columns(n, carry):
            cols = pl.ds(pl.multiple_of(n * 512, 512), 512)
            part = [w[pl.ds(pl.multiple_of(t * HEADS * HD + c * WIDTH, WIDTH), WIDTH), cols] for t in slots]
            total = jnp.dot(rows, jnp.concatenate(part, axis=0), preferred_element_type=F32) + acc[:, cols]
            target[:, cols] = total.astype(target.dtype)
            return carry

        lax.fori_loop(0, OUT // 512, columns, 0, unroll=2)

    def from_mate(c):
        share(c, mate, mate_near).wait_recv()
        share(c, across_mate, mate_far).wait_recv()

    def project(c):
        from_mate(c)
        add_columns(c, range(4), acc)

    def step(s, carry):
        @pl.when((s >= LAG) & (s < CHUNKS + LAG))
        def _():
            unpack(s - LAG)

        @pl.when(s < CHUNKS)
        def _():
            attend(s)

        @pl.when((s >= LAG + 1) & (s < CHUNKS + LAG + 1))
        def _():
            forward(s - LAG - 1)

        @pl.when(s == LAG + 1)
        def _():
            w_copy.wait()

        @pl.when(s >= LAG + 2)
        def _():
            project(s - LAG - 2)

        return carry

    acc[...] = jnp.zeros((ROWS, OUT), F32)
    lax.fori_loop(0, CHUNKS + LAG + 1, step, 0)
    add_columns(CHUNKS - 1, (tp, across), acc)
    from_mate(CHUNKS - 1)
    add_columns(CHUNKS - 1, (mate, across_mate), out)

    def sent(d, carry):
        @pl.when(direct(d))
        def _():
            key_copy(0, d, me).wait_send()

        return carry

    lax.fori_loop(1, BACK + 1, sent, 0)
    pl.when(place_in != 7)(relay_two.wait_send)
    pl.when(place_in != 0)(relay_six.wait_send)
    for c in range(CHUNKS):
        rest = packed.at[c, pl.ds(0, NCTX - 1)]
        pltpu.make_async_copy(rest, rest, a_send.at[c]).wait()
        hand(c, tp, near).wait_send()
        hand(c, across, far_off).wait_send()
        share(c, tp, mate_near).wait_send()
        share(c, across, mate_far).wait_send()


def on_device(balance_list, doc_ids, raw_queries, raw_keys, values, out_weight):
    inner, outer = rope_tables()
    vmem = pl.BlockSpec(memory_space=pltpu.VMEM)
    dma = pltpu.SemaphoreType.DMA
    return pl.pallas_call(
        kernel,
        out_shape=pltpu.VMEM((ROWS, OUT), BF16),
        in_specs=[pl.BlockSpec(memory_space=pl.ANY)] * 8,
        out_specs=vmem,
        scratch_shapes=[
            pltpu.VMEM((64, 128), jnp.int32),
            pltpu.VMEM((64, 128), jnp.int32),
            pltpu.VMEM((ROWS, HEADS * HD), BF16),
            pltpu.VMEM((ROWS, HD), BF16),
            pltpu.VMEM((ROWS, HD), BF16),
            pltpu.VMEM((2, ROWS, HD), F32),
            pltpu.VMEM((2, NCTX, HD), F32),
            pltpu.VMEM((HEADS * ROWS, 2 * HD), BF16),
            pltpu.VMEM((BACK + 1, ROWS, 2 * HD), BF16),
            pltpu.VMEM((BACK + 1, HD, ROWS), BF16),
            pltpu.VMEM((CHUNKS, BACK + 1, PER_CHUNK * ROWS, ROWS), F32),
            pltpu.VMEM((CHUNKS, PER_CHUNK * ROWS, HD), F32),
            pltpu.VMEM((NCTX, ROWS), F32),
            pltpu.VMEM((NCTX, ROWS), F32),
            pltpu.VMEM((NCTX * SLOTS, ROWS), BF16),
            pltpu.VMEM((ROWS, NCTX * SLOTS), BF16),
            pltpu.VMEM((CHUNKS, NCTX, SLOTS, WIDTH), BF16),
            pltpu.VMEM((CHUNKS, NCTX, SLOTS, WIDTH), BF16),
            pltpu.VMEM((CHUNKS, ROWS, WIDTH), BF16),
            pltpu.VMEM((CHUNKS, 4, ROWS, WIDTH), BF16),
            pltpu.VMEM((4096, OUT), BF16),
            pltpu.VMEM((ROWS, OUT), F32),
            dma((BACK + 2,)), dma((BACK,)),
            dma((CHUNKS,)), dma((CHUNKS,)),
            dma((CHUNKS,)), dma((CHUNKS,)),
            dma((CHUNKS,)), dma((CHUNKS,)),
            dma((CHUNKS,)), dma((CHUNKS,)),
            dma((CHUNKS,)), dma((CHUNKS,)),
            dma,
            dma((7,)),
        ],
        compiler_params=pltpu.CompilerParams(
            collective_id=0, has_side_effects=True, vmem_limit_bytes=60 * 1024 * 1024
        ),
        cost_estimate=pl.CostEstimate(
            flops=7_000_000_000, bytes_accessed=19_000_000, transcendentals=4_700_000
        ),
    )(
        balance_list.reshape(64, 128), doc_ids.reshape(64, 128), raw_queries, raw_keys, values,
        jnp.asarray(inner), jnp.asarray(outer), out_weight,
    )


def solution(mesh):
    in_specs = (P(), P(), P("ctx", "tp"), P("ctx", "tp"), P("ctx", "tp"), P(None, "tp"))
    out_specs = P("ctx", "tp")
    return jax.shard_map(
        on_device, mesh=mesh, in_specs=in_specs, out_specs=out_specs, check_vma=False
    )
```

```python
import functools
import math

import jax
import jax.numpy as jnp
import numpy as np
from jax import lax
from jax.experimental import pallas as pl
from jax.experimental.pallas import tpu as pltpu
from jax.sharding import PartitionSpec as P

MESH = pl.DeviceIdType.MESH
HD = 128
NCTX = 32
ROWS = 256
HEADS = 8
BACK = 8
SLOTS = 16
CHUNKS = 4
LAG = 3
PER_CHUNK = HEADS // CHUNKS
WIDTH = HEADS * HD // CHUNKS
OUT = 2048
FAR = 1048576.0
ROPE_BASE = 500000.0
F32 = jnp.float32
BF16 = jnp.bfloat16


def hops(d):
    return min(d % 4, 4 - d % 4) + min(d // 8, 4 - d // 8) + d // 4 % 2


FAR_FIRST = sorted(range(1, NCTX), key=hops, reverse=True)


def rope_tables():
    freq = ROPE_BASE ** (-(np.arange(HD // 2, dtype=np.float64) * 2.0 / HD))
    freq = np.concatenate([freq, freq])[None, :]
    inner = np.arange(ROWS, dtype=np.float64)[:, None] * freq
    outer = (np.arange(NCTX, dtype=np.float64) * ROWS)[:, None] * freq
    inner = np.stack([np.cos(inner), np.sin(inner)]).astype(np.float32)
    outer = np.stack([np.cos(outer), np.sin(outer)]).astype(np.float32)
    return inner, outer


def iota(shape, dim):
    return lax.broadcasted_iota(jnp.int32, shape, dim)


def kernel(
    bl_h, docs_h, q_h, k_h, v_h, inner_h, outer_h, w_hbm, out,
    bl, docs, q_in, k_in, v_in, inner, outer,
    qx, kv, feat, scores, tops, code, local, pack_m, unpack_m, packed, landed, merged, gath, w, acc,
    kv_send, kv_recv, a_send, a_recv, n_send, n_recv, z_send, z_recv, c_send, c_recv, f_send, f_recv, w_sem, in_sem, ready,
):
    me = lax.axis_index("ctx")
    tp = lax.axis_index("tp")
    hi, core = tp // 2, tp % 2
    mate = hi * 2 + 1 - core
    across = (1 - hi) * 2 + core
    across_mate = (1 - hi) * 2 + 1 - core
    twin = me + 4 - 8 * ((me // 4) % 2)

    w_copy = pltpu.make_async_copy(w_hbm, w, w_sem)
    pairs = (
        (k_h, k_in), (inner_h, inner), (outer_h, outer), (v_h, v_in), (q_h, q_in), (docs_h, docs), (bl_h, bl)
    )
    loads = [pltpu.make_async_copy(a, b, in_sem.at[n]) for n, (a, b) in enumerate(pairs)]
    for load in loads:
        load.start()

    barrier = pltpu.get_barrier_semaphore()

    def others(body):
        for d in FAR_FIRST:
            body(lax.rem(me + d, NCTX), 0)

    slab, place_in = me // BACK * BACK, me % BACK
    above, below = (me + BACK) % NCTX, (me + NCTX - BACK) % NCTX

    def greet(d, carry):
        to = slab + (place_in + d) % BACK
        pl.semaphore_signal(barrier, inc=1, device_id=(to, tp), device_id_type=MESH)
        return carry

    for who in ((above, tp), (below, tp), (me, mate), (twin, across)):
        pl.semaphore_signal(barrier, inc=1, device_id=who, device_id_type=MESH)
    lax.fori_loop(1, BACK, greet, 0)

    def tell(n):
        for to in (above, below):
            pl.semaphore_signal(ready.at[n], inc=1, device_id=(to, tp), device_id_type=MESH)

    for load in loads[:4]:
        load.wait()
    cos_o = outer[0, pl.ds(me, 1), :]
    sin_o = outer[1, pl.ds(me, 1), :]
    cos = cos_o * inner[0] - sin_o * inner[1]
    sin = sin_o * inner[0] + cos_o * inner[1]
    lane = iota((ROWS, HD), 1)
    sin = jnp.where(lane < HD // 2, -sin, sin)

    def rotate(x):
        x = x.astype(F32)
        return (x * cos + pltpu.roll(x, HD // 2, 1) * sin).astype(BF16)

    kv[0, 0:HD, :] = jnp.transpose(rotate(k_in[...]).astype(F32)).astype(BF16)
    kv[0, HD : 2 * HD, 0:HD] = v_in[0:HD, :]
    kv[0, HD : 2 * HD, HD : 2 * HD] = v_in[HD : 2 * HD, :]

    pl.semaphore_wait(barrier, BACK - 1 + 4)

    def key_copy(source, d, to):
        return pltpu.make_async_remote_copy(
            src_ref=kv.at[source],
            dst_ref=kv.at[d],
            send_sem=kv_send.at[d - 1],
            recv_sem=kv_recv.at[d - 1],
            device_id=(to, tp),
            device_id_type=MESH,
        )

    key_copy(0, BACK, above).start()
    tell(0)

    def send_own(d, carry):
        @pl.when(place_in + d < BACK)
        def _():
            key_copy(0, d, me + d).start()

        return carry

    def send_previous(d, carry):
        @pl.when(place_in + d >= BACK)
        def _():
            key_copy(BACK, d, slab + (place_in + d) % BACK).start()

        return carry

    lax.fori_loop(1, BACK, send_own, 0)
    w_copy.start()
    for load in loads[4:]:
        load.wait()

    def doc_row(block):
        row = jnp.concatenate([docs[pl.ds(2 * block, 1), :], docs[pl.ds(2 * block + 1, 1), :]], axis=1)
        return jnp.broadcast_to(row, (HD, ROWS))

    far = jnp.where(jnp.transpose(doc_row(me).astype(F32)) == lane.astype(F32), 0.0, -FAR).astype(BF16)

    def queries(h, carry):
        rows = pl.ds(pl.multiple_of(h * ROWS, ROWS), ROWS)
        qx[rows, 0:HD] = rotate(q_in[:, pl.ds(pl.multiple_of(h * HD, HD), HD)])
        qx[rows, HD : 2 * HD] = far
        return carry

    lax.fori_loop(0, HEADS, queries, 0)
    key_copy(0, BACK, me).wait_recv()
    lax.fori_loop(1, BACK, send_previous, 0)

    doc_iota = iota((HD, ROWS), 0)

    def features(d, carry):
        feat[d] = jnp.where(doc_row((me - d + NCTX) % NCTX) == doc_iota, 1.0, 0.0).astype(BF16)
        return carry

    lax.fori_loop(0, BACK + 1, features, 0)

    square_r, square_c = iota((ROWS, ROWS), 0), iota((ROWS, ROWS), 1)
    lists = jnp.concatenate(
        [bl[pl.ds(0, NCTX, stride=2), :], bl[pl.ds(1, NCTX, stride=2), :]], axis=1
    )
    mine = (lists >> 8) == me
    before = jnp.where(square_r < square_c, 1.0, 0.0).astype(BF16)
    rank = jnp.dot(jnp.where(mine, 1.0, 0.0).astype(BF16), before, preferred_element_type=F32)
    code[...] = jnp.where(mine, rank, -1.0)
    local[...] = ((lists & 255) + 1).astype(F32)
    slot_iota = iota((SLOTS, ROWS), 0).astype(F32)
    lane_next = (iota((SLOTS, ROWS), 1) + 1).astype(F32)

    def pack_rows(o, carry):
        hit = code[pl.ds(o, 1), :] == slot_iota
        token = jnp.sum(jnp.where(hit, local[pl.ds(o, 1), :], 0.0), axis=1, keepdims=True)
        at = pl.multiple_of((o + 4 - 8 * ((o // 4) % 2)) * SLOTS, SLOTS)
        pack_m[pl.ds(at, SLOTS), :] = jnp.where(token == lane_next, 1.0, 0.0).astype(BF16)
        return carry

    lax.fori_loop(0, NCTX, pack_rows, 0, unroll=8)

    own = jnp.concatenate([bl[pl.ds(2 * twin, 1), :], bl[pl.ds(2 * twin + 1, 1), :]], axis=1)
    source_row = (own >> 8).astype(F32)
    source_col = jnp.sum(jnp.where(square_r == square_c, source_row, 0.0), axis=1, keepdims=True)
    earlier = (source_row == source_col) & (square_c < square_r)
    slot_col = jnp.sum(jnp.where(earlier, 1.0, 0.0), axis=1, keepdims=True)
    place = source_col * SLOTS + slot_col
    wide = iota((ROWS, NCTX * SLOTS), 1).astype(F32)
    unpack_m[...] = jnp.where(wide == place, 1.0, 0.0).astype(BF16)

    factor = math.log2(math.e) / math.sqrt(HD)
    chunk_rows = PER_CHUNK * ROWS

    def score_own(c, carry):
        keys = jnp.concatenate([kv[0, 0:HD, :], feat[0]], axis=0)
        rows = pl.ds(pl.multiple_of(c * chunk_rows, chunk_rows), chunk_rows)
        part = jnp.dot(qx[rows, :], keys, preferred_element_type=F32) * factor
        allowed = iota((chunk_rows, ROWS), 1) <= (iota((chunk_rows, ROWS), 0) & (ROWS - 1))
        part = jnp.where(allowed, part, -2.0 * FAR)
        scores[c, 0] = part
        tops[c] = jnp.maximum(part[:, 0:HD], part[:, HD:])
        return carry

    lax.fori_loop(0, CHUNKS, score_own, 0)

    def score(i, carry):
        d = (i + BACK - 1) % BACK + 1

        @pl.when(i > 0)
        def _():
            key_copy(0, d, me).wait_recv()

        keys = jnp.concatenate([kv[d, 0:HD, :], feat[d]], axis=0)
        for c in range(CHUNKS):
            rows = slice(c * chunk_rows, (c + 1) * chunk_rows)
            part = jnp.dot(qx[rows, :], keys, preferred_element_type=F32) * factor
            scores[c, d] = part
            tops[c] = jnp.maximum(tops[c], jnp.maximum(part[:, 0:HD], part[:, HD:]))
        return carry

    pl.semaphore_wait(ready.at[0], 2)
    tell(1)
    lax.fori_loop(0, BACK, score, 0)
    pl.semaphore_wait(ready.at[1], 2)

    def attend(c):
        ones = jnp.ones((ROWS, HD), BF16)
        vals = []
        for d in range(BACK + 1):
            block = jnp.concatenate([kv[d, HD : 2 * HD, 0:HD], kv[d, HD : 2 * HD, HD : 2 * HD]], axis=0)
            vals.append(jnp.concatenate([block, ones], axis=1))
        vals = jnp.concatenate(vals, axis=0)
        part = []
        for h in range(PER_CHUNK):
            rows = slice(h * ROWS, (h + 1) * ROWS)
            top = jnp.max(tops[c, rows, :], axis=1, keepdims=True)
            weights = [jnp.exp2(scores[c, d, rows, :] - top).astype(BF16) for d in range(BACK + 1)]
            mixed = jnp.dot(jnp.concatenate(weights, axis=1), vals, preferred_element_type=F32)
            part.append((mixed[:, 0:HD] / mixed[:, HD : 2 * HD]).astype(BF16))
        part = jnp.concatenate(part, axis=1)
        rows = jnp.dot(pack_m[...], part, preferred_element_type=F32).astype(BF16)
        packed[c] = rows.reshape(NCTX, SLOTS, WIDTH)
        landed[c, me] = packed[c, me]

        def send(to, inner_carry):
            pltpu.make_async_remote_copy(
                src_ref=packed.at[c, to],
                dst_ref=landed.at[c, me],
                send_sem=a_send.at[c],
                recv_sem=a_recv.at[c],
                device_id=(to, tp),
                device_id_type=MESH,
            ).start()
            return inner_carry

        others(send)

    def hand(c, to, sems):
        return pltpu.make_async_remote_copy(
            src_ref=merged.at[c],
            dst_ref=gath.at[c, tp],
            send_sem=sems[0].at[c],
            recv_sem=sems[1].at[c],
            device_id=(twin, to),
            device_id_type=MESH,
        )

    near, far_off, mate_near, mate_far = (n_send, n_recv), (z_send, z_recv), (c_send, c_recv), (f_send, f_recv)

    def share(c, slot, sems):
        return pltpu.make_async_remote_copy(
            src_ref=gath.at[c, slot],
            dst_ref=gath.at[c, slot],
            send_sem=sems[0].at[c],
            recv_sem=sems[1].at[c],
            device_id=(me, mate),
            device_id_type=MESH,
        )

    def unpack(c):
        rest = packed.at[c, pl.ds(0, NCTX - 1)]
        pltpu.make_async_copy(rest, rest, a_recv.at[c]).wait()
        rows = jnp.dot(unpack_m[...], landed[c].reshape(NCTX * SLOTS, WIDTH), preferred_element_type=F32)
        merged[c] = rows.astype(BF16)
        hand(c, tp, near).start()
        hand(c, across, far_off).start()

    def forward(c):
        hand(c, tp, near).wait_recv()
        share(c, tp, mate_near).start()
        hand(c, across, far_off).wait_recv()
        share(c, across, mate_far).start()

    def add_columns(c, slots, target):
        rows = jnp.concatenate([gath[c, t] for t in slots], axis=1)

        def columns(n, carry):
            cols = pl.ds(pl.multiple_of(n * 512, 512), 512)
            part = [w[pl.ds(pl.multiple_of(t * HEADS * HD + c * WIDTH, WIDTH), WIDTH), cols] for t in slots]
            total = jnp.dot(rows, jnp.concatenate(part, axis=0), preferred_element_type=F32) + acc[:, cols]
            target[:, cols] = total.astype(target.dtype)
            return carry

        lax.fori_loop(0, OUT // 512, columns, 0, unroll=2)

    def from_mate(c):
        share(c, mate, mate_near).wait_recv()
        share(c, across_mate, mate_far).wait_recv()

    def project(c):
        from_mate(c)
        add_columns(c, range(4), acc)

    def step(s, carry):
        @pl.when((s >= LAG) & (s < CHUNKS + LAG))
        def _():
            unpack(s - LAG)

        @pl.when(s < CHUNKS)
        def _():
            attend(s)

        @pl.when((s >= LAG + 1) & (s < CHUNKS + LAG + 1))
        def _():
            forward(s - LAG - 1)

        @pl.when(s == LAG + 1)
        def _():
            w_copy.wait()

        @pl.when(s >= LAG + 2)
        def _():
            project(s - LAG - 2)

        return carry

    acc[...] = jnp.zeros((ROWS, OUT), F32)
    lax.fori_loop(0, CHUNKS + LAG + 1, step, 0)
    add_columns(CHUNKS - 1, (tp, across), acc)
    from_mate(CHUNKS - 1)
    add_columns(CHUNKS - 1, (mate, across_mate), out)

    for d in range(1, BACK + 1):
        key_copy(0, d, me).wait_send()
    for c in range(CHUNKS):
        rest = packed.at[c, pl.ds(0, NCTX - 1)]
        pltpu.make_async_copy(rest, rest, a_send.at[c]).wait()
        hand(c, tp, near).wait_send()
        hand(c, across, far_off).wait_send()
        share(c, tp, mate_near).wait_send()
        share(c, across, mate_far).wait_send()


def on_device(balance_list, doc_ids, raw_queries, raw_keys, values, out_weight):
    inner, outer = rope_tables()
    vmem = pl.BlockSpec(memory_space=pltpu.VMEM)
    dma = pltpu.SemaphoreType.DMA
    return pl.pallas_call(
        kernel,
        out_shape=pltpu.VMEM((ROWS, OUT), BF16),
        in_specs=[pl.BlockSpec(memory_space=pl.ANY)] * 8,
        out_specs=vmem,
        scratch_shapes=[
            pltpu.VMEM((64, 128), jnp.int32),
            pltpu.VMEM((64, 128), jnp.int32),
            pltpu.VMEM((ROWS, HEADS * HD), BF16),
            pltpu.VMEM((ROWS, HD), BF16),
            pltpu.VMEM((ROWS, HD), BF16),
            pltpu.VMEM((2, ROWS, HD), F32),
            pltpu.VMEM((2, NCTX, HD), F32),
            pltpu.VMEM((HEADS * ROWS, 2 * HD), BF16),
            pltpu.VMEM((BACK + 1, ROWS, 2 * HD), BF16),
            pltpu.VMEM((BACK + 1, HD, ROWS), BF16),
            pltpu.VMEM((CHUNKS, BACK + 1, PER_CHUNK * ROWS, ROWS), F32),
            pltpu.VMEM((CHUNKS, PER_CHUNK * ROWS, HD), F32),
            pltpu.VMEM((NCTX, ROWS), F32),
            pltpu.VMEM((NCTX, ROWS), F32),
            pltpu.VMEM((NCTX * SLOTS, ROWS), BF16),
            pltpu.VMEM((ROWS, NCTX * SLOTS), BF16),
            pltpu.VMEM((CHUNKS, NCTX, SLOTS, WIDTH), BF16),
            pltpu.VMEM((CHUNKS, NCTX, SLOTS, WIDTH), BF16),
            pltpu.VMEM((CHUNKS, ROWS, WIDTH), BF16),
            pltpu.VMEM((CHUNKS, 4, ROWS, WIDTH), BF16),
            pltpu.VMEM((4096, OUT), BF16),
            pltpu.VMEM((ROWS, OUT), F32),
            dma((BACK,)), dma((BACK,)),
            dma((CHUNKS,)), dma((CHUNKS,)),
            dma((CHUNKS,)), dma((CHUNKS,)),
            dma((CHUNKS,)), dma((CHUNKS,)),
            dma((CHUNKS,)), dma((CHUNKS,)),
            dma((CHUNKS,)), dma((CHUNKS,)),
            dma,
            dma((7,)),
            pltpu.SemaphoreType.REGULAR((2,)),
        ],
        compiler_params=pltpu.CompilerParams(
            collective_id=0, has_side_effects=True, vmem_limit_bytes=60 * 1024 * 1024
        ),
        cost_estimate=pl.CostEstimate(
            flops=7_000_000_000, bytes_accessed=19_000_000, transcendentals=4_700_000
        ),
    )(
        balance_list.reshape(64, 128), doc_ids.reshape(64, 128), raw_queries, raw_keys, values,
        jnp.asarray(inner), jnp.asarray(outer), out_weight,
    )


def solution(mesh):
    in_specs = (P(), P(), P("ctx", "tp"), P("ctx", "tp"), P("ctx", "tp"), P(None, "tp"))
    out_specs = P("ctx", "tp")
    return jax.shard_map(
        on_device, mesh=mesh, in_specs=in_specs, out_specs=out_specs, check_vma=False
    )
```

```python
import functools
import math

import jax
import jax.numpy as jnp
import numpy as np
from jax import lax
from jax.experimental import pallas as pl
from jax.experimental.pallas import tpu as pltpu
from jax.sharding import PartitionSpec as P

MESH = pl.DeviceIdType.MESH
HD = 128
NCTX = 32
ROWS = 256
HEADS = 8
BACK = 8
SLOTS = 16
CHUNKS = 4
LAG = 3
EARLY = 2
PER_CHUNK = HEADS // CHUNKS
WIDTH = HEADS * HD // CHUNKS
OUT = 2048
FAR = 1048576.0
ROPE_BASE = 500000.0
F32 = jnp.float32
BF16 = jnp.bfloat16


def hops(d):
    return min(d % 4, 4 - d % 4) + min(d // 8, 4 - d // 8) + d // 4 % 2


FAR_FIRST = sorted(range(1, NCTX), key=hops, reverse=True)


def rope_tables():
    freq = ROPE_BASE ** (-(np.arange(HD // 2, dtype=np.float64) * 2.0 / HD))
    freq = np.concatenate([freq, freq])[None, :]
    inner = np.arange(ROWS, dtype=np.float64)[:, None] * freq
    outer = (np.arange(NCTX, dtype=np.float64) * ROWS)[:, None] * freq
    inner = np.stack([np.cos(inner), np.sin(inner)]).astype(np.float32)
    outer = np.stack([np.cos(outer), np.sin(outer)]).astype(np.float32)
    return inner, outer


def iota(shape, dim):
    return lax.broadcasted_iota(jnp.int32, shape, dim)


def kernel(
    bl_h, docs_h, q_h, k_h, v_h, inner_h, outer_h, w_hbm, out,
    bl, docs, q_in, k_in, v_in, inner, outer,
    qx, kv, feat, scores, tops, code, local, pack_m, unpack_m, packed, landed, merged, gath, w, acc,
    kv_send, kv_recv, a_send, a_recv, n_send, n_recv, z_send, z_recv, c_send, c_recv, f_send, f_recv, w_sem, in_sem, ready,
):
    me = lax.axis_index("ctx")
    tp = lax.axis_index("tp")
    hi, core = tp // 2, tp % 2
    mate = hi * 2 + 1 - core
    across = (1 - hi) * 2 + core
    across_mate = (1 - hi) * 2 + 1 - core
    twin = me + 4 - 8 * ((me // 4) % 2)

    w_copy = pltpu.make_async_copy(w_hbm, w, w_sem)
    pairs = (
        (k_h, k_in), (inner_h, inner), (outer_h, outer), (v_h, v_in), (q_h, q_in), (docs_h, docs), (bl_h, bl)
    )
    loads = [pltpu.make_async_copy(a, b, in_sem.at[n]) for n, (a, b) in enumerate(pairs)]
    for load in loads:
        load.start()

    barrier = pltpu.get_barrier_semaphore()

    def others(body):
        for d in FAR_FIRST:
            body(lax.rem(me + d, NCTX), 0)

    slab, place_in = me // BACK * BACK, me % BACK
    above, below = (me + BACK) % NCTX, (me + NCTX - BACK) % NCTX

    def greet(d, carry):
        to = slab + (place_in + d) % BACK
        pl.semaphore_signal(barrier, inc=1, device_id=(to, tp), device_id_type=MESH)
        return carry

    for who in ((above, tp), (below, tp), (me, mate), (twin, across)):
        pl.semaphore_signal(barrier, inc=1, device_id=who, device_id_type=MESH)
    lax.fori_loop(1, BACK, greet, 0)

    def tell(n):
        for to in (above, below):
            pl.semaphore_signal(ready.at[n], inc=1, device_id=(to, tp), device_id_type=MESH)

    for load in loads[:4]:
        load.wait()
    cos_o = outer[0, pl.ds(me, 1), :]
    sin_o = outer[1, pl.ds(me, 1), :]
    cos = cos_o * inner[0] - sin_o * inner[1]
    sin = sin_o * inner[0] + cos_o * inner[1]
    lane = iota((ROWS, HD), 1)
    sin = jnp.where(lane < HD // 2, -sin, sin)

    def rotate(x):
        x = x.astype(F32)
        return (x * cos + pltpu.roll(x, HD // 2, 1) * sin).astype(BF16)

    kv[0, 0:HD, :] = jnp.transpose(rotate(k_in[...]).astype(F32)).astype(BF16)
    kv[0, HD : 2 * HD, 0:HD] = v_in[0:HD, :]
    kv[0, HD : 2 * HD, HD : 2 * HD] = v_in[HD : 2 * HD, :]

    pl.semaphore_wait(barrier, BACK - 1 + 4)

    def key_copy(source, d, to):
        return pltpu.make_async_remote_copy(
            src_ref=kv.at[source],
            dst_ref=kv.at[d],
            send_sem=kv_send.at[d - 1],
            recv_sem=kv_recv.at[d - 1],
            device_id=(to, tp),
            device_id_type=MESH,
        )

    key_copy(0, BACK, above).start()
    tell(0)

    def send_own(d, carry):
        @pl.when(place_in + d < BACK)
        def _():
            key_copy(0, d, me + d).start()

        return carry

    def send_previous(d, carry):
        @pl.when(place_in + d >= BACK)
        def _():
            key_copy(BACK, d, slab + (place_in + d) % BACK).start()

        return carry

    lax.fori_loop(1, BACK, send_own, 0)
    for load in loads[4:]:
        load.wait()

    def doc_row(block):
        row = jnp.concatenate([docs[pl.ds(2 * block, 1), :], docs[pl.ds(2 * block + 1, 1), :]], axis=1)
        return jnp.broadcast_to(row, (HD, ROWS))

    far = jnp.where(jnp.transpose(doc_row(me).astype(F32)) == lane.astype(F32), 0.0, -FAR).astype(BF16)

    def queries(h, carry):
        rows = pl.ds(pl.multiple_of(h * ROWS, ROWS), ROWS)
        qx[rows, 0:HD] = rotate(q_in[:, pl.ds(pl.multiple_of(h * HD, HD), HD)])
        qx[rows, HD : 2 * HD] = far
        return carry

    lax.fori_loop(0, HEADS, queries, 0)
    key_copy(0, BACK, me).wait_recv()
    lax.fori_loop(1, BACK, send_previous, 0)

    doc_iota = iota((HD, ROWS), 0)

    def features(d, carry):
        feat[d] = jnp.where(doc_row((me - d + NCTX) % NCTX) == doc_iota, 1.0, 0.0).astype(BF16)
        return carry

    lax.fori_loop(0, BACK + 1, features, 0)

    square_r, square_c = iota((ROWS, ROWS), 0), iota((ROWS, ROWS), 1)
    lists = jnp.concatenate(
        [bl[pl.ds(0, NCTX, stride=2), :], bl[pl.ds(1, NCTX, stride=2), :]], axis=1
    )
    mine = (lists >> 8) == me
    before = jnp.where(square_r < square_c, 1.0, 0.0).astype(BF16)
    rank = jnp.dot(jnp.where(mine, 1.0, 0.0).astype(BF16), before, preferred_element_type=F32)
    code[...] = jnp.where(mine, rank, -1.0)
    local[...] = ((lists & 255) + 1).astype(F32)
    slot_iota = iota((SLOTS, ROWS), 0).astype(F32)
    lane_next = (iota((SLOTS, ROWS), 1) + 1).astype(F32)

    def pack_rows(o, carry):
        hit = code[pl.ds(o, 1), :] == slot_iota
        token = jnp.sum(jnp.where(hit, local[pl.ds(o, 1), :], 0.0), axis=1, keepdims=True)
        at = pl.multiple_of((o + 4 - 8 * ((o // 4) % 2)) * SLOTS, SLOTS)
        pack_m[pl.ds(at, SLOTS), :] = jnp.where(token == lane_next, 1.0, 0.0).astype(BF16)
        return carry

    lax.fori_loop(0, NCTX, pack_rows, 0, unroll=8)

    def merge_table():
        own = jnp.concatenate([bl[pl.ds(2 * twin, 1), :], bl[pl.ds(2 * twin + 1, 1), :]], axis=1)
        source_row = (own >> 8).astype(F32)
        source_col = jnp.sum(jnp.where(square_r == square_c, source_row, 0.0), axis=1, keepdims=True)
        earlier = (source_row == source_col) & (square_c < square_r)
        slot_col = jnp.sum(jnp.where(earlier, 1.0, 0.0), axis=1, keepdims=True)
        place = source_col * SLOTS + slot_col
        wide = iota((ROWS, NCTX * SLOTS), 1).astype(F32)
        unpack_m[...] = jnp.where(wide == place, 1.0, 0.0).astype(BF16)

    factor = math.log2(math.e) / math.sqrt(HD)
    chunk_rows = PER_CHUNK * ROWS

    def score_own(c, carry):
        keys = jnp.concatenate([kv[0, 0:HD, :], feat[0]], axis=0)
        rows = pl.ds(pl.multiple_of(c * chunk_rows, chunk_rows), chunk_rows)
        part = jnp.dot(qx[rows, :], keys, preferred_element_type=F32) * factor
        allowed = iota((chunk_rows, ROWS), 1) <= (iota((chunk_rows, ROWS), 0) & (ROWS - 1))
        part = jnp.where(allowed, part, -2.0 * FAR)
        scores[c, 0] = part
        tops[c] = jnp.maximum(part[:, 0:HD], part[:, HD:])
        return carry

    lax.fori_loop(0, EARLY, score_own, 0)

    def score(i, carry):
        d = (i + BACK - 1) % BACK + 1
        part = pl.ds(pl.multiple_of(i * (4096 // BACK), 4096 // BACK), 4096 // BACK)
        pltpu.make_async_copy(w_hbm.at[part, :], w.at[part, :], w_sem).start()

        @pl.when(i > 0)
        def _():
            key_copy(0, d, me).wait_recv()

        keys = jnp.concatenate([kv[d, 0:HD, :], feat[d]], axis=0)
        every = jnp.dot(qx[0 : EARLY * chunk_rows, :], keys, preferred_element_type=F32) * factor
        for c in range(EARLY):
            part = every[c * chunk_rows : (c + 1) * chunk_rows, :]
            scores[c, d] = part
            tops[c] = jnp.maximum(tops[c], jnp.maximum(part[:, 0:HD], part[:, HD:]))
        return carry

    pl.semaphore_wait(ready.at[0], 2)
    tell(1)
    lax.fori_loop(0, BACK, score, 0)
    pl.semaphore_wait(ready.at[1], 2)

    def score_late(c):
        score_own(c, 0)
        rows = pl.ds(pl.multiple_of(c * chunk_rows, chunk_rows), chunk_rows)
        top = tops[c]
        for d in range(1, BACK + 1):
            keys = jnp.concatenate([kv[d, 0:HD, :], feat[d]], axis=0)
            part = jnp.dot(qx[rows, :], keys, preferred_element_type=F32) * factor
            scores[c, d] = part
            top = jnp.maximum(top, jnp.maximum(part[:, 0:HD], part[:, HD:]))
        tops[c] = top

    def attend(c):
        ones = jnp.ones((ROWS, HD), BF16)
        vals = []
        for d in range(BACK + 1):
            block = jnp.concatenate([kv[d, HD : 2 * HD, 0:HD], kv[d, HD : 2 * HD, HD : 2 * HD]], axis=0)
            vals.append(jnp.concatenate([block, ones], axis=1))
        vals = jnp.concatenate(vals, axis=0)
        top = jnp.max(tops[c], axis=1, keepdims=True)
        weights = [jnp.exp2(scores[c, d] - top).astype(BF16) for d in range(BACK + 1)]
        mixed = jnp.dot(jnp.concatenate(weights, axis=1), vals, preferred_element_type=F32)
        mixed = (mixed[:, 0:HD] / mixed[:, HD : 2 * HD]).astype(BF16)
        part = jnp.concatenate([mixed[h * ROWS : (h + 1) * ROWS, :] for h in range(PER_CHUNK)], axis=1)
        rows = jnp.dot(pack_m[...], part, preferred_element_type=F32).astype(BF16)
        packed[c] = rows.reshape(NCTX, SLOTS, WIDTH)
        landed[c, me] = packed[c, me]

        def send(to, inner_carry):
            pltpu.make_async_remote_copy(
                src_ref=packed.at[c, to],
                dst_ref=landed.at[c, me],
                send_sem=a_send.at[c],
                recv_sem=a_recv.at[c],
                device_id=(to, tp),
                device_id_type=MESH,
            ).start()
            return inner_carry

        others(send)

    def hand(c, to, sems):
        return pltpu.make_async_remote_copy(
            src_ref=merged.at[c],
            dst_ref=gath.at[c, tp],
            send_sem=sems[0].at[c],
            recv_sem=sems[1].at[c],
            device_id=(twin, to),
            device_id_type=MESH,
        )

    near, far_off, mate_near, mate_far = (n_send, n_recv), (z_send, z_recv), (c_send, c_recv), (f_send, f_recv)

    def share(c, slot, sems):
        return pltpu.make_async_remote_copy(
            src_ref=gath.at[c, slot],
            dst_ref=gath.at[c, slot],
            send_sem=sems[0].at[c],
            recv_sem=sems[1].at[c],
            device_id=(me, mate),
            device_id_type=MESH,
        )

    def unpack(c):
        rest = packed.at[c, pl.ds(0, NCTX - 1)]
        pltpu.make_async_copy(rest, rest, a_recv.at[c]).wait()
        rows = jnp.dot(unpack_m[...], landed[c].reshape(NCTX * SLOTS, WIDTH), preferred_element_type=F32)
        merged[c] = rows.astype(BF16)
        hand(c, tp, near).start()
        hand(c, across, far_off).start()

    def forward(c):
        hand(c, tp, near).wait_recv()
        share(c, tp, mate_near).start()
        hand(c, across, far_off).wait_recv()
        share(c, across, mate_far).start()

    def add_columns(c, slots, target):
        rows = jnp.concatenate([gath[c, t] for t in slots], axis=1)

        def columns(n, carry):
            cols = pl.ds(pl.multiple_of(n * 512, 512), 512)
            part = [w[pl.ds(pl.multiple_of(t * HEADS * HD + c * WIDTH, WIDTH), WIDTH), cols] for t in slots]
            total = jnp.dot(rows, jnp.concatenate(part, axis=0), preferred_element_type=F32) + acc[:, cols]
            target[:, cols] = total.astype(target.dtype)
            return carry

        lax.fori_loop(0, OUT // 512, columns, 0, unroll=2)

    def from_mate(c):
        share(c, mate, mate_near).wait_recv()
        share(c, across_mate, mate_far).wait_recv()

    def project(c):
        from_mate(c)
        add_columns(c, range(4), acc)

    def step(s, carry):
        @pl.when((s >= LAG) & (s < CHUNKS + LAG))
        def _():
            unpack(s - LAG)

        @pl.when((s >= EARLY) & (s < CHUNKS))
        def _():
            score_late(s)

        @pl.when(s < CHUNKS)
        def _():
            attend(s)

        @pl.when(s == 0)
        def _():
            merge_table()
            acc[...] = jnp.zeros((ROWS, OUT), F32)

        @pl.when((s >= LAG + 1) & (s < CHUNKS + LAG + 1))
        def _():
            forward(s - LAG - 1)

        @pl.when(s == LAG + 1)
        def _():
            w_copy.wait()

        @pl.when(s >= LAG + 2)
        def _():
            project(s - LAG - 2)

        return carry

    lax.fori_loop(0, CHUNKS + LAG + 1, step, 0)
    add_columns(CHUNKS - 1, (tp, across), acc)
    from_mate(CHUNKS - 1)
    add_columns(CHUNKS - 1, (mate, across_mate), out)

    for d in range(1, BACK + 1):
        key_copy(0, d, me).wait_send()
    for c in range(CHUNKS):
        rest = packed.at[c, pl.ds(0, NCTX - 1)]
        pltpu.make_async_copy(rest, rest, a_send.at[c]).wait()
        hand(c, tp, near).wait_send()
        hand(c, across, far_off).wait_send()
        share(c, tp, mate_near).wait_send()
        share(c, across, mate_far).wait_send()


def on_device(balance_list, doc_ids, raw_queries, raw_keys, values, out_weight):
    inner, outer = rope_tables()
    vmem = pl.BlockSpec(memory_space=pltpu.VMEM)
    dma = pltpu.SemaphoreType.DMA
    return pl.pallas_call(
        kernel,
        out_shape=pltpu.VMEM((ROWS, OUT), BF16),
        in_specs=[pl.BlockSpec(memory_space=pl.ANY)] * 8,
        out_specs=vmem,
        scratch_shapes=[
            pltpu.VMEM((64, 128), jnp.int32),
            pltpu.VMEM((64, 128), jnp.int32),
            pltpu.VMEM((ROWS, HEADS * HD), BF16),
            pltpu.VMEM((ROWS, HD), BF16),
            pltpu.VMEM((ROWS, HD), BF16),
            pltpu.VMEM((2, ROWS, HD), F32),
            pltpu.VMEM((2, NCTX, HD), F32),
            pltpu.VMEM((HEADS * ROWS, 2 * HD), BF16),
            pltpu.VMEM((BACK + 1, ROWS, 2 * HD), BF16),
            pltpu.VMEM((BACK + 1, HD, ROWS), BF16),
            pltpu.VMEM((CHUNKS, BACK + 1, PER_CHUNK * ROWS, ROWS), F32),
            pltpu.VMEM((CHUNKS, PER_CHUNK * ROWS, HD), F32),
            pltpu.VMEM((NCTX, ROWS), F32),
            pltpu.VMEM((NCTX, ROWS), F32),
            pltpu.VMEM((NCTX * SLOTS, ROWS), BF16),
            pltpu.VMEM((ROWS, NCTX * SLOTS), BF16),
            pltpu.VMEM((CHUNKS, NCTX, SLOTS, WIDTH), BF16),
            pltpu.VMEM((CHUNKS, NCTX, SLOTS, WIDTH), BF16),
            pltpu.VMEM((CHUNKS, ROWS, WIDTH), BF16),
            pltpu.VMEM((CHUNKS, 4, ROWS, WIDTH), BF16),
            pltpu.VMEM((4096, OUT), BF16),
            pltpu.VMEM((ROWS, OUT), F32),
            dma((BACK,)), dma((BACK,)),
            dma((CHUNKS,)), dma((CHUNKS,)),
            dma((CHUNKS,)), dma((CHUNKS,)),
            dma((CHUNKS,)), dma((CHUNKS,)),
            dma((CHUNKS,)), dma((CHUNKS,)),
            dma((CHUNKS,)), dma((CHUNKS,)),
            dma,
            dma((7,)),
            pltpu.SemaphoreType.REGULAR((2,)),
        ],
        compiler_params=pltpu.CompilerParams(
            collective_id=0, has_side_effects=True, vmem_limit_bytes=60 * 1024 * 1024
        ),
        cost_estimate=pl.CostEstimate(
            flops=7_000_000_000, bytes_accessed=19_000_000, transcendentals=4_700_000
        ),
    )(
        balance_list.reshape(64, 128), doc_ids.reshape(64, 128), raw_queries, raw_keys, values,
        jnp.asarray(inner), jnp.asarray(outer), out_weight,
    )


def solution(mesh):
    in_specs = (P(), P(), P("ctx", "tp"), P("ctx", "tp"), P("ctx", "tp"), P(None, "tp"))
    out_specs = P("ctx", "tp")
    return jax.shard_map(
        on_device, mesh=mesh, in_specs=in_specs, out_specs=out_specs, check_vma=False
    )
```

```python
import functools
import math

import jax
import jax.numpy as jnp
import numpy as np
from jax import lax
from jax.experimental import pallas as pl
from jax.experimental.pallas import tpu as pltpu
from jax.sharding import PartitionSpec as P

MESH = pl.DeviceIdType.MESH
HD = 128
NCTX = 32
ROWS = 256
HEADS = 8
BACK = 8
SLOTS = 16
CHUNKS = 4
LAG = 3
EARLY = 2
PER_CHUNK = HEADS // CHUNKS
WIDTH = HEADS * HD // CHUNKS
OUT = 2048
FAR = 1048576.0
ROPE_BASE = 500000.0
F32 = jnp.float32
BF16 = jnp.bfloat16


def hops(d):
    return min(d % 4, 4 - d % 4) + min(d // 8, 4 - d // 8) + d // 4 % 2


FAR_FIRST = sorted(range(1, NCTX), key=hops, reverse=True)


def rope_tables():
    freq = ROPE_BASE ** (-(np.arange(HD // 2, dtype=np.float64) * 2.0 / HD))
    freq = np.concatenate([freq, freq])[None, :]
    inner = np.arange(ROWS, dtype=np.float64)[:, None] * freq
    outer = (np.arange(NCTX, dtype=np.float64) * ROWS)[:, None] * freq
    inner = np.stack([np.cos(inner), np.sin(inner)]).astype(np.float32)
    outer = np.stack([np.cos(outer), np.sin(outer)]).astype(np.float32)
    return inner, outer


def iota(shape, dim):
    return lax.broadcasted_iota(jnp.int32, shape, dim)


def kernel(
    bl_h, docs_h, q_h, k_h, v_h, inner_h, outer_h, w_hbm, out,
    bl, docs, q_in, k_in, v_in, inner, outer,
    qx, kv, feat, scores, tops, code, local, pack_m, unpack_m, packed, landed, merged, gath, w, acc,
    kv_send, kv_recv, a_send, a_recv, n_send, n_recv, z_send, z_recv, c_send, c_recv, f_send, f_recv, w_sem, in_sem, ready,
):
    me = lax.axis_index("ctx")
    tp = lax.axis_index("tp")
    hi, core = tp // 2, tp % 2
    mate = hi * 2 + 1 - core
    across = (1 - hi) * 2 + core
    across_mate = (1 - hi) * 2 + 1 - core
    twin = me + 4 - 8 * ((me // 4) % 2)

    w_copy = pltpu.make_async_copy(w_hbm, w, w_sem)
    pairs = (
        (k_h, k_in), (inner_h, inner), (outer_h, outer), (v_h, v_in), (q_h, q_in), (docs_h, docs), (bl_h, bl)
    )
    loads = [pltpu.make_async_copy(a, b, in_sem.at[n]) for n, (a, b) in enumerate(pairs)]
    for load in loads:
        load.start()

    barrier = pltpu.get_barrier_semaphore()

    def others(body):
        for d in FAR_FIRST:
            body(lax.rem(me + d, NCTX), 0)

    slab, place_in = me // BACK * BACK, me % BACK
    above, below = (me + BACK) % NCTX, (me + NCTX - BACK) % NCTX

    def greet(d, carry):
        to = slab + (place_in + d) % BACK
        pl.semaphore_signal(barrier, inc=1, device_id=(to, tp), device_id_type=MESH)
        return carry

    for who in ((above, tp), (below, tp), (me, mate), (twin, across)):
        pl.semaphore_signal(barrier, inc=1, device_id=who, device_id_type=MESH)
    lax.fori_loop(1, BACK, greet, 0)

    def tell(n):
        for to in (above, below):
            pl.semaphore_signal(ready.at[n], inc=1, device_id=(to, tp), device_id_type=MESH)

    for load in loads[:4]:
        load.wait()
    cos_o = outer[0, pl.ds(me, 1), :]
    sin_o = outer[1, pl.ds(me, 1), :]
    cos = cos_o * inner[0] - sin_o * inner[1]
    sin = sin_o * inner[0] + cos_o * inner[1]
    lane = iota((ROWS, HD), 1)
    sin = jnp.where(lane < HD // 2, -sin, sin)

    def rotate(x):
        x = x.astype(F32)
        return (x * cos + pltpu.roll(x, HD // 2, 1) * sin).astype(BF16)

    kv[0, 0:HD, :] = jnp.transpose(rotate(k_in[...]).astype(F32)).astype(BF16)
    kv[0, HD : 2 * HD, 0:HD] = v_in[0:HD, :]
    kv[0, HD : 2 * HD, HD : 2 * HD] = v_in[HD : 2 * HD, :]

    pl.semaphore_wait(barrier, BACK - 1 + 4)

    def key_copy(source, d, to):
        return pltpu.make_async_remote_copy(
            src_ref=kv.at[source],
            dst_ref=kv.at[d],
            send_sem=kv_send.at[d - 1],
            recv_sem=kv_recv.at[d - 1],
            device_id=(to, tp),
            device_id_type=MESH,
        )

    key_copy(0, BACK, above).start()
    tell(0)

    def send_own(d, carry):
        @pl.when(place_in + d < BACK)
        def _():
            key_copy(0, d, me + d).start()

        return carry

    def send_previous(d, carry):
        @pl.when(place_in + d >= BACK)
        def _():
            key_copy(BACK, d, slab + (place_in + d) % BACK).start()

        return carry

    lax.fori_loop(1, BACK, send_own, 0)
    for load in loads[4:]:
        load.wait()

    def doc_row(block):
        row = jnp.concatenate([docs[pl.ds(2 * block, 1), :], docs[pl.ds(2 * block + 1, 1), :]], axis=1)
        return jnp.broadcast_to(row, (HD, ROWS))

    far = jnp.where(jnp.transpose(doc_row(me).astype(F32)) == lane.astype(F32), 0.0, -FAR).astype(BF16)

    def queries(h, carry):
        rows = pl.ds(pl.multiple_of(h * ROWS, ROWS), ROWS)
        qx[rows, 0:HD] = rotate(q_in[:, pl.ds(pl.multiple_of(h * HD, HD), HD)])
        qx[rows, HD : 2 * HD] = far
        return carry

    lax.fori_loop(0, HEADS, queries, 0)
    key_copy(0, BACK, me).wait_recv()
    lax.fori_loop(1, BACK, send_previous, 0)

    doc_iota = iota((HD, ROWS), 0)

    def features(d, carry):
        feat[d] = jnp.where(doc_row((me - d + NCTX) % NCTX) == doc_iota, 1.0, 0.0).astype(BF16)
        return carry

    lax.fori_loop(0, BACK + 1, features, 0)

    square_r, square_c = iota((ROWS, ROWS), 0), iota((ROWS, ROWS), 1)
    lists = jnp.concatenate(
        [bl[pl.ds(0, NCTX, stride=2), :], bl[pl.ds(1, NCTX, stride=2), :]], axis=1
    )
    mine = (lists >> 8) == me
    before = jnp.where(square_r < square_c, 1.0, 0.0).astype(BF16)
    rank = jnp.dot(jnp.where(mine, 1.0, 0.0).astype(BF16), before, preferred_element_type=F32)
    code[...] = jnp.where(mine, rank, -1.0)
    local[...] = ((lists & 255) + 1).astype(F32)
    slot_iota = iota((SLOTS, ROWS), 0).astype(F32)
    lane_next = (iota((SLOTS, ROWS), 1) + 1).astype(F32)

    def pack_rows(o, carry):
        hit = code[pl.ds(o, 1), :] == slot_iota
        token = jnp.sum(jnp.where(hit, local[pl.ds(o, 1), :], 0.0), axis=1, keepdims=True)
        at = pl.multiple_of((o + 4 - 8 * ((o // 4) % 2)) * SLOTS, SLOTS)
        pack_m[pl.ds(at, SLOTS), :] = jnp.where(token == lane_next, 1.0, 0.0).astype(BF16)
        return carry

    lax.fori_loop(0, NCTX, pack_rows, 0, unroll=8)

    def merge_table():
        own = jnp.concatenate([bl[pl.ds(2 * twin, 1), :], bl[pl.ds(2 * twin + 1, 1), :]], axis=1)
        source_row = (own >> 8).astype(F32)
        source_col = jnp.sum(jnp.where(square_r == square_c, source_row, 0.0), axis=1, keepdims=True)
        earlier = (source_row == source_col) & (square_c < square_r)
        slot_col = jnp.sum(jnp.where(earlier, 1.0, 0.0), axis=1, keepdims=True)
        place = source_col * SLOTS + slot_col
        wide = iota((ROWS, NCTX * SLOTS), 1).astype(F32)
        unpack_m[...] = jnp.where(wide == place, 1.0, 0.0).astype(BF16)

    factor = math.log2(math.e) / math.sqrt(HD)
    chunk_rows = PER_CHUNK * ROWS

    def score_own(c, carry):
        keys = jnp.concatenate([kv[0, 0:HD, :], feat[0]], axis=0)
        rows = pl.ds(pl.multiple_of(c * chunk_rows, chunk_rows), chunk_rows)
        part = jnp.dot(qx[rows, :], keys, preferred_element_type=F32) * factor
        allowed = iota((chunk_rows, ROWS), 1) <= (iota((chunk_rows, ROWS), 0) & (ROWS - 1))
        part = jnp.where(allowed, part, -2.0 * FAR)
        scores[c, 0] = part
        tops[c] = jnp.maximum(part[:, 0:HD], part[:, HD:])
        return carry

    lax.fori_loop(0, EARLY, score_own, 0)

    def score(i, carry):
        d = (i + BACK - 1) % BACK + 1
        part = pl.ds(pl.multiple_of(i * (4096 // BACK), 4096 // BACK), 4096 // BACK)
        pltpu.make_async_copy(w_hbm.at[part, :], w.at[part, :], w_sem).start()

        @pl.when(i > 0)
        def _():
            key_copy(0, d, me).wait_recv()

        keys = jnp.concatenate([kv[d, 0:HD, :], feat[d]], axis=0)
        for c in range(EARLY):
            rows = slice(c * chunk_rows, (c + 1) * chunk_rows)
            part = jnp.dot(qx[rows, :], keys, preferred_element_type=F32) * factor
            scores[c, d] = part
            tops[c] = jnp.maximum(tops[c], jnp.maximum(part[:, 0:HD], part[:, HD:]))
        return carry

    pl.semaphore_wait(ready.at[0], 2)
    tell(1)
    lax.fori_loop(0, BACK, score, 0)
    pl.semaphore_wait(ready.at[1], 2)

    def score_late(c):
        score_own(c, 0)
        rows = pl.ds(pl.multiple_of(c * chunk_rows, chunk_rows), chunk_rows)
        top = tops[c]
        for d in range(1, BACK + 1):
            keys = jnp.concatenate([kv[d, 0:HD, :], feat[d]], axis=0)
            part = jnp.dot(qx[rows, :], keys, preferred_element_type=F32) * factor
            scores[c, d] = part
            top = jnp.maximum(top, jnp.maximum(part[:, 0:HD], part[:, HD:]))
        tops[c] = top

    def attend(c):
        ones = jnp.ones((ROWS, HD), BF16)
        vals = []
        for d in range(BACK + 1):
            block = jnp.concatenate([kv[d, HD : 2 * HD, 0:HD], kv[d, HD : 2 * HD, HD : 2 * HD]], axis=0)
            vals.append(jnp.concatenate([block, ones], axis=1))
        vals = jnp.concatenate(vals, axis=0)
        part = []
        for h in range(PER_CHUNK):
            rows = slice(h * ROWS, (h + 1) * ROWS)
            top = jnp.max(tops[c, rows, :], axis=1, keepdims=True)
            weights = [jnp.exp2(scores[c, d, rows, :] - top).astype(BF16) for d in range(BACK + 1)]
            mixed = jnp.dot(jnp.concatenate(weights, axis=1), vals, preferred_element_type=F32)
            part.append((mixed[:, 0:HD] / mixed[:, HD : 2 * HD]).astype(BF16))
        part = jnp.concatenate(part, axis=1)
        rows = jnp.dot(pack_m[...], part, preferred_element_type=F32).astype(BF16)
        packed[c] = rows.reshape(NCTX, SLOTS, WIDTH)
        landed[c, me] = packed[c, me]

        def send(to, inner_carry):
            pltpu.make_async_remote_copy(
                src_ref=packed.at[c, to],
                dst_ref=landed.at[c, me],
                send_sem=a_send.at[c],
                recv_sem=a_recv.at[c],
                device_id=(to, tp),
                device_id_type=MESH,
            ).start()
            return inner_carry

        others(send)

    def hand(c, to, sems):
        return pltpu.make_async_remote_copy(
            src_ref=merged.at[c],
            dst_ref=gath.at[c, tp],
            send_sem=sems[0].at[c],
            recv_sem=sems[1].at[c],
            device_id=(twin, to),
            device_id_type=MESH,
        )

    near, far_off, mate_near, mate_far = (n_send, n_recv), (z_send, z_recv), (c_send, c_recv), (f_send, f_recv)

    def share(c, slot, sems):
        return pltpu.make_async_remote_copy(
            src_ref=gath.at[c, slot],
            dst_ref=gath.at[c, slot],
            send_sem=sems[0].at[c],
            recv_sem=sems[1].at[c],
            device_id=(me, mate),
            device_id_type=MESH,
        )

    def unpack(c):
        rest = packed.at[c, pl.ds(0, NCTX - 1)]
        pltpu.make_async_copy(rest, rest, a_recv.at[c]).wait()
        rows = jnp.dot(unpack_m[...], landed[c].reshape(NCTX * SLOTS, WIDTH), preferred_element_type=F32)
        merged[c] = rows.astype(BF16)
        hand(c, tp, near).start()
        hand(c, across, far_off).start()

    def forward(c):
        hand(c, tp, near).wait_recv()
        share(c, tp, mate_near).start()
        hand(c, across, far_off).wait_recv()
        share(c, across, mate_far).start()

    def add_columns(c, slots, target):
        rows = jnp.concatenate([gath[c, t] for t in slots], axis=1)

        def columns(n, carry):
            cols = pl.ds(pl.multiple_of(n * 512, 512), 512)
            part = [w[pl.ds(pl.multiple_of(t * HEADS * HD + c * WIDTH, WIDTH), WIDTH), cols] for t in slots]
            total = jnp.dot(rows, jnp.concatenate(part, axis=0), preferred_element_type=F32) + acc[:, cols]
            target[:, cols] = total.astype(target.dtype)
            return carry

        lax.fori_loop(0, OUT // 512, columns, 0, unroll=4)

    def from_mate(c):
        share(c, mate, mate_near).wait_recv()
        share(c, across_mate, mate_far).wait_recv()

    def project(c):
        from_mate(c)
        add_columns(c, range(4), acc)

    def step(s, carry):
        @pl.when((s >= LAG) & (s < CHUNKS + LAG))
        def _():
            unpack(s - LAG)

        @pl.when((s >= EARLY) & (s < CHUNKS))
        def _():
            score_late(s)

        @pl.when(s < CHUNKS)
        def _():
            attend(s)

        @pl.when(s == 0)
        def _():
            merge_table()
            acc[...] = jnp.zeros((ROWS, OUT), F32)

        @pl.when((s >= LAG + 1) & (s < CHUNKS + LAG + 1))
        def _():
            forward(s - LAG - 1)

        @pl.when(s == LAG + 1)
        def _():
            w_copy.wait()

        @pl.when(s >= LAG + 2)
        def _():
            project(s - LAG - 2)

        return carry

    lax.fori_loop(0, CHUNKS + LAG, step, 0)
    project(CHUNKS - 2)
    forward(CHUNKS - 1)
    add_columns(CHUNKS - 1, (tp, across), acc)
    from_mate(CHUNKS - 1)
    add_columns(CHUNKS - 1, (mate, across_mate), out)

    for d in range(1, BACK + 1):
        key_copy(0, d, me).wait_send()
    for c in range(CHUNKS):
        rest = packed.at[c, pl.ds(0, NCTX - 1)]
        pltpu.make_async_copy(rest, rest, a_send.at[c]).wait()
        hand(c, tp, near).wait_send()
        hand(c, across, far_off).wait_send()
        share(c, tp, mate_near).wait_send()
        share(c, across, mate_far).wait_send()


def on_device(balance_list, doc_ids, raw_queries, raw_keys, values, out_weight):
    inner, outer = rope_tables()
    vmem = pl.BlockSpec(memory_space=pltpu.VMEM)
    dma = pltpu.SemaphoreType.DMA
    return pl.pallas_call(
        kernel,
        out_shape=pltpu.VMEM((ROWS, OUT), BF16),
        in_specs=[pl.BlockSpec(memory_space=pl.ANY)] * 8,
        out_specs=vmem,
        scratch_shapes=[
            pltpu.VMEM((64, 128), jnp.int32),
            pltpu.VMEM((64, 128), jnp.int32),
            pltpu.VMEM((ROWS, HEADS * HD), BF16),
            pltpu.VMEM((ROWS, HD), BF16),
            pltpu.VMEM((ROWS, HD), BF16),
            pltpu.VMEM((2, ROWS, HD), F32),
            pltpu.VMEM((2, NCTX, HD), F32),
            pltpu.VMEM((HEADS * ROWS, 2 * HD), BF16),
            pltpu.VMEM((BACK + 1, ROWS, 2 * HD), BF16),
            pltpu.VMEM((BACK + 1, HD, ROWS), BF16),
            pltpu.VMEM((CHUNKS, BACK + 1, PER_CHUNK * ROWS, ROWS), F32),
            pltpu.VMEM((CHUNKS, PER_CHUNK * ROWS, HD), F32),
            pltpu.VMEM((NCTX, ROWS), F32),
            pltpu.VMEM((NCTX, ROWS), F32),
            pltpu.VMEM((NCTX * SLOTS, ROWS), BF16),
            pltpu.VMEM((ROWS, NCTX * SLOTS), BF16),
            pltpu.VMEM((CHUNKS, NCTX, SLOTS, WIDTH), BF16),
            pltpu.VMEM((CHUNKS, NCTX, SLOTS, WIDTH), BF16),
            pltpu.VMEM((CHUNKS, ROWS, WIDTH), BF16),
            pltpu.VMEM((CHUNKS, 4, ROWS, WIDTH), BF16),
            pltpu.VMEM((4096, OUT), BF16),
            pltpu.VMEM((ROWS, OUT), F32),
            dma((BACK,)), dma((BACK,)),
            dma((CHUNKS,)), dma((CHUNKS,)),
            dma((CHUNKS,)), dma((CHUNKS,)),
            dma((CHUNKS,)), dma((CHUNKS,)),
            dma((CHUNKS,)), dma((CHUNKS,)),
            dma((CHUNKS,)), dma((CHUNKS,)),
            dma,
            dma((7,)),
            pltpu.SemaphoreType.REGULAR((2,)),
        ],
        compiler_params=pltpu.CompilerParams(
            collective_id=0, has_side_effects=True, vmem_limit_bytes=60 * 1024 * 1024
        ),
        cost_estimate=pl.CostEstimate(
            flops=7_000_000_000, bytes_accessed=19_000_000, transcendentals=4_700_000
        ),
    )(
        balance_list.reshape(64, 128), doc_ids.reshape(64, 128), raw_queries, raw_keys, values,
        jnp.asarray(inner), jnp.asarray(outer), out_weight,
    )


def solution(mesh):
    in_specs = (P(), P(), P("ctx", "tp"), P("ctx", "tp"), P("ctx", "tp"), P(None, "tp"))
    out_specs = P("ctx", "tp")
    return jax.shard_map(
        on_device, mesh=mesh, in_specs=in_specs, out_specs=out_specs, check_vma=False
    )
```

```python
import functools
import math

import jax
import jax.numpy as jnp
import numpy as np
from jax import lax
from jax.experimental import pallas as pl
from jax.experimental.pallas import tpu as pltpu
from jax.sharding import PartitionSpec as P

MESH = pl.DeviceIdType.MESH
HD = 128
NCTX = 32
ROWS = 256
HEADS = 8
BACK = 8
SLOTS = 16
CHUNKS = 4
LAG = 3
EARLY = 2
PER_CHUNK = HEADS // CHUNKS
WIDTH = HEADS * HD // CHUNKS
OUT = 2048
FAR = 1048576.0
ROPE_BASE = 500000.0
F32 = jnp.float32
BF16 = jnp.bfloat16


def hops(d):
    return min(d % 4, 4 - d % 4) + min(d // 8, 4 - d // 8) + d // 4 % 2


FAR_FIRST = sorted(range(1, NCTX), key=hops, reverse=True)


def rope_tables():
    freq = ROPE_BASE ** (-(np.arange(HD // 2, dtype=np.float64) * 2.0 / HD))
    freq = np.concatenate([freq, freq])[None, :]
    inner = np.arange(ROWS, dtype=np.float64)[:, None] * freq
    outer = (np.arange(NCTX, dtype=np.float64) * ROWS)[:, None] * freq
    inner = np.stack([np.cos(inner), np.sin(inner)]).astype(np.float32)
    outer = np.stack([np.cos(outer), np.sin(outer)]).astype(np.float32)
    return inner, outer


def iota(shape, dim):
    return lax.broadcasted_iota(jnp.int32, shape, dim)


def kernel(
    bl_h, docs_h, q_h, k_h, v_h, inner_h, outer_h, w_hbm, out,
    bl, docs, q_in, k_in, v_in, inner, outer,
    qx, kv, feat, scores, tops, code, local, pack_m, unpack_m, packed, landed, gath, w, acc,
    kv_send, kv_recv, a_send, a_recv, z_send, z_recv, c_send, c_recv, f_send, f_recv, w_sem, in_sem, ready,
):
    me = lax.axis_index("ctx")
    tp = lax.axis_index("tp")
    hi, core = tp // 2, tp % 2
    mate = hi * 2 + 1 - core
    across = (1 - hi) * 2 + core
    across_mate = (1 - hi) * 2 + 1 - core

    w_copy = pltpu.make_async_copy(w_hbm, w, w_sem)
    pairs = (
        (k_h, k_in), (inner_h, inner), (outer_h, outer), (v_h, v_in), (q_h, q_in), (docs_h, docs), (bl_h, bl)
    )
    loads = [pltpu.make_async_copy(a, b, in_sem.at[n]) for n, (a, b) in enumerate(pairs)]
    for load in loads:
        load.start()

    barrier = pltpu.get_barrier_semaphore()

    def others(body):
        for d in FAR_FIRST:
            body(lax.rem(me + d, NCTX), 0)

    slab, place_in = me // BACK * BACK, me % BACK
    above, below = (me + BACK) % NCTX, (me + NCTX - BACK) % NCTX

    def greet(d, carry):
        to = slab + (place_in + d) % BACK
        pl.semaphore_signal(barrier, inc=1, device_id=(to, tp), device_id_type=MESH)
        return carry

    for who in ((above, tp), (below, tp), (me, mate), (me, across)):
        pl.semaphore_signal(barrier, inc=1, device_id=who, device_id_type=MESH)
    lax.fori_loop(1, BACK, greet, 0)

    def tell(n):
        for to in (above, below):
            pl.semaphore_signal(ready.at[n], inc=1, device_id=(to, tp), device_id_type=MESH)

    for load in loads[:4]:
        load.wait()
    cos_o = outer[0, pl.ds(me, 1), :]
    sin_o = outer[1, pl.ds(me, 1), :]
    cos = cos_o * inner[0] - sin_o * inner[1]
    sin = sin_o * inner[0] + cos_o * inner[1]
    lane = iota((ROWS, HD), 1)
    sin = jnp.where(lane < HD // 2, -sin, sin)

    def rotate(x):
        x = x.astype(F32)
        return (x * cos + pltpu.roll(x, HD // 2, 1) * sin).astype(BF16)

    kv[0, 0:HD, :] = jnp.transpose(rotate(k_in[...]).astype(F32)).astype(BF16)
    kv[0, HD : 2 * HD, 0:HD] = v_in[0:HD, :]
    kv[0, HD : 2 * HD, HD : 2 * HD] = v_in[HD : 2 * HD, :]

    pl.semaphore_wait(barrier, BACK - 1 + 4)

    def key_copy(source, d, to):
        return pltpu.make_async_remote_copy(
            src_ref=kv.at[source],
            dst_ref=kv.at[d],
            send_sem=kv_send.at[d - 1],
            recv_sem=kv_recv.at[d - 1],
            device_id=(to, tp),
            device_id_type=MESH,
        )

    key_copy(0, BACK, above).start()
    tell(0)

    def send_own(d, carry):
        @pl.when(place_in + d < BACK)
        def _():
            key_copy(0, d, me + d).start()

        return carry

    def send_previous(d, carry):
        @pl.when(place_in + d >= BACK)
        def _():
            key_copy(BACK, d, slab + (place_in + d) % BACK).start()

        return carry

    lax.fori_loop(1, BACK, send_own, 0)
    for load in loads[4:]:
        load.wait()

    def doc_row(block):
        row = jnp.concatenate([docs[pl.ds(2 * block, 1), :], docs[pl.ds(2 * block + 1, 1), :]], axis=1)
        return jnp.broadcast_to(row, (HD, ROWS))

    far = jnp.where(jnp.transpose(doc_row(me).astype(F32)) == lane.astype(F32), 0.0, -FAR).astype(BF16)

    def queries(h, carry):
        rows = pl.ds(pl.multiple_of(h * ROWS, ROWS), ROWS)
        qx[rows, 0:HD] = rotate(q_in[:, pl.ds(pl.multiple_of(h * HD, HD), HD)])
        qx[rows, HD : 2 * HD] = far
        return carry

    def pass_on():
        key_copy(0, BACK, me).wait_recv()
        lax.fori_loop(1, BACK, send_previous, 0)

    pl.when(me >= BACK)(pass_on)
    lax.fori_loop(0, HEADS, queries, 0)
    pl.when(me < BACK)(pass_on)

    doc_iota = iota((HD, ROWS), 0)

    def features(d, carry):
        feat[d] = jnp.where(doc_row((me - d + NCTX) % NCTX) == doc_iota, 1.0, 0.0).astype(BF16)
        return carry

    lax.fori_loop(0, BACK + 1, features, 0)

    square_r, square_c = iota((ROWS, ROWS), 0), iota((ROWS, ROWS), 1)
    lists = jnp.concatenate(
        [bl[pl.ds(0, NCTX, stride=2), :], bl[pl.ds(1, NCTX, stride=2), :]], axis=1
    )
    mine = (lists >> 8) == me
    before = jnp.where(square_r < square_c, 1.0, 0.0).astype(BF16)
    rank = jnp.dot(jnp.where(mine, 1.0, 0.0).astype(BF16), before, preferred_element_type=F32)
    code[...] = jnp.where(mine, rank, -1.0)
    local[...] = ((lists & 255) + 1).astype(F32)
    slot_iota = iota((SLOTS, ROWS), 0).astype(F32)
    lane_next = (iota((SLOTS, ROWS), 1) + 1).astype(F32)

    def pack_rows(o, carry):
        hit = code[pl.ds(o, 1), :] == slot_iota
        token = jnp.sum(jnp.where(hit, local[pl.ds(o, 1), :], 0.0), axis=1, keepdims=True)
        at = pl.multiple_of(o * SLOTS, SLOTS)
        pack_m[pl.ds(at, SLOTS), :] = jnp.where(token == lane_next, 1.0, 0.0).astype(BF16)
        return carry

    lax.fori_loop(0, NCTX, pack_rows, 0, unroll=8)

    def merge_table():
        own = jnp.concatenate([bl[pl.ds(2 * me, 1), :], bl[pl.ds(2 * me + 1, 1), :]], axis=1)
        source_row = (own >> 8).astype(F32)
        source_col = jnp.sum(jnp.where(square_r == square_c, source_row, 0.0), axis=1, keepdims=True)
        earlier = (source_row == source_col) & (square_c < square_r)
        slot_col = jnp.sum(jnp.where(earlier, 1.0, 0.0), axis=1, keepdims=True)
        place = source_col * SLOTS + slot_col
        wide = iota((ROWS, NCTX * SLOTS), 1).astype(F32)
        unpack_m[...] = jnp.where(wide == place, 1.0, 0.0).astype(BF16)

    factor = math.log2(math.e) / math.sqrt(HD)
    chunk_rows = PER_CHUNK * ROWS

    def score_own(c, carry):
        keys = jnp.concatenate([kv[0, 0:HD, :], feat[0]], axis=0)
        rows = pl.ds(pl.multiple_of(c * chunk_rows, chunk_rows), chunk_rows)
        part = jnp.dot(qx[rows, :], keys, preferred_element_type=F32) * factor
        allowed = iota((chunk_rows, ROWS), 1) <= (iota((chunk_rows, ROWS), 0) & (ROWS - 1))
        part = jnp.where(allowed, part, -2.0 * FAR)
        scores[c, 0] = part
        tops[c] = jnp.maximum(part[:, 0:HD], part[:, HD:])
        return carry

    lax.fori_loop(0, EARLY, score_own, 0)

    def score(i, carry):
        d = (i + BACK - 1) % BACK + 1
        part = pl.ds(pl.multiple_of(i * (4096 // BACK), 4096 // BACK), 4096 // BACK)
        pltpu.make_async_copy(w_hbm.at[part, :], w.at[part, :], w_sem).start()

        @pl.when(i > 0)
        def _():
            key_copy(0, d, me).wait_recv()

        keys = jnp.concatenate([kv[d, 0:HD, :], feat[d]], axis=0)
        for c in range(EARLY):
            rows = slice(c * chunk_rows, (c + 1) * chunk_rows)
            part = jnp.dot(qx[rows, :], keys, preferred_element_type=F32) * factor
            scores[c, d] = part
            tops[c] = jnp.maximum(tops[c], jnp.maximum(part[:, 0:HD], part[:, HD:]))
        return carry

    pl.semaphore_wait(ready.at[0], 2)
    tell(1)
    lax.fori_loop(0, BACK, score, 0)
    pl.semaphore_wait(ready.at[1], 2)

    def score_late(c):
        score_own(c, 0)
        rows = pl.ds(pl.multiple_of(c * chunk_rows, chunk_rows), chunk_rows)
        top = tops[c]
        for d in range(1, BACK + 1):
            keys = jnp.concatenate([kv[d, 0:HD, :], feat[d]], axis=0)
            part = jnp.dot(qx[rows, :], keys, preferred_element_type=F32) * factor
            scores[c, d] = part
            top = jnp.maximum(top, jnp.maximum(part[:, 0:HD], part[:, HD:]))
        tops[c] = top

    def attend(c):
        ones = jnp.ones((ROWS, HD), BF16)
        vals = []
        for d in range(BACK + 1):
            block = jnp.concatenate([kv[d, HD : 2 * HD, 0:HD], kv[d, HD : 2 * HD, HD : 2 * HD]], axis=0)
            vals.append(jnp.concatenate([block, ones], axis=1))
        vals = jnp.concatenate(vals, axis=0)
        part = []
        for h in range(PER_CHUNK):
            rows = slice(h * ROWS, (h + 1) * ROWS)
            top = jnp.max(tops[c, rows, :], axis=1, keepdims=True)
            weights = [jnp.exp2(scores[c, d, rows, :] - top).astype(BF16) for d in range(BACK + 1)]
            mixed = jnp.dot(jnp.concatenate(weights, axis=1), vals, preferred_element_type=F32)
            part.append((mixed[:, 0:HD] / mixed[:, HD : 2 * HD]).astype(BF16))
        part = jnp.concatenate(part, axis=1)
        rows = jnp.dot(pack_m[...], part, preferred_element_type=F32).astype(BF16)
        packed[c] = rows.reshape(NCTX, SLOTS, WIDTH)
        landed[c, me] = packed[c, me]

        def send(to, inner_carry):
            pltpu.make_async_remote_copy(
                src_ref=packed.at[c, to],
                dst_ref=landed.at[c, me],
                send_sem=a_send.at[c],
                recv_sem=a_recv.at[c],
                device_id=(to, tp),
                device_id_type=MESH,
            ).start()
            return inner_carry

        others(send)

    def give(c, slot, to, sems):
        return pltpu.make_async_remote_copy(
            src_ref=gath.at[c, slot],
            dst_ref=gath.at[c, slot],
            send_sem=sems[0].at[c],
            recv_sem=sems[1].at[c],
            device_id=(me, to),
            device_id_type=MESH,
        )

    far_off, mate_near, mate_far = (z_send, z_recv), (c_send, c_recv), (f_send, f_recv)

    def unpack(c):
        rest = packed.at[c, pl.ds(0, NCTX - 1)]
        pltpu.make_async_copy(rest, rest, a_recv.at[c]).wait()
        rows = jnp.dot(unpack_m[...], landed[c].reshape(NCTX * SLOTS, WIDTH), preferred_element_type=F32)
        gath[c, tp] = rows.astype(BF16)
        give(c, tp, across, far_off).start()
        give(c, tp, mate, mate_near).start()

    def forward(c):
        give(c, across, across, far_off).wait_recv()
        give(c, across, mate, mate_far).start()

    def add_columns(c, slots, target):
        rows = jnp.concatenate([gath[c, t] for t in slots], axis=1)

        def columns(n, carry):
            cols = pl.ds(pl.multiple_of(n * 512, 512), 512)
            part = [w[pl.ds(pl.multiple_of(t * HEADS * HD + c * WIDTH, WIDTH), WIDTH), cols] for t in slots]
            total = jnp.dot(rows, jnp.concatenate(part, axis=0), preferred_element_type=F32) + acc[:, cols]
            target[:, cols] = total.astype(target.dtype)
            return carry

        lax.fori_loop(0, OUT // 512, columns, 0, unroll=4)

    def from_mate(c):
        give(c, mate, mate, mate_near).wait_recv()
        give(c, across_mate, mate, mate_far).wait_recv()

    def project(c):
        from_mate(c)
        add_columns(c, range(4), acc)

    def step(s, carry):
        @pl.when((s >= LAG) & (s < CHUNKS + LAG))
        def _():
            unpack(s - LAG)

        @pl.when((s >= EARLY) & (s < CHUNKS))
        def _():
            score_late(s)

        @pl.when(s < CHUNKS)
        def _():
            attend(s)

        @pl.when(s == 0)
        def _():
            merge_table()
            acc[...] = jnp.zeros((ROWS, OUT), F32)

        @pl.when((s >= LAG + 1) & (s < CHUNKS + LAG + 1))
        def _():
            forward(s - LAG - 1)

        @pl.when(s == LAG + 1)
        def _():
            w_copy.wait()

        @pl.when(s >= LAG + 2)
        def _():
            project(s - LAG - 2)

        return carry

    lax.fori_loop(0, CHUNKS + LAG, step, 0)
    project(CHUNKS - 2)
    forward(CHUNKS - 1)
    add_columns(CHUNKS - 1, (tp, across), acc)
    from_mate(CHUNKS - 1)
    add_columns(CHUNKS - 1, (mate, across_mate), out)

    for d in range(1, BACK + 1):
        key_copy(0, d, me).wait_send()
    for c in range(CHUNKS):
        rest = packed.at[c, pl.ds(0, NCTX - 1)]
        pltpu.make_async_copy(rest, rest, a_send.at[c]).wait()
        give(c, tp, across, far_off).wait_send()
        give(c, tp, mate, mate_near).wait_send()
        give(c, across, mate, mate_far).wait_send()


def on_device(balance_list, doc_ids, raw_queries, raw_keys, values, out_weight):
    inner, outer = rope_tables()
    vmem = pl.BlockSpec(memory_space=pltpu.VMEM)
    dma = pltpu.SemaphoreType.DMA
    return pl.pallas_call(
        kernel,
        out_shape=pltpu.VMEM((ROWS, OUT), BF16),
        in_specs=[pl.BlockSpec(memory_space=pl.ANY)] * 8,
        out_specs=vmem,
        scratch_shapes=[
            pltpu.VMEM((64, 128), jnp.int32),
            pltpu.VMEM((64, 128), jnp.int32),
            pltpu.VMEM((ROWS, HEADS * HD), BF16),
            pltpu.VMEM((ROWS, HD), BF16),
            pltpu.VMEM((ROWS, HD), BF16),
            pltpu.VMEM((2, ROWS, HD), F32),
            pltpu.VMEM((2, NCTX, HD), F32),
            pltpu.VMEM((HEADS * ROWS, 2 * HD), BF16),
            pltpu.VMEM((BACK + 1, ROWS, 2 * HD), BF16),
            pltpu.VMEM((BACK + 1, HD, ROWS), BF16),
            pltpu.VMEM((CHUNKS, BACK + 1, PER_CHUNK * ROWS, ROWS), F32),
            pltpu.VMEM((CHUNKS, PER_CHUNK * ROWS, HD), F32),
            pltpu.VMEM((NCTX, ROWS), F32),
            pltpu.VMEM((NCTX, ROWS), F32),
            pltpu.VMEM((NCTX * SLOTS, ROWS), BF16),
            pltpu.VMEM((ROWS, NCTX * SLOTS), BF16),
            pltpu.VMEM((CHUNKS, NCTX, SLOTS, WIDTH), BF16),
            pltpu.VMEM((CHUNKS, NCTX, SLOTS, WIDTH), BF16),
            pltpu.VMEM((CHUNKS, 4, ROWS, WIDTH), BF16),
            pltpu.VMEM((4096, OUT), BF16),
            pltpu.VMEM((ROWS, OUT), F32),
            dma((BACK,)), dma((BACK,)),
            dma((CHUNKS,)), dma((CHUNKS,)),
            dma((CHUNKS,)), dma((CHUNKS,)),
            dma((CHUNKS,)), dma((CHUNKS,)),
            dma((CHUNKS,)), dma((CHUNKS,)),
            dma,
            dma((7,)),
            pltpu.SemaphoreType.REGULAR((2,)),
        ],
        compiler_params=pltpu.CompilerParams(
            collective_id=0, has_side_effects=True, vmem_limit_bytes=60 * 1024 * 1024
        ),
        cost_estimate=pl.CostEstimate(
            flops=7_000_000_000, bytes_accessed=19_000_000, transcendentals=4_700_000
        ),
    )(
        balance_list.reshape(64, 128), doc_ids.reshape(64, 128), raw_queries, raw_keys, values,
        jnp.asarray(inner), jnp.asarray(outer), out_weight,
    )


def solution(mesh):
    in_specs = (P(), P(), P("ctx", "tp"), P("ctx", "tp"), P("ctx", "tp"), P(None, "tp"))
    out_specs = P("ctx", "tp")
    return jax.shard_map(
        on_device, mesh=mesh, in_specs=in_specs, out_specs=out_specs, check_vma=False
    )
```

```python
import functools
import math

import jax
import jax.numpy as jnp
import numpy as np
from jax import lax
from jax.experimental import pallas as pl
from jax.experimental.pallas import tpu as pltpu
from jax.sharding import PartitionSpec as P

MESH = pl.DeviceIdType.MESH
HD = 128
NCTX = 32
ROWS = 256
HEADS = 8
BACK = 8
SLOTS = 16
CHUNKS = 4
LAG = 3
EARLY = 2
PER_CHUNK = HEADS // CHUNKS
WIDTH = HEADS * HD // CHUNKS
OUT = 2048
FAR = 1048576.0
ROPE_BASE = 500000.0
F32 = jnp.float32
BF16 = jnp.bfloat16


def hops(d):
    return min(d % 4, 4 - d % 4) + min(d // 8, 4 - d // 8) + d // 4 % 2


FAR_FIRST = sorted(range(1, NCTX), key=lambda d: (d // 4 % 2, hops(d)), reverse=True)


def rope_tables():
    freq = ROPE_BASE ** (-(np.arange(HD // 2, dtype=np.float64) * 2.0 / HD))
    freq = np.concatenate([freq, freq])[None, :]
    inner = np.arange(ROWS, dtype=np.float64)[:, None] * freq
    outer = (np.arange(NCTX, dtype=np.float64) * ROWS)[:, None] * freq
    inner = np.stack([np.cos(inner), np.sin(inner)]).astype(np.float32)
    outer = np.stack([np.cos(outer), np.sin(outer)]).astype(np.float32)
    return inner, outer


def iota(shape, dim):
    return lax.broadcasted_iota(jnp.int32, shape, dim)


def kernel(
    bl_h, docs_h, q_h, k_h, v_h, inner_h, outer_h, w_hbm, out,
    bl, docs, q_in, k_in, v_in, inner, outer,
    qx, kv, feat, scores, tops, code, local, pack_m, unpack_m, packed, landed, gath, w, acc,
    kv_send, kv_recv, a_send, a_recv, z_send, z_recv, c_send, c_recv, f_send, f_recv, w_sem, in_sem, ready,
):
    me = lax.axis_index("ctx")
    tp = lax.axis_index("tp")
    hi, core = tp // 2, tp % 2
    mate = hi * 2 + 1 - core
    across = (1 - hi) * 2 + core
    across_mate = (1 - hi) * 2 + 1 - core

    w_copy = pltpu.make_async_copy(w_hbm, w, w_sem)
    pairs = (
        (k_h, k_in), (inner_h, inner), (outer_h, outer), (v_h, v_in), (q_h, q_in), (docs_h, docs), (bl_h, bl)
    )
    loads = [pltpu.make_async_copy(a, b, in_sem.at[n]) for n, (a, b) in enumerate(pairs)]
    for load in loads:
        load.start()

    barrier = pltpu.get_barrier_semaphore()

    def others(body):
        for d in FAR_FIRST:
            body(lax.rem(me + d, NCTX), 0)

    slab, place_in = me // BACK * BACK, me % BACK
    above, below = (me + BACK) % NCTX, (me + NCTX - BACK) % NCTX

    def greet(d, carry):
        to = slab + (place_in + d) % BACK
        pl.semaphore_signal(barrier, inc=1, device_id=(to, tp), device_id_type=MESH)
        return carry

    for who in ((above, tp), (below, tp), (me, mate), (me, across)):
        pl.semaphore_signal(barrier, inc=1, device_id=who, device_id_type=MESH)
    lax.fori_loop(1, BACK, greet, 0)

    def tell(n):
        for to in (above, below):
            pl.semaphore_signal(ready.at[n], inc=1, device_id=(to, tp), device_id_type=MESH)

    for load in loads[:4]:
        load.wait()
    cos_o = outer[0, pl.ds(me, 1), :]
    sin_o = outer[1, pl.ds(me, 1), :]
    cos = cos_o * inner[0] - sin_o * inner[1]
    sin = sin_o * inner[0] + cos_o * inner[1]
    lane = iota((ROWS, HD), 1)
    sin = jnp.where(lane < HD // 2, -sin, sin)

    def rotate(x):
        x = x.astype(F32)
        return (x * cos + pltpu.roll(x, HD // 2, 1) * sin).astype(BF16)

    kv[0, 0:HD, :] = jnp.transpose(rotate(k_in[...]).astype(F32)).astype(BF16)
    kv[0, HD : 2 * HD, 0:HD] = v_in[0:HD, :]
    kv[0, HD : 2 * HD, HD : 2 * HD] = v_in[HD : 2 * HD, :]

    pl.semaphore_wait(barrier, BACK - 1 + 4)

    def key_copy(source, d, to):
        return pltpu.make_async_remote_copy(
            src_ref=kv.at[source],
            dst_ref=kv.at[d],
            send_sem=kv_send.at[d - 1],
            recv_sem=kv_recv.at[d - 1],
            device_id=(to, tp),
            device_id_type=MESH,
        )

    first_slab, last_slab = me < BACK, me >= NCTX - BACK

    @pl.when(jnp.logical_not(last_slab))
    def _():
        key_copy(0, BACK, above).start()

    tell(0)

    def clear(d, carry):
        @pl.when(first_slab & (d > place_in))
        def _():
            kv[d] = jnp.zeros((ROWS, 2 * HD), BF16)

        return carry


    def send_own(d, carry):
        @pl.when(place_in + d < BACK)
        def _():
            key_copy(0, d, me + d).start()

        return carry

    def send_previous(d, carry):
        @pl.when(place_in + d >= BACK)
        def _():
            key_copy(BACK, d, slab + (place_in + d) % BACK).start()

        return carry

    lax.fori_loop(1, BACK, send_own, 0)
    for load in loads[4:]:
        load.wait()

    def doc_row(block):
        row = jnp.concatenate([docs[pl.ds(2 * block, 1), :], docs[pl.ds(2 * block + 1, 1), :]], axis=1)
        return jnp.broadcast_to(row, (HD, ROWS))

    far = jnp.where(jnp.transpose(doc_row(me).astype(F32)) == lane.astype(F32), 0.0, -FAR).astype(BF16)

    def queries(h, carry):
        rows = pl.ds(pl.multiple_of(h * ROWS, ROWS), ROWS)
        qx[rows, 0:HD] = rotate(q_in[:, pl.ds(pl.multiple_of(h * HD, HD), HD)])
        qx[rows, HD : 2 * HD] = far
        return carry

    def pass_on():
        key_copy(0, BACK, me).wait_recv()
        lax.fori_loop(1, BACK, send_previous, 0)

    pl.when(jnp.logical_not(first_slab))(pass_on)
    lax.fori_loop(1, BACK + 1, clear, 0)
    lax.fori_loop(0, HEADS, queries, 0)

    doc_iota = iota((HD, ROWS), 0)

    def features(d, carry):
        feat[d] = jnp.where(doc_row((me - d + NCTX) % NCTX) == doc_iota, 1.0, 0.0).astype(BF16)
        return carry

    lax.fori_loop(0, BACK + 1, features, 0)

    square_r, square_c = iota((ROWS, ROWS), 0), iota((ROWS, ROWS), 1)
    lists = jnp.concatenate(
        [bl[pl.ds(0, NCTX, stride=2), :], bl[pl.ds(1, NCTX, stride=2), :]], axis=1
    )
    mine = (lists >> 8) == me
    before = jnp.where(square_r < square_c, 1.0, 0.0).astype(BF16)
    rank = jnp.dot(jnp.where(mine, 1.0, 0.0).astype(BF16), before, preferred_element_type=F32)
    code[...] = jnp.where(mine, rank, -1.0)
    local[...] = ((lists & 255) + 1).astype(F32)
    slot_iota = iota((SLOTS, ROWS), 0).astype(F32)
    lane_next = (iota((SLOTS, ROWS), 1) + 1).astype(F32)

    def pack_rows(o, carry):
        hit = code[pl.ds(o, 1), :] == slot_iota
        token = jnp.sum(jnp.where(hit, local[pl.ds(o, 1), :], 0.0), axis=1, keepdims=True)
        at = pl.multiple_of(o * SLOTS, SLOTS)
        pack_m[pl.ds(at, SLOTS), :] = jnp.where(token == lane_next, 1.0, 0.0).astype(BF16)
        return carry

    lax.fori_loop(0, NCTX, pack_rows, 0, unroll=8)

    def merge_table():
        own = jnp.concatenate([bl[pl.ds(2 * me, 1), :], bl[pl.ds(2 * me + 1, 1), :]], axis=1)
        source_row = (own >> 8).astype(F32)
        source_col = jnp.sum(jnp.where(square_r == square_c, source_row, 0.0), axis=1, keepdims=True)
        earlier = (source_row == source_col) & (square_c < square_r)
        slot_col = jnp.sum(jnp.where(earlier, 1.0, 0.0), axis=1, keepdims=True)
        place = source_col * SLOTS + slot_col
        wide = iota((ROWS, NCTX * SLOTS), 1).astype(F32)
        unpack_m[...] = jnp.where(wide == place, 1.0, 0.0).astype(BF16)

    factor = math.log2(math.e) / math.sqrt(HD)
    chunk_rows = PER_CHUNK * ROWS

    def score_own(c, carry):
        keys = jnp.concatenate([kv[0, 0:HD, :], feat[0]], axis=0)
        rows = pl.ds(pl.multiple_of(c * chunk_rows, chunk_rows), chunk_rows)
        part = jnp.dot(qx[rows, :], keys, preferred_element_type=F32) * factor
        allowed = iota((chunk_rows, ROWS), 1) <= (iota((chunk_rows, ROWS), 0) & (ROWS - 1))
        part = jnp.where(allowed, part, -2.0 * FAR)
        scores[c, 0] = part
        tops[c] = jnp.maximum(part[:, 0:HD], part[:, HD:])
        return carry

    lax.fori_loop(0, EARLY, score_own, 0)

    def score(i, carry):
        d = (i + BACK - 1) % BACK + 1
        part = pl.ds(pl.multiple_of(i * (4096 // BACK), 4096 // BACK), 4096 // BACK)
        pltpu.make_async_copy(w_hbm.at[part, :], w.at[part, :], w_sem).start()

        @pl.when((i > 0) & (jnp.logical_not(first_slab) | (d <= place_in)))
        def _():
            key_copy(0, d, me).wait_recv()

        keys = jnp.concatenate([kv[d, 0:HD, :], feat[d]], axis=0)
        for c in range(EARLY):
            rows = slice(c * chunk_rows, (c + 1) * chunk_rows)
            part = jnp.dot(qx[rows, :], keys, preferred_element_type=F32) * factor
            scores[c, d] = part
            tops[c] = jnp.maximum(tops[c], jnp.maximum(part[:, 0:HD], part[:, HD:]))
        return carry

    pl.semaphore_wait(ready.at[0], 2)
    tell(1)
    lax.fori_loop(0, BACK, score, 0)
    pl.semaphore_wait(ready.at[1], 2)

    def score_late(c):
        score_own(c, 0)
        rows = pl.ds(pl.multiple_of(c * chunk_rows, chunk_rows), chunk_rows)
        top = tops[c]
        for d in range(1, BACK + 1):
            keys = jnp.concatenate([kv[d, 0:HD, :], feat[d]], axis=0)
            part = jnp.dot(qx[rows, :], keys, preferred_element_type=F32) * factor
            scores[c, d] = part
            top = jnp.maximum(top, jnp.maximum(part[:, 0:HD], part[:, HD:]))
        tops[c] = top

    def attend(c):
        ones = jnp.ones((ROWS, HD), BF16)
        vals = []
        for d in range(BACK + 1):
            block = jnp.concatenate([kv[d, HD : 2 * HD, 0:HD], kv[d, HD : 2 * HD, HD : 2 * HD]], axis=0)
            vals.append(jnp.concatenate([block, ones], axis=1))
        vals = jnp.concatenate(vals, axis=0)
        part = []
        for h in range(PER_CHUNK):
            rows = slice(h * ROWS, (h + 1) * ROWS)
            top = jnp.max(tops[c, rows, :], axis=1, keepdims=True)
            weights = [jnp.exp2(scores[c, d, rows, :] - top).astype(BF16) for d in range(BACK + 1)]
            mixed = jnp.dot(jnp.concatenate(weights, axis=1), vals, preferred_element_type=F32)
            part.append((mixed[:, 0:HD] / mixed[:, HD : 2 * HD]).astype(BF16))
        part = jnp.concatenate(part, axis=1)
        rows = jnp.dot(pack_m[...], part, preferred_element_type=F32).astype(BF16)
        packed[c] = rows.reshape(NCTX, SLOTS, WIDTH)
        landed[c, me] = packed[c, me]

        def send(to, inner_carry):
            pltpu.make_async_remote_copy(
                src_ref=packed.at[c, to],
                dst_ref=landed.at[c, me],
                send_sem=a_send.at[c],
                recv_sem=a_recv.at[c],
                device_id=(to, tp),
                device_id_type=MESH,
            ).start()
            return inner_carry

        others(send)

    def give(c, slot, to, sems):
        return pltpu.make_async_remote_copy(
            src_ref=gath.at[c, slot],
            dst_ref=gath.at[c, slot],
            send_sem=sems[0].at[c],
            recv_sem=sems[1].at[c],
            device_id=(me, to),
            device_id_type=MESH,
        )

    far_off, mate_near, mate_far = (z_send, z_recv), (c_send, c_recv), (f_send, f_recv)

    def unpack(c):
        rest = packed.at[c, pl.ds(0, NCTX - 1)]
        pltpu.make_async_copy(rest, rest, a_recv.at[c]).wait()
        rows = jnp.dot(unpack_m[...], landed[c].reshape(NCTX * SLOTS, WIDTH), preferred_element_type=F32)
        gath[c, tp] = rows.astype(BF16)
        give(c, tp, across, far_off).start()
        give(c, tp, mate, mate_near).start()

    def forward(c):
        give(c, across, across, far_off).wait_recv()
        give(c, across, mate, mate_far).start()

    def add_columns(c, slots, target):
        rows = jnp.concatenate([gath[c, t] for t in slots], axis=1)

        def columns(n, carry):
            cols = pl.ds(pl.multiple_of(n * 512, 512), 512)
            part = [w[pl.ds(pl.multiple_of(t * HEADS * HD + c * WIDTH, WIDTH), WIDTH), cols] for t in slots]
            total = jnp.dot(rows, jnp.concatenate(part, axis=0), preferred_element_type=F32) + acc[:, cols]
            target[:, cols] = total.astype(target.dtype)
            return carry

        lax.fori_loop(0, OUT // 512, columns, 0, unroll=4)

    def from_mate(c):
        give(c, mate, mate, mate_near).wait_recv()
        give(c, across_mate, mate, mate_far).wait_recv()

    def project(c):
        from_mate(c)
        add_columns(c, range(4), acc)

    def step(s, carry):
        @pl.when((s >= LAG) & (s < CHUNKS + LAG))
        def _():
            unpack(s - LAG)

        @pl.when((s >= EARLY) & (s < CHUNKS))
        def _():
            score_late(s)

        @pl.when(s < CHUNKS)
        def _():
            attend(s)

        @pl.when(s == 0)
        def _():
            merge_table()
            acc[...] = jnp.zeros((ROWS, OUT), F32)

        @pl.when((s >= LAG + 1) & (s < CHUNKS + LAG + 1))
        def _():
            forward(s - LAG - 1)

        @pl.when(s == LAG + 1)
        def _():
            w_copy.wait()

        @pl.when(s >= LAG + 2)
        def _():
            project(s - LAG - 2)

        return carry

    lax.fori_loop(0, CHUNKS + LAG, step, 0)
    project(CHUNKS - 2)
    forward(CHUNKS - 1)
    add_columns(CHUNKS - 1, (tp, across), acc)
    from_mate(CHUNKS - 1)
    add_columns(CHUNKS - 1, (mate, across_mate), out)

    def sent(d, carry):
        @pl.when((place_in + d < BACK) | jnp.logical_not(first_slab))
        def _():
            key_copy(0, d, me).wait_send()

        return carry

    lax.fori_loop(1, BACK, sent, 0)

    @pl.when(jnp.logical_not(last_slab))
    def _():
        key_copy(0, BACK, me).wait_send()

    for c in range(CHUNKS):
        rest = packed.at[c, pl.ds(0, NCTX - 1)]
        pltpu.make_async_copy(rest, rest, a_send.at[c]).wait()
        give(c, tp, across, far_off).wait_send()
        give(c, tp, mate, mate_near).wait_send()
        give(c, across, mate, mate_far).wait_send()


def on_device(balance_list, doc_ids, raw_queries, raw_keys, values, out_weight):
    inner, outer = rope_tables()
    vmem = pl.BlockSpec(memory_space=pltpu.VMEM)
    dma = pltpu.SemaphoreType.DMA
    return pl.pallas_call(
        kernel,
        out_shape=pltpu.VMEM((ROWS, OUT), BF16),
        in_specs=[pl.BlockSpec(memory_space=pl.ANY)] * 8,
        out_specs=vmem,
        scratch_shapes=[
            pltpu.VMEM((64, 128), jnp.int32),
            pltpu.VMEM((64, 128), jnp.int32),
            pltpu.VMEM((ROWS, HEADS * HD), BF16),
            pltpu.VMEM((ROWS, HD), BF16),
            pltpu.VMEM((ROWS, HD), BF16),
            pltpu.VMEM((2, ROWS, HD), F32),
            pltpu.VMEM((2, NCTX, HD), F32),
            pltpu.VMEM((HEADS * ROWS, 2 * HD), BF16),
            pltpu.VMEM((BACK + 1, ROWS, 2 * HD), BF16),
            pltpu.VMEM((BACK + 1, HD, ROWS), BF16),
            pltpu.VMEM((CHUNKS, BACK + 1, PER_CHUNK * ROWS, ROWS), F32),
            pltpu.VMEM((CHUNKS, PER_CHUNK * ROWS, HD), F32),
            pltpu.VMEM((NCTX, ROWS), F32),
            pltpu.VMEM((NCTX, ROWS), F32),
            pltpu.VMEM((NCTX * SLOTS, ROWS), BF16),
            pltpu.VMEM((ROWS, NCTX * SLOTS), BF16),
            pltpu.VMEM((CHUNKS, NCTX, SLOTS, WIDTH), BF16),
            pltpu.VMEM((CHUNKS, NCTX, SLOTS, WIDTH), BF16),
            pltpu.VMEM((CHUNKS, 4, ROWS, WIDTH), BF16),
            pltpu.VMEM((4096, OUT), BF16),
            pltpu.VMEM((ROWS, OUT), F32),
            dma((BACK,)), dma((BACK,)),
            dma((CHUNKS,)), dma((CHUNKS,)),
            dma((CHUNKS,)), dma((CHUNKS,)),
            dma((CHUNKS,)), dma((CHUNKS,)),
            dma((CHUNKS,)), dma((CHUNKS,)),
            dma,
            dma((7,)),
            pltpu.SemaphoreType.REGULAR((2,)),
        ],
        compiler_params=pltpu.CompilerParams(
            collective_id=0, has_side_effects=True, vmem_limit_bytes=60 * 1024 * 1024
        ),
        cost_estimate=pl.CostEstimate(
            flops=7_000_000_000, bytes_accessed=19_000_000, transcendentals=4_700_000
        ),
    )(
        balance_list.reshape(64, 128), doc_ids.reshape(64, 128), raw_queries, raw_keys, values,
        jnp.asarray(inner), jnp.asarray(outer), out_weight,
    )


def solution(mesh):
    in_specs = (P(), P(), P("ctx", "tp"), P("ctx", "tp"), P("ctx", "tp"), P(None, "tp"))
    out_specs = P("ctx", "tp")
    return jax.shard_map(
        on_device, mesh=mesh, in_specs=in_specs, out_specs=out_specs, check_vma=False
    )
```

```python
import functools
import math

import jax
import jax.numpy as jnp
import numpy as np
from jax import lax
from jax.experimental import pallas as pl
from jax.experimental.pallas import tpu as pltpu
from jax.sharding import PartitionSpec as P

MESH = pl.DeviceIdType.MESH
HD = 128
NCTX = 32
ROWS = 256
HEADS = 8
BACK = 8
SLOTS = 16
CHUNKS = 4
LAG = 3
EARLY = 3
PER_CHUNK = HEADS // CHUNKS
WIDTH = HEADS * HD // CHUNKS
OUT = 2048
FAR = 1048576.0
ROPE_BASE = 500000.0
F32 = jnp.float32
BF16 = jnp.bfloat16


def hops(d):
    return min(d % 4, 4 - d % 4) + min(d // 8, 4 - d // 8) + d // 4 % 2


FAR_FIRST = sorted(range(1, NCTX), key=lambda d: (d // 4 % 2, hops(d)), reverse=True)


def rope_tables():
    freq = ROPE_BASE ** (-(np.arange(HD // 2, dtype=np.float64) * 2.0 / HD))
    freq = np.concatenate([freq, freq])[None, :]
    inner = np.arange(ROWS, dtype=np.float64)[:, None] * freq
    outer = (np.arange(NCTX, dtype=np.float64) * ROWS)[:, None] * freq
    inner = np.stack([np.cos(inner), np.sin(inner)]).astype(np.float32)
    outer = np.stack([np.cos(outer), np.sin(outer)]).astype(np.float32)
    return inner, outer


def iota(shape, dim):
    return lax.broadcasted_iota(jnp.int32, shape, dim)


def kernel(
    bl_h, docs_h, q_h, k_h, v_h, inner_h, outer_h, w_hbm, out,
    bl, docs, q_in, k_in, v_in, inner, outer,
    qx, kv, feat, scores, tops, code, local, pack_m, unpack_m, packed, landed, gath, w, acc,
    kv_send, kv_recv, a_send, a_recv, z_send, z_recv, c_send, c_recv, f_send, f_recv, w_sem, in_sem, ready,
):
    me = lax.axis_index("ctx")
    tp = lax.axis_index("tp")
    hi, core = tp // 2, tp % 2
    mate = hi * 2 + 1 - core
    across = (1 - hi) * 2 + core
    across_mate = (1 - hi) * 2 + 1 - core

    w_copy = pltpu.make_async_copy(w_hbm, w, w_sem)
    pairs = (
        (k_h, k_in), (inner_h, inner), (outer_h, outer), (v_h, v_in), (q_h, q_in), (docs_h, docs), (bl_h, bl)
    )
    loads = [pltpu.make_async_copy(a, b, in_sem.at[n]) for n, (a, b) in enumerate(pairs)]
    for load in loads:
        load.start()

    barrier = pltpu.get_barrier_semaphore()

    def others(body):
        for d in FAR_FIRST:
            body(lax.rem(me + d, NCTX), 0)

    slab, place_in = me // BACK * BACK, me % BACK
    above, below = (me + BACK) % NCTX, (me + NCTX - BACK) % NCTX

    def greet(d, carry):
        to = slab + (place_in + d) % BACK
        pl.semaphore_signal(barrier, inc=1, device_id=(to, tp), device_id_type=MESH)
        return carry

    for who in ((above, tp), (below, tp), (me, mate), (me, across)):
        pl.semaphore_signal(barrier, inc=1, device_id=who, device_id_type=MESH)
    lax.fori_loop(1, BACK, greet, 0)

    def tell(n):
        for to in (above, below):
            pl.semaphore_signal(ready.at[n], inc=1, device_id=(to, tp), device_id_type=MESH)

    for load in loads[:4]:
        load.wait()
    cos_o = outer[0, pl.ds(me, 1), :]
    sin_o = outer[1, pl.ds(me, 1), :]
    cos = cos_o * inner[0] - sin_o * inner[1]
    sin = sin_o * inner[0] + cos_o * inner[1]
    lane = iota((ROWS, HD), 1)
    sin = jnp.where(lane < HD // 2, -sin, sin)

    def rotate(x):
        x = x.astype(F32)
        return (x * cos + pltpu.roll(x, HD // 2, 1) * sin).astype(BF16)

    kv[0, 0:HD, :] = jnp.transpose(rotate(k_in[...]).astype(F32)).astype(BF16)
    kv[0, HD : 2 * HD, 0:HD] = v_in[0:HD, :]
    kv[0, HD : 2 * HD, HD : 2 * HD] = v_in[HD : 2 * HD, :]

    pl.semaphore_wait(barrier, BACK - 1 + 4)

    def key_copy(source, d, to):
        return pltpu.make_async_remote_copy(
            src_ref=kv.at[source],
            dst_ref=kv.at[d],
            send_sem=kv_send.at[d - 1],
            recv_sem=kv_recv.at[d - 1],
            device_id=(to, tp),
            device_id_type=MESH,
        )

    first_slab, last_slab = me < BACK, me >= NCTX - BACK

    @pl.when(jnp.logical_not(last_slab))
    def _():
        key_copy(0, BACK, above).start()

    tell(0)

    def clear(d, carry):
        @pl.when(first_slab & (d > place_in))
        def _():
            kv[d] = jnp.zeros((ROWS, 2 * HD), BF16)

        return carry


    def send_own(d, carry):
        @pl.when(place_in + d < BACK)
        def _():
            key_copy(0, d, me + d).start()

        return carry

    def send_previous(d, carry):
        @pl.when(place_in + d >= BACK)
        def _():
            key_copy(BACK, d, slab + (place_in + d) % BACK).start()

        return carry

    lax.fori_loop(1, BACK, send_own, 0)
    for load in loads[4:]:
        load.wait()

    def doc_row(block):
        row = jnp.concatenate([docs[pl.ds(2 * block, 1), :], docs[pl.ds(2 * block + 1, 1), :]], axis=1)
        return jnp.broadcast_to(row, (HD, ROWS))

    far = jnp.where(jnp.transpose(doc_row(me).astype(F32)) == lane.astype(F32), 0.0, -FAR).astype(BF16)

    def queries(h, carry):
        rows = pl.ds(pl.multiple_of(h * ROWS, ROWS), ROWS)
        qx[rows, 0:HD] = rotate(q_in[:, pl.ds(pl.multiple_of(h * HD, HD), HD)])
        qx[rows, HD : 2 * HD] = far
        return carry

    def pass_on():
        key_copy(0, BACK, me).wait_recv()
        lax.fori_loop(1, BACK, send_previous, 0)

    pl.when(jnp.logical_not(first_slab))(pass_on)
    lax.fori_loop(1, BACK + 1, clear, 0)
    lax.fori_loop(0, HEADS, queries, 0)

    doc_iota = iota((HD, ROWS), 0)

    def features(d, carry):
        feat[d] = jnp.where(doc_row((me - d + NCTX) % NCTX) == doc_iota, 1.0, 0.0).astype(BF16)
        return carry

    lax.fori_loop(0, BACK + 1, features, 0)

    square_r, square_c = iota((ROWS, ROWS), 0), iota((ROWS, ROWS), 1)
    lists = jnp.concatenate(
        [bl[pl.ds(0, NCTX, stride=2), :], bl[pl.ds(1, NCTX, stride=2), :]], axis=1
    )
    mine = (lists >> 8) == me
    before = jnp.where(square_r < square_c, 1.0, 0.0).astype(BF16)
    rank = jnp.dot(jnp.where(mine, 1.0, 0.0).astype(BF16), before, preferred_element_type=F32)
    code[...] = jnp.where(mine, rank, -1.0)
    local[...] = ((lists & 255) + 1).astype(F32)
    slot_iota = iota((SLOTS, ROWS), 0).astype(F32)
    lane_next = (iota((SLOTS, ROWS), 1) + 1).astype(F32)

    def pack_rows(o, carry):
        hit = code[pl.ds(o, 1), :] == slot_iota
        token = jnp.sum(jnp.where(hit, local[pl.ds(o, 1), :], 0.0), axis=1, keepdims=True)
        at = pl.multiple_of(o * SLOTS, SLOTS)
        pack_m[pl.ds(at, SLOTS), :] = jnp.where(token == lane_next, 1.0, 0.0).astype(BF16)
        return carry

    lax.fori_loop(0, NCTX, pack_rows, 0, unroll=8)

    def merge_table():
        own = jnp.concatenate([bl[pl.ds(2 * me, 1), :], bl[pl.ds(2 * me + 1, 1), :]], axis=1)
        source_row = (own >> 8).astype(F32)
        source_col = jnp.sum(jnp.where(square_r == square_c, source_row, 0.0), axis=1, keepdims=True)
        earlier = (source_row == source_col) & (square_c < square_r)
        slot_col = jnp.sum(jnp.where(earlier, 1.0, 0.0), axis=1, keepdims=True)
        place = source_col * SLOTS + slot_col
        wide = iota((ROWS, NCTX * SLOTS), 1).astype(F32)
        unpack_m[...] = jnp.where(wide == place, 1.0, 0.0).astype(BF16)

    factor = math.log2(math.e) / math.sqrt(HD)
    chunk_rows = PER_CHUNK * ROWS

    def score_own(c, carry):
        keys = jnp.concatenate([kv[0, 0:HD, :], feat[0]], axis=0)
        rows = pl.ds(pl.multiple_of(c * chunk_rows, chunk_rows), chunk_rows)
        part = jnp.dot(qx[rows, :], keys, preferred_element_type=F32) * factor
        allowed = iota((chunk_rows, ROWS), 1) <= (iota((chunk_rows, ROWS), 0) & (ROWS - 1))
        part = jnp.where(allowed, part, -2.0 * FAR)
        scores[c, 0] = part
        tops[c] = jnp.maximum(part[:, 0:HD], part[:, HD:])
        return carry

    lax.fori_loop(0, EARLY, score_own, 0)

    def score(i, carry):
        d = (i + BACK - 1) % BACK + 1
        part = pl.ds(pl.multiple_of(i * (4096 // BACK), 4096 // BACK), 4096 // BACK)
        pltpu.make_async_copy(w_hbm.at[part, :], w.at[part, :], w_sem).start()

        @pl.when((i > 0) & (jnp.logical_not(first_slab) | (d <= place_in)))
        def _():
            key_copy(0, d, me).wait_recv()

        keys = jnp.concatenate([kv[d, 0:HD, :], feat[d]], axis=0)
        for c in range(EARLY):
            rows = slice(c * chunk_rows, (c + 1) * chunk_rows)
            part = jnp.dot(qx[rows, :], keys, preferred_element_type=F32) * factor
            scores[c, d] = part
            tops[c] = jnp.maximum(tops[c], jnp.maximum(part[:, 0:HD], part[:, HD:]))
        return carry

    pl.semaphore_wait(ready.at[0], 2)
    tell(1)
    lax.fori_loop(0, BACK, score, 0)
    pl.semaphore_wait(ready.at[1], 2)

    def score_late(c):
        score_own(c, 0)
        rows = pl.ds(pl.multiple_of(c * chunk_rows, chunk_rows), chunk_rows)
        top = tops[c]
        for d in range(1, BACK + 1):
            keys = jnp.concatenate([kv[d, 0:HD, :], feat[d]], axis=0)
            part = jnp.dot(qx[rows, :], keys, preferred_element_type=F32) * factor
            scores[c, d] = part
            top = jnp.maximum(top, jnp.maximum(part[:, 0:HD], part[:, HD:]))
        tops[c] = top

    def attend(c):
        ones = jnp.ones((ROWS, HD), BF16)
        vals = []
        for d in range(BACK + 1):
            block = jnp.concatenate([kv[d, HD : 2 * HD, 0:HD], kv[d, HD : 2 * HD, HD : 2 * HD]], axis=0)
            vals.append(jnp.concatenate([block, ones], axis=1))
        vals = jnp.concatenate(vals, axis=0)
        part = []
        for h in range(PER_CHUNK):
            rows = slice(h * ROWS, (h + 1) * ROWS)
            top = jnp.max(tops[c, rows, :], axis=1, keepdims=True)
            weights = [jnp.exp2(scores[c, d, rows, :] - top).astype(BF16) for d in range(BACK + 1)]
            mixed = jnp.dot(jnp.concatenate(weights, axis=1), vals, preferred_element_type=F32)
            part.append((mixed[:, 0:HD] / mixed[:, HD : 2 * HD]).astype(BF16))
        part = jnp.concatenate(part, axis=1)
        rows = jnp.dot(pack_m[...], part, preferred_element_type=F32).astype(BF16)
        packed[c] = rows.reshape(NCTX, SLOTS, WIDTH)
        landed[c, me] = packed[c, me]

        def send(to, inner_carry):
            pltpu.make_async_remote_copy(
                src_ref=packed.at[c, to],
                dst_ref=landed.at[c, me],
                send_sem=a_send.at[c],
                recv_sem=a_recv.at[c],
                device_id=(to, tp),
                device_id_type=MESH,
            ).start()
            return inner_carry

        others(send)

    def give(c, slot, to, sems):
        return pltpu.make_async_remote_copy(
            src_ref=gath.at[c, slot],
            dst_ref=gath.at[c, slot],
            send_sem=sems[0].at[c],
            recv_sem=sems[1].at[c],
            device_id=(me, to),
            device_id_type=MESH,
        )

    far_off, mate_near, mate_far = (z_send, z_recv), (c_send, c_recv), (f_send, f_recv)

    def unpack(c):
        rest = packed.at[c, pl.ds(0, NCTX - 1)]
        pltpu.make_async_copy(rest, rest, a_recv.at[c]).wait()
        rows = jnp.dot(unpack_m[...], landed[c].reshape(NCTX * SLOTS, WIDTH), preferred_element_type=F32)
        gath[c, tp] = rows.astype(BF16)
        give(c, tp, across, far_off).start()
        give(c, tp, mate, mate_near).start()

    def forward(c):
        give(c, across, across, far_off).wait_recv()
        give(c, across, mate, mate_far).start()

    def add_columns(c, slots, target):
        rows = jnp.concatenate([gath[c, t] for t in slots], axis=1)

        def columns(n, carry):
            cols = pl.ds(pl.multiple_of(n * 512, 512), 512)
            part = [w[pl.ds(pl.multiple_of(t * HEADS * HD + c * WIDTH, WIDTH), WIDTH), cols] for t in slots]
            total = jnp.dot(rows, jnp.concatenate(part, axis=0), preferred_element_type=F32) + acc[:, cols]
            target[:, cols] = total.astype(target.dtype)
            return carry

        lax.fori_loop(0, OUT // 512, columns, 0, unroll=4)

    def from_mate(c):
        give(c, mate, mate, mate_near).wait_recv()

    def from_far(c):
        give(c, across_mate, mate, mate_far).wait_recv()

    def project(c):
        from_mate(c)
        from_far(c)
        add_columns(c, range(4), acc)

    def step(s, carry):
        @pl.when((s >= LAG) & (s < CHUNKS + LAG))
        def _():
            unpack(s - LAG)

        @pl.when((s >= EARLY) & (s < CHUNKS))
        def _():
            score_late(s)

        @pl.when(s < CHUNKS)
        def _():
            attend(s)

        @pl.when(s == 0)
        def _():
            merge_table()
            acc[...] = jnp.zeros((ROWS, OUT), F32)

        @pl.when((s >= LAG + 1) & (s < CHUNKS + LAG + 1))
        def _():
            forward(s - LAG - 1)

        @pl.when(s == LAG + 1)
        def _():
            w_copy.wait()

        @pl.when(s >= LAG + 2)
        def _():
            project(s - LAG - 2)

        return carry

    lax.fori_loop(0, CHUNKS + LAG, step, 0)
    project(CHUNKS - 2)
    from_mate(CHUNKS - 1)
    add_columns(CHUNKS - 1, (tp, mate), acc)
    forward(CHUNKS - 1)
    add_columns(CHUNKS - 1, (across,), acc)
    from_far(CHUNKS - 1)
    add_columns(CHUNKS - 1, (across_mate,), out)

    def sent(d, carry):
        @pl.when((place_in + d < BACK) | jnp.logical_not(first_slab))
        def _():
            key_copy(0, d, me).wait_send()

        return carry

    lax.fori_loop(1, BACK, sent, 0)

    @pl.when(jnp.logical_not(last_slab))
    def _():
        key_copy(0, BACK, me).wait_send()

    for c in range(CHUNKS):
        rest = packed.at[c, pl.ds(0, NCTX - 1)]
        pltpu.make_async_copy(rest, rest, a_send.at[c]).wait()
        give(c, tp, across, far_off).wait_send()
        give(c, tp, mate, mate_near).wait_send()
        give(c, across, mate, mate_far).wait_send()


def on_device(balance_list, doc_ids, raw_queries, raw_keys, values, out_weight):
    inner, outer = rope_tables()
    vmem = pl.BlockSpec(memory_space=pltpu.VMEM)
    dma = pltpu.SemaphoreType.DMA
    return pl.pallas_call(
        kernel,
        out_shape=pltpu.VMEM((ROWS, OUT), BF16),
        in_specs=[pl.BlockSpec(memory_space=pl.ANY)] * 8,
        out_specs=vmem,
        scratch_shapes=[
            pltpu.VMEM((64, 128), jnp.int32),
            pltpu.VMEM((64, 128), jnp.int32),
            pltpu.VMEM((ROWS, HEADS * HD), BF16),
            pltpu.VMEM((ROWS, HD), BF16),
            pltpu.VMEM((ROWS, HD), BF16),
            pltpu.VMEM((2, ROWS, HD), F32),
            pltpu.VMEM((2, NCTX, HD), F32),
            pltpu.VMEM((HEADS * ROWS, 2 * HD), BF16),
            pltpu.VMEM((BACK + 1, ROWS, 2 * HD), BF16),
            pltpu.VMEM((BACK + 1, HD, ROWS), BF16),
            pltpu.VMEM((CHUNKS, BACK + 1, PER_CHUNK * ROWS, ROWS), F32),
            pltpu.VMEM((CHUNKS, PER_CHUNK * ROWS, HD), F32),
            pltpu.VMEM((NCTX, ROWS), F32),
            pltpu.VMEM((NCTX, ROWS), F32),
            pltpu.VMEM((NCTX * SLOTS, ROWS), BF16),
            pltpu.VMEM((ROWS, NCTX * SLOTS), BF16),
            pltpu.VMEM((CHUNKS, NCTX, SLOTS, WIDTH), BF16),
            pltpu.VMEM((CHUNKS, NCTX, SLOTS, WIDTH), BF16),
            pltpu.VMEM((CHUNKS, 4, ROWS, WIDTH), BF16),
            pltpu.VMEM((4096, OUT), BF16),
            pltpu.VMEM((ROWS, OUT), F32),
            dma((BACK,)), dma((BACK,)),
            dma((CHUNKS,)), dma((CHUNKS,)),
            dma((CHUNKS,)), dma((CHUNKS,)),
            dma((CHUNKS,)), dma((CHUNKS,)),
            dma((CHUNKS,)), dma((CHUNKS,)),
            dma,
            dma((7,)),
            pltpu.SemaphoreType.REGULAR((2,)),
        ],
        compiler_params=pltpu.CompilerParams(
            collective_id=0, has_side_effects=True, vmem_limit_bytes=60 * 1024 * 1024
        ),
        cost_estimate=pl.CostEstimate(
            flops=7_000_000_000, bytes_accessed=19_000_000, transcendentals=4_700_000
        ),
    )(
        balance_list.reshape(64, 128), doc_ids.reshape(64, 128), raw_queries, raw_keys, values,
        jnp.asarray(inner), jnp.asarray(outer), out_weight,
    )


def solution(mesh):
    in_specs = (P(), P(), P("ctx", "tp"), P("ctx", "tp"), P("ctx", "tp"), P(None, "tp"))
    out_specs = P("ctx", "tp")
    return jax.shard_map(
        on_device, mesh=mesh, in_specs=in_specs, out_specs=out_specs, check_vma=False
    )
```

```python
import functools
import math

import jax
import jax.numpy as jnp
import numpy as np
from jax import lax
from jax.experimental import pallas as pl
from jax.experimental.pallas import tpu as pltpu
from jax.sharding import PartitionSpec as P

MESH = pl.DeviceIdType.MESH
HD = 128
NCTX = 32
ROWS = 256
HEADS = 8
BACK = 8
SLOTS = 16
CHUNKS = 4
LAG = 3
EARLY = 1
PER_CHUNK = HEADS // CHUNKS
WIDTH = HEADS * HD // CHUNKS
OUT = 2048
FAR = 1048576.0
ROPE_BASE = 500000.0
F32 = jnp.float32
BF16 = jnp.bfloat16


def hops(d):
    return min(d % 4, 4 - d % 4) + min(d // 8, 4 - d // 8) + d // 4 % 2


FAR_FIRST = sorted(range(1, NCTX), key=lambda d: (d // 4 % 2, hops(d)), reverse=True)


def rope_tables():
    freq = ROPE_BASE ** (-(np.arange(HD // 2, dtype=np.float64) * 2.0 / HD))
    freq = np.concatenate([freq, freq])[None, :]
    inner = np.arange(ROWS, dtype=np.float64)[:, None] * freq
    outer = (np.arange(NCTX, dtype=np.float64) * ROWS)[:, None] * freq
    inner = np.stack([np.cos(inner), np.sin(inner)]).astype(np.float32)
    outer = np.stack([np.cos(outer), np.sin(outer)]).astype(np.float32)
    return inner, outer


def iota(shape, dim):
    return lax.broadcasted_iota(jnp.int32, shape, dim)


def kernel(
    bl_h, docs_h, q_h, k_h, v_h, inner_h, outer_h, w_hbm, out,
    bl, docs, q_in, k_in, v_in, inner, outer,
    qx, kv, feat, scores, tops, code, local, pack_m, unpack_m, packed, landed, gath, w, acc,
    kv_send, kv_recv, a_send, a_recv, z_send, z_recv, c_send, c_recv, f_send, f_recv, w_sem, in_sem, ready,
):
    me = lax.axis_index("ctx")
    tp = lax.axis_index("tp")
    hi, core = tp // 2, tp % 2
    mate = hi * 2 + 1 - core
    across = (1 - hi) * 2 + core
    across_mate = (1 - hi) * 2 + 1 - core

    w_copy = pltpu.make_async_copy(w_hbm, w, w_sem)
    pairs = (
        (k_h, k_in), (inner_h, inner), (outer_h, outer), (v_h, v_in), (q_h, q_in), (docs_h, docs), (bl_h, bl)
    )
    loads = [pltpu.make_async_copy(a, b, in_sem.at[n]) for n, (a, b) in enumerate(pairs)]
    for load in loads:
        load.start()

    barrier = pltpu.get_barrier_semaphore()

    def others(body):
        for d in FAR_FIRST:
            body(lax.rem(me + d, NCTX), 0)

    slab, place_in = me // BACK * BACK, me % BACK
    above, below = (me + BACK) % NCTX, (me + NCTX - BACK) % NCTX

    def greet(d, carry):
        to = slab + (place_in + d) % BACK
        pl.semaphore_signal(barrier, inc=1, device_id=(to, tp), device_id_type=MESH)
        return carry

    for who in ((above, tp), (below, tp), (me, mate), (me, across)):
        pl.semaphore_signal(barrier, inc=1, device_id=who, device_id_type=MESH)
    lax.fori_loop(1, BACK, greet, 0)

    def tell(n):
        for to in (above, below):
            pl.semaphore_signal(ready.at[n], inc=1, device_id=(to, tp), device_id_type=MESH)

    for load in loads[:4]:
        load.wait()
    cos_o = outer[0, pl.ds(me, 1), :]
    sin_o = outer[1, pl.ds(me, 1), :]
    cos = cos_o * inner[0] - sin_o * inner[1]
    sin = sin_o * inner[0] + cos_o * inner[1]
    lane = iota((ROWS, HD), 1)
    sin = jnp.where(lane < HD // 2, -sin, sin)

    def rotate(x):
        x = x.astype(F32)
        return (x * cos + pltpu.roll(x, HD // 2, 1) * sin).astype(BF16)

    kv[0, 0:HD, :] = jnp.transpose(rotate(k_in[...]).astype(F32)).astype(BF16)
    kv[0, HD : 2 * HD, 0:HD] = v_in[0:HD, :]
    kv[0, HD : 2 * HD, HD : 2 * HD] = v_in[HD : 2 * HD, :]

    pl.semaphore_wait(barrier, BACK - 1 + 4)

    def key_copy(source, d, to):
        return pltpu.make_async_remote_copy(
            src_ref=kv.at[source],
            dst_ref=kv.at[d],
            send_sem=kv_send.at[d - 1],
            recv_sem=kv_recv.at[d - 1],
            device_id=(to, tp),
            device_id_type=MESH,
        )

    first_slab, last_slab = me < BACK, me >= NCTX - BACK

    @pl.when(jnp.logical_not(last_slab))
    def _():
        key_copy(0, BACK, above).start()

    tell(0)

    def clear(d, carry):
        @pl.when(first_slab & (d > place_in))
        def _():
            kv[d] = jnp.zeros((ROWS, 2 * HD), BF16)

        return carry


    def send_own(d, carry):
        @pl.when(place_in + d < BACK)
        def _():
            key_copy(0, d, me + d).start()

        return carry

    def send_previous(d, carry):
        @pl.when(place_in + d >= BACK)
        def _():
            key_copy(BACK, d, slab + (place_in + d) % BACK).start()

        return carry

    lax.fori_loop(1, BACK, send_own, 0)
    for load in loads[4:]:
        load.wait()

    def doc_row(block):
        row = jnp.concatenate([docs[pl.ds(2 * block, 1), :], docs[pl.ds(2 * block + 1, 1), :]], axis=1)
        return jnp.broadcast_to(row, (HD, ROWS))

    far = jnp.where(jnp.transpose(doc_row(me).astype(F32)) == lane.astype(F32), 0.0, -FAR).astype(BF16)

    def queries(h, carry):
        rows = pl.ds(pl.multiple_of(h * ROWS, ROWS), ROWS)
        qx[rows, 0:HD] = rotate(q_in[:, pl.ds(pl.multiple_of(h * HD, HD), HD)])
        qx[rows, HD : 2 * HD] = far
        return carry

    def pass_on():
        key_copy(0, BACK, me).wait_recv()
        lax.fori_loop(1, BACK, send_previous, 0)

    pl.when(jnp.logical_not(first_slab))(pass_on)
    lax.fori_loop(1, BACK + 1, clear, 0)
    lax.fori_loop(0, HEADS, queries, 0)

    doc_iota = iota((HD, ROWS), 0)

    def features(d, carry):
        feat[d] = jnp.where(doc_row((me - d + NCTX) % NCTX) == doc_iota, 1.0, 0.0).astype(BF16)
        return carry

    lax.fori_loop(0, BACK + 1, features, 0)

    square_r, square_c = iota((ROWS, ROWS), 0), iota((ROWS, ROWS), 1)
    lists = jnp.concatenate(
        [bl[pl.ds(0, NCTX, stride=2), :], bl[pl.ds(1, NCTX, stride=2), :]], axis=1
    )
    mine = (lists >> 8) == me
    before = jnp.where(square_r < square_c, 1.0, 0.0).astype(BF16)
    rank = jnp.dot(jnp.where(mine, 1.0, 0.0).astype(BF16), before, preferred_element_type=F32)
    code[...] = jnp.where(mine, rank, -1.0)
    local[...] = ((lists & 255) + 1).astype(F32)
    slot_iota = iota((SLOTS, ROWS), 0).astype(F32)
    lane_next = (iota((SLOTS, ROWS), 1) + 1).astype(F32)

    def pack_rows(o, carry):
        hit = code[pl.ds(o, 1), :] == slot_iota
        token = jnp.sum(jnp.where(hit, local[pl.ds(o, 1), :], 0.0), axis=1, keepdims=True)
        at = pl.multiple_of(o * SLOTS, SLOTS)
        pack_m[pl.ds(at, SLOTS), :] = jnp.where(token == lane_next, 1.0, 0.0).astype(BF16)
        return carry

    lax.fori_loop(0, NCTX, pack_rows, 0, unroll=8)

    def merge_table():
        own = jnp.concatenate([bl[pl.ds(2 * me, 1), :], bl[pl.ds(2 * me + 1, 1), :]], axis=1)
        source_row = (own >> 8).astype(F32)
        source_col = jnp.sum(jnp.where(square_r == square_c, source_row, 0.0), axis=1, keepdims=True)
        earlier = (source_row == source_col) & (square_c < square_r)
        slot_col = jnp.sum(jnp.where(earlier, 1.0, 0.0), axis=1, keepdims=True)
        place = source_col * SLOTS + slot_col
        wide = iota((ROWS, NCTX * SLOTS), 1).astype(F32)
        unpack_m[...] = jnp.where(wide == place, 1.0, 0.0).astype(BF16)

    factor = math.log2(math.e) / math.sqrt(HD)
    chunk_rows = PER_CHUNK * ROWS

    def score_own(c, carry):
        keys = jnp.concatenate([kv[0, 0:HD, :], feat[0]], axis=0)
        rows = pl.ds(pl.multiple_of(c * chunk_rows, chunk_rows), chunk_rows)
        part = jnp.dot(qx[rows, :], keys, preferred_element_type=F32) * factor
        allowed = iota((chunk_rows, ROWS), 1) <= (iota((chunk_rows, ROWS), 0) & (ROWS - 1))
        part = jnp.where(allowed, part, -2.0 * FAR)
        scores[c, 0] = part
        tops[c] = jnp.maximum(part[:, 0:HD], part[:, HD:])
        return carry

    lax.fori_loop(0, EARLY, score_own, 0)

    def score(i, carry):
        d = (i + BACK - 1) % BACK + 1
        part = pl.ds(pl.multiple_of(i * (4096 // BACK), 4096 // BACK), 4096 // BACK)
        pltpu.make_async_copy(w_hbm.at[part, :], w.at[part, :], w_sem).start()

        @pl.when((i > 0) & (jnp.logical_not(first_slab) | (d <= place_in)))
        def _():
            key_copy(0, d, me).wait_recv()

        keys = jnp.concatenate([kv[d, 0:HD, :], feat[d]], axis=0)
        for c in range(EARLY):
            rows = slice(c * chunk_rows, (c + 1) * chunk_rows)
            part = jnp.dot(qx[rows, :], keys, preferred_element_type=F32) * factor
            scores[c, d] = part
            tops[c] = jnp.maximum(tops[c], jnp.maximum(part[:, 0:HD], part[:, HD:]))
        return carry

    pl.semaphore_wait(ready.at[0], 2)
    tell(1)
    lax.fori_loop(0, BACK, score, 0)
    pl.semaphore_wait(ready.at[1], 2)

    def score_late(c):
        score_own(c, 0)
        rows = pl.ds(pl.multiple_of(c * chunk_rows, chunk_rows), chunk_rows)
        top = tops[c]
        for d in range(1, BACK + 1):
            keys = jnp.concatenate([kv[d, 0:HD, :], feat[d]], axis=0)
            part = jnp.dot(qx[rows, :], keys, preferred_element_type=F32) * factor
            scores[c, d] = part
            top = jnp.maximum(top, jnp.maximum(part[:, 0:HD], part[:, HD:]))
        tops[c] = top

    def attend(c):
        ones = jnp.ones((ROWS, HD), BF16)
        vals = []
        for d in range(BACK + 1):
            block = jnp.concatenate([kv[d, HD : 2 * HD, 0:HD], kv[d, HD : 2 * HD, HD : 2 * HD]], axis=0)
            vals.append(jnp.concatenate([block, ones], axis=1))
        vals = jnp.concatenate(vals, axis=0)
        part = []
        for h in range(PER_CHUNK):
            rows = slice(h * ROWS, (h + 1) * ROWS)
            top = jnp.max(tops[c, rows, :], axis=1, keepdims=True)
            weights = [jnp.exp2(scores[c, d, rows, :] - top).astype(BF16) for d in range(BACK + 1)]
            mixed = jnp.dot(jnp.concatenate(weights, axis=1), vals, preferred_element_type=F32)
            part.append((mixed[:, 0:HD] / mixed[:, HD : 2 * HD]).astype(BF16))
        part = jnp.concatenate(part, axis=1)
        rows = jnp.dot(pack_m[...], part, preferred_element_type=F32).astype(BF16)
        packed[c] = rows.reshape(NCTX, SLOTS, WIDTH)
        landed[c, me] = packed[c, me]

        def send(to, inner_carry):
            pltpu.make_async_remote_copy(
                src_ref=packed.at[c, to],
                dst_ref=landed.at[c, me],
                send_sem=a_send.at[c],
                recv_sem=a_recv.at[c],
                device_id=(to, tp),
                device_id_type=MESH,
            ).start()
            return inner_carry

        others(send)

    def give(c, slot, to, sems):
        return pltpu.make_async_remote_copy(
            src_ref=gath.at[c, slot],
            dst_ref=gath.at[c, slot],
            send_sem=sems[0].at[c],
            recv_sem=sems[1].at[c],
            device_id=(me, to),
            device_id_type=MESH,
        )

    far_off, mate_near, mate_far = (z_send, z_recv), (c_send, c_recv), (f_send, f_recv)

    def unpack(c):
        rest = packed.at[c, pl.ds(0, NCTX - 1)]
        pltpu.make_async_copy(rest, rest, a_recv.at[c]).wait()
        rows = jnp.dot(unpack_m[...], landed[c].reshape(NCTX * SLOTS, WIDTH), preferred_element_type=F32)
        gath[c, tp] = rows.astype(BF16)
        give(c, tp, across, far_off).start()
        give(c, tp, mate, mate_near).start()

    def forward(c):
        give(c, across, across, far_off).wait_recv()
        give(c, across, mate, mate_far).start()

    def add_columns(c, slots, target):
        rows = jnp.concatenate([gath[c, t] for t in slots], axis=1)

        def columns(n, carry):
            cols = pl.ds(pl.multiple_of(n * 512, 512), 512)
            part = [w[pl.ds(pl.multiple_of(t * HEADS * HD + c * WIDTH, WIDTH), WIDTH), cols] for t in slots]
            total = jnp.dot(rows, jnp.concatenate(part, axis=0), preferred_element_type=F32) + acc[:, cols]
            target[:, cols] = total.astype(target.dtype)
            return carry

        lax.fori_loop(0, OUT // 512, columns, 0, unroll=4)

    def from_mate(c):
        give(c, mate, mate, mate_near).wait_recv()
        give(c, across_mate, mate, mate_far).wait_recv()

    def project(c):
        from_mate(c)
        add_columns(c, range(4), acc)

    def step(s, carry):
        @pl.when((s >= LAG) & (s < CHUNKS + LAG))
        def _():
            unpack(s - LAG)

        @pl.when((s >= EARLY) & (s < CHUNKS))
        def _():
            score_late(s)

        @pl.when(s < CHUNKS)
        def _():
            attend(s)

        @pl.when(s == 0)
        def _():
            merge_table()
            acc[...] = jnp.zeros((ROWS, OUT), F32)

        @pl.when((s >= LAG + 1) & (s < CHUNKS + LAG + 1))
        def _():
            forward(s - LAG - 1)

        @pl.when(s == LAG + 1)
        def _():
            w_copy.wait()

        @pl.when(s >= LAG + 2)
        def _():
            project(s - LAG - 2)

        return carry

    lax.fori_loop(0, CHUNKS + LAG, step, 0)
    project(CHUNKS - 2)
    forward(CHUNKS - 1)
    add_columns(CHUNKS - 1, (tp, across), acc)
    from_mate(CHUNKS - 1)
    add_columns(CHUNKS - 1, (mate, across_mate), out)

    def sent(d, carry):
        @pl.when((place_in + d < BACK) | jnp.logical_not(first_slab))
        def _():
            key_copy(0, d, me).wait_send()

        return carry

    lax.fori_loop(1, BACK, sent, 0)

    @pl.when(jnp.logical_not(last_slab))
    def _():
        key_copy(0, BACK, me).wait_send()

    for c in range(CHUNKS):
        rest = packed.at[c, pl.ds(0, NCTX - 1)]
        pltpu.make_async_copy(rest, rest, a_send.at[c]).wait()
        give(c, tp, across, far_off).wait_send()
        give(c, tp, mate, mate_near).wait_send()
        give(c, across, mate, mate_far).wait_send()


def on_device(balance_list, doc_ids, raw_queries, raw_keys, values, out_weight):
    inner, outer = rope_tables()
    vmem = pl.BlockSpec(memory_space=pltpu.VMEM)
    dma = pltpu.SemaphoreType.DMA
    return pl.pallas_call(
        kernel,
        out_shape=pltpu.VMEM((ROWS, OUT), BF16),
        in_specs=[pl.BlockSpec(memory_space=pl.ANY)] * 8,
        out_specs=vmem,
        scratch_shapes=[
            pltpu.VMEM((64, 128), jnp.int32),
            pltpu.VMEM((64, 128), jnp.int32),
            pltpu.VMEM((ROWS, HEADS * HD), BF16),
            pltpu.VMEM((ROWS, HD), BF16),
            pltpu.VMEM((ROWS, HD), BF16),
            pltpu.VMEM((2, ROWS, HD), F32),
            pltpu.VMEM((2, NCTX, HD), F32),
            pltpu.VMEM((HEADS * ROWS, 2 * HD), BF16),
            pltpu.VMEM((BACK + 1, ROWS, 2 * HD), BF16),
            pltpu.VMEM((BACK + 1, HD, ROWS), BF16),
            pltpu.VMEM((CHUNKS, BACK + 1, PER_CHUNK * ROWS, ROWS), F32),
            pltpu.VMEM((CHUNKS, PER_CHUNK * ROWS, HD), F32),
            pltpu.VMEM((NCTX, ROWS), F32),
            pltpu.VMEM((NCTX, ROWS), F32),
            pltpu.VMEM((NCTX * SLOTS, ROWS), BF16),
            pltpu.VMEM((ROWS, NCTX * SLOTS), BF16),
            pltpu.VMEM((CHUNKS, NCTX, SLOTS, WIDTH), BF16),
            pltpu.VMEM((CHUNKS, NCTX, SLOTS, WIDTH), BF16),
            pltpu.VMEM((CHUNKS, 4, ROWS, WIDTH), BF16),
            pltpu.VMEM((4096, OUT), BF16),
            pltpu.VMEM((ROWS, OUT), F32),
            dma((BACK,)), dma((BACK,)),
            dma((CHUNKS,)), dma((CHUNKS,)),
            dma((CHUNKS,)), dma((CHUNKS,)),
            dma((CHUNKS,)), dma((CHUNKS,)),
            dma((CHUNKS,)), dma((CHUNKS,)),
            dma,
            dma((7,)),
            pltpu.SemaphoreType.REGULAR((2,)),
        ],
        compiler_params=pltpu.CompilerParams(
            collective_id=0, has_side_effects=True, vmem_limit_bytes=60 * 1024 * 1024
        ),
        cost_estimate=pl.CostEstimate(
            flops=7_000_000_000, bytes_accessed=19_000_000, transcendentals=4_700_000
        ),
    )(
        balance_list.reshape(64, 128), doc_ids.reshape(64, 128), raw_queries, raw_keys, values,
        jnp.asarray(inner), jnp.asarray(outer), out_weight,
    )


def solution(mesh):
    in_specs = (P(), P(), P("ctx", "tp"), P("ctx", "tp"), P("ctx", "tp"), P(None, "tp"))
    out_specs = P("ctx", "tp")
    return jax.shard_map(
        on_device, mesh=mesh, in_specs=in_specs, out_specs=out_specs, check_vma=False
    )
```
